512 devices in a mesh: head: 8 (over x, core), expert: 64 (over y, z).
Axes of the slice: x: 4, y: 4, z: 16, core: 2. Of those that a mesh axis runs over, the one named last changes fastest.
Arguments:
- out_grad: bfloat16 [16384, 2048], P('expert'), may hold values from -6 to 6
- expert_ids: int32 [16384, 8], P('expert'), may hold values from 0 to 63, all different within a row; in each aligned block of 256 rows (0 to 255, 256 to 511, ...) at most 40 rows name the same one
- chosen_logits: float32 [16384, 8], P('expert'), may hold values from -6 to 6
- down_weight: bfloat16 [64, 768, 2048], P('expert', 'head'), may hold values from -0.21875 to 0.21875
- saved_hidden: bfloat16 [64, 64, 40, 768], P('expert', None, None, 'head'), may hold values from -0.29882812 to 0.29882812
- router_weight: bfloat16 [2048, 64], P('head'), may hold values from -6 to 6
Outputs:
- router_input_grad: bfloat16 [16384, 2048], P('expert', 'head')
- weight_grad: float32 [16384, 8], P('expert')
The draws below stay inside these ranges and needn't reach their ends.
Inputs may be any that keep to these rules, and one draw needn't show every extreme that they name: `expert_ids`: each row names 8 different experts. Among the 256 rows of one expert index no expert is named more than 40 times, and in every draw some expert index names some expert exactly 40 times.
All inputs are finite; a program needn't handle non-finite values.
Results may differ from the reference program's by a relative error of at most 0.012.
Values may be sent and summed in bfloat16 or wider, within the bound.
No kernel may reach another device: no remote copies, remote signals or barrier semaphores. Data moves between devices by JAX's collectives and lax.ppermute only.
A program may use at most 64 MiB of HBM per device.

```python
import math
import jax
import jax.numpy as jnp
import numpy as np
from jax import lax

D = 2048
FF = 768
TOPK = 8
TOK_DEV = 256
EXPERTS = 64
CAP = 40
TOKENS = 16384
N_EXPERT = 64


def block_levels(own_key, extent, shards, smallest, high):
    loudness, own = 1.0, jax.random.fold_in(own_key, 6)
    for dim, parts in shards:
        heights = jnp.exp(jax.random.uniform(jax.random.fold_in(own, dim), (parts,), jnp.float32, smallest / len(shards), high / len(shards)))
        loudness = loudness * jnp.repeat(heights, extent[dim] // parts).reshape([-1 if axis == dim else 1 for axis in range(len(extent))])
    return loudness


def shared_out(own_key, own, number, rows, amount, top, most, lean):
    order = jax.random.permutation(own_key, amount)
    packed, common = load_shares(amount, rows * top, most, lean, True), load_shares(amount, rows * top, most, lean, False)
    places = jnp.arange(amount)

    def named(sizes, offset_by):
        used = int((sizes > 0).sum())
        fixed = max(1, used // 4)
        moved = fixed + (places - fixed + offset_by * (used - fixed)) % max(1, amount - fixed)
        return jnp.zeros((amount,), jnp.int32).at[order[jnp.where(places < fixed, places, moved)]].set(jnp.asarray(sizes, jnp.int32))

    sizes = jnp.where(number % 4 == 0, named(packed, number // 4), named(common, number - number // 4 - 1))
    mixed = jax.random.permutation(jax.random.fold_in(own, 3), amount)
    giver, receiver = mixed[0:amount // 2 * 2:2], mixed[1:amount // 2 * 2:2]
    margin = jnp.minimum(sizes[giver] - 1, most - sizes[receiver]) // 2
    margin = jnp.where((giver == order[0]) | (receiver == order[0]) | (sizes[receiver] == 0), 0, jnp.maximum(margin, 0))
    moved = jax.random.randint(jax.random.fold_in(own, 4), (amount // 2,), 0, 1 << 20) % (margin + 1)
    sizes = sizes.at[giver].add(-moved).at[receiver].add(moved)
    members = jnp.searchsorted(jnp.cumsum(sizes), jnp.arange(rows * top), side="right").astype(jnp.int32)
    listing = members.reshape(top, rows).T
    listing = listing[jax.random.permutation(jax.random.fold_in(own, 1), rows)]
    offset_by = jax.random.randint(jax.random.fold_in(own, 2), (rows, 1), 0, top)
    return jnp.take_along_axis(listing, (jnp.arange(top)[None, :] + offset_by) % top, axis=1)


def load_shares(amount, total, most, slope, full):
    portions = [(1 << 20) // math.isqrt(standing ** slope) + 1 for standing in range(1, amount + 1)]
    largest = most if full else min(most, max(-(-total // amount), total * portions[0] // sum(portions)))
    least = 1 if total - largest >= amount - 1 else 0
    holding, surplus = [largest] + [least] * (amount - 1), total - largest - least * (amount - 1)
    while surplus > 0:
        candidates = [i for i in range(1, amount) if holding[i] < largest] or [i for i in range(1, amount) if holding[i] < most]
        whole, budget = sum([portions[i] for i in candidates]), surplus
        for i in candidates:
            more = min(most - holding[i], max(1, budget * portions[i] // whole), surplus)
            holding[i] = holding[i] + more
            surplus = surplus - more
    return np.array(holding)


def centred(stream_key, extent, scale, most, shards=(), kind=jnp.bfloat16):
    drawn = jax.random.normal(stream_key, extent, jnp.float32) * scale
    if len(shards) > 0:
        drawn = block_levels(stream_key, extent, shards, -0.22, 0.18) * drawn
    return jnp.clip(drawn, min=-most, max=most).astype(kind)


def setup_inputs(seed: int = 0) -> dict:
    key_of = jax.random.split(jax.random.key(seed), 7)
    out_grad = centred(key_of[0], (TOKENS, D), 1.0, 6.0, ((0, 64),))
    expert_ids_keys = jax.random.split(jax.random.fold_in(key_of[1], 1), TOKENS // TOK_DEV)
    expert_ids_turns = jax.random.permutation(jax.random.fold_in(key_of[1], 3), TOKENS // TOK_DEV)
    expert_ids = jax.vmap(lambda own, number: shared_out(jax.random.fold_in(key_of[1], 2), own, number, TOK_DEV, EXPERTS, TOPK, CAP, 2))(expert_ids_keys, expert_ids_turns).reshape((TOKENS, TOPK))
    chosen_logits = centred(key_of[2], (TOKENS, TOPK), 1.5, 6.0, ((0, 64),), jnp.float32)
    down_weight = centred(key_of[3], (EXPERTS, FF, D), FF ** -0.5, 0.21875, ((0, 64), (1, 8)))
    saved_hidden = centred(key_of[4], (EXPERTS, N_EXPERT, CAP, FF), 0.05, 0.29882812, ((0, 64), (3, 8)))
    router_weight = centred(key_of[5], (D, EXPERTS), 1.0, 6.0, ((0, 8),))
    return {"out_grad": out_grad, "expert_ids": expert_ids, "chosen_logits": chosen_logits, "down_weight": down_weight, "saved_hidden": saved_hidden, "router_weight": router_weight}


def slot_numbers(block_ids, count):
    onehot = (block_ids[:, :, None] == jnp.arange(count, dtype=jnp.int32)[None, None, :]).astype(jnp.float32)
    hits = jnp.sum(onehot, axis=1)
    rows = block_ids.shape[0]
    lower = (jnp.arange(rows, dtype=jnp.int32)[:, None] > jnp.arange(rows, dtype=jnp.int32)[None, :]).astype(jnp.float32)
    before = jnp.dot(lower, hits, precision=lax.Precision.HIGHEST)
    return jnp.sum(before[:, None, :] * onehot, axis=2).astype(jnp.int32)


def reference(out_grad, expert_ids, chosen_logits, down_weight, saved_hidden, router_weight):
    blocks = N_EXPERT
    ids = expert_ids.reshape(blocks, TOK_DEV, TOPK).astype(jnp.int32)
    slots = jax.vmap(lambda block: slot_numbers(block, EXPERTS))(ids)
    position = (ids * CAP + slots).astype(jnp.int32).reshape(blocks, TOK_DEV * TOPK)
    marks = (jnp.arange(TOK_DEV * TOPK, dtype=jnp.int32) // TOPK + 1).astype(jnp.int32)

    def fill_owner(pos):
        return jnp.zeros((EXPERTS * CAP,), jnp.int32).at[pos].set(marks)

    owner = jax.vmap(fill_owner)(position).reshape(blocks, EXPERTS, CAP)
    grads = out_grad.reshape(blocks, TOK_DEV, D)

    def per_expert(expert):
        own = lax.dynamic_index_in_dim(owner, expert, 1, keepdims=False)
        index = jnp.maximum(own - 1, 0).astype(jnp.int32)
        rows = jnp.take_along_axis(grads, index[:, :, None], axis=1)
        rows = jnp.where((own > 0)[:, :, None], rows, jnp.zeros((), rows.dtype))
        weight = lax.dynamic_index_in_dim(down_weight, expert, 0, keepdims=False)
        inner = jnp.einsum("scd,fd->scf", rows.astype(jnp.float32), weight.astype(jnp.float32))
        hidden = lax.dynamic_index_in_dim(saved_hidden, expert, 0, keepdims=False)
        return jnp.sum(inner * hidden.astype(jnp.float32), axis=2)

    slot_grads = lax.map(per_expert, jnp.arange(EXPERTS, dtype=jnp.int32))
    flat = jnp.transpose(slot_grads, (1, 0, 2)).reshape(blocks, EXPERTS * CAP)
    weight_grad = jnp.take_along_axis(flat, position, axis=1).reshape(TOKENS, TOPK)
    raised = jnp.exp(chosen_logits)
    probs = raised / jnp.sum(raised, axis=1, keepdims=True)
    logit_grad = probs * (weight_grad - jnp.sum(probs * weight_grad, axis=1, keepdims=True))
    onehot = (expert_ids[:, :, None] == jnp.arange(EXPERTS, dtype=jnp.int32)[None, None, :]).astype(jnp.float32)
    dense_grad = jnp.sum(logit_grad[:, :, None] * onehot, axis=1).astype(jnp.bfloat16)
    router_input_grad = jnp.dot(dense_grad, router_weight.T, preferred_element_type=jnp.float32).astype(jnp.bfloat16)
    return router_input_grad, weight_grad
```

```python
import jax
import jax.numpy as jnp
from jax import lax
from jax.experimental import pallas as pl
from jax.experimental.pallas import tpu as pltpu
from jax.sharding import Mesh, PartitionSpec as P

X, CORES, Y, ZH, ZL = 4, 2, 4, 4, 4
EXPERT = ("y", "zh", "zl")
HEAD = ("x", "core")
TOK = 256
CAP = 40
TOPK = 8
EXPERTS = 64
DS = 256
NEAR = Y * ZL
F32 = jnp.float32
BF16 = jnp.bfloat16


def select_kernel(zh_ref, blocks_ref, out_ref, picked):
    zh = zh_ref[0]
    j = lax.broadcasted_iota(jnp.int32, (NEAR, TOK), 0)
    expert = ((j // ZL) * (ZH * ZL) + zh * ZL + j % ZL).astype(F32)
    hits = []
    for b in range(ZH):
        ids = blocks_ref[b, TOK : TOK + 16, :].astype(F32)
        hit = jnp.zeros((NEAR, TOK), F32)
        for k in range(TOPK):
            hit = hit + (ids[k : k + 1, :] == expert).astype(F32)
        hits.append(hit)
    hits = jnp.concatenate(hits, axis=0)
    earlier = lax.broadcasted_iota(jnp.int32, (TOK, TOK), 0) < lax.broadcasted_iota(
        jnp.int32, (TOK, TOK), 1
    )
    before = jnp.dot(hits.astype(BF16), earlier.astype(BF16), preferred_element_type=F32)
    key = jnp.where(hits > 0, before, -1.0)
    slot = lax.broadcasted_iota(jnp.int32, (CAP, TOK), 0).astype(F32)
    for b in range(ZH):
        pick = jnp.concatenate(
            [(key[b * NEAR + e : b * NEAR + e + 1, :] == slot).astype(F32) for e in range(NEAR)],
            axis=0,
        )
        picked[b] = jnp.dot(
            pick.astype(BF16), blocks_ref[b, 0:TOK, :], preferred_element_type=F32
        )
    for e in range(NEAR):
        rows = [picked[b, e * CAP : (e + 1) * CAP, :] for b in range(ZH)]
        out_ref[e] = jnp.concatenate(rows, axis=0).astype(BF16)


def select_rows(zh, blocks):
    return pl.pallas_call(
        select_kernel,
        out_shape=jax.ShapeDtypeStruct((NEAR, ZH * CAP, DS), BF16),
        in_specs=[
            pl.BlockSpec(memory_space=pltpu.SMEM),
            pl.BlockSpec(memory_space=pltpu.VMEM),
        ],
        out_specs=pl.BlockSpec(memory_space=pltpu.VMEM),
        scratch_shapes=[pltpu.VMEM((ZH, NEAR * CAP, DS), F32)],
        compiler_params=pltpu.CompilerParams(vmem_limit_bytes=32 << 20),
    )(zh, blocks)


def plan_kernel(ids_ref, logits_ref, key_ref, probs_ref):
    ids = ids_ref[...]
    raised = jnp.exp(logits_ref[...])
    probs = raised / jnp.sum(raised, axis=1, keepdims=True)
    expert = lax.broadcasted_iota(jnp.int32, (TOK, EXPERTS), 1)
    hits = jnp.zeros((TOK, EXPERTS), F32)
    spread = jnp.zeros((TOK, EXPERTS), F32)
    for k in range(TOPK):
        mine = ids[:, k : k + 1] == expert
        hits = hits + mine.astype(F32)
        spread = spread + jnp.where(mine, probs[:, k : k + 1], 0.0)
    earlier = lax.broadcasted_iota(jnp.int32, (TOK, TOK), 0) > lax.broadcasted_iota(
        jnp.int32, (TOK, TOK), 1
    )
    before = jnp.dot(earlier.astype(BF16), hits.astype(BF16), preferred_element_type=F32)
    key_ref[...] = jnp.where(hits > 0, before, -1.0)
    probs_ref[...] = spread


def plan(ids, logits):
    shape = jax.ShapeDtypeStruct((TOK, EXPERTS), F32)
    return pl.pallas_call(plan_kernel, out_shape=(shape, shape))(ids, logits)


def final_kernel(back_ref, key_ref, probs_ref, ids_ref, router_ref, grad_ref, weight_ref):
    key = key_ref[...]
    probs = probs_ref[...]
    dense = jnp.zeros((TOK, EXPERTS), F32)
    for c in range(CAP):
        dense = jnp.where(key == float(c), back_ref[c : c + 1, :], dense)
    mean = jnp.sum(probs * dense, axis=1, keepdims=True)
    logit = (probs * (dense - mean)).astype(BF16)
    grad_ref[...] = lax.dot_general(
        logit, router_ref[...], (((1,), (1,)), ((), ())), preferred_element_type=F32
    ).astype(BF16)
    ids = ids_ref[...]
    expert = lax.broadcasted_iota(jnp.int32, (TOK, EXPERTS), 1)
    cols = [
        jnp.sum(jnp.where(ids[:, k : k + 1] == expert, dense, 0.0), axis=1, keepdims=True)
        for k in range(TOPK)
    ]
    weight_ref[...] = jnp.concatenate(cols, axis=1)


def finish(back, key, probs, ids, router):
    return pl.pallas_call(
        final_kernel,
        out_shape=(
            jax.ShapeDtypeStruct((TOK, DS), BF16),
            jax.ShapeDtypeStruct((TOK, TOPK), F32),
        ),
    )(back, key, probs, ids, router)


def body(out_grad, expert_ids, chosen_logits, down_weight, saved_hidden, router_weight):
    x, core = lax.axis_index("x"), lax.axis_index("core")
    head = x * CORES + core
    width = down_weight.shape[1]
    hidden = saved_hidden[0].reshape(Y, ZH, ZL, CAP, width).transpose(4, 0, 2, 1, 3)
    hidden = hidden.reshape(width, EXPERTS * CAP)
    weight = down_weight[0].reshape(width, X, CORES * DS).transpose(1, 0, 2)
    along = jnp.concatenate(
        [jnp.broadcast_to(hidden[None], (X,) + hidden.shape), weight], axis=2
    )
    along = lax.all_to_all(along, "x", split_axis=0, concat_axis=0, tiled=True)
    mine = along.reshape(X * width, EXPERTS * CAP + CORES * DS)
    slots = EXPERTS * CAP
    weight_mine = lax.dynamic_slice_in_dim(mine, slots + core * DS, DS, axis=1)
    weight_other = lax.dynamic_slice_in_dim(mine, slots + (1 - core) * DS, DS, axis=1)
    theirs = lax.ppermute(
        jnp.concatenate([mine[:, :slots], weight_other], axis=1), "core", [(0, 1), (1, 0)]
    )
    mixed = lax.dot_general(
        mine[:, :slots], weight_mine, (((0,), (0,)), ((), ())), preferred_element_type=F32
    ) + lax.dot_general(
        theirs[:, :slots], theirs[:, slots:], (((0,), (0,)), ((), ())), preferred_element_type=F32
    )
    own = lax.dynamic_slice_in_dim(out_grad, head * DS, DS, axis=1)
    ids_rows = jnp.pad(expert_ids.T.astype(BF16), ((0, 8), (0, 0)))
    blocks = lax.all_gather(jnp.concatenate([own, ids_rows], axis=0), "zh", axis=0, tiled=False)
    outgoing = select_rows(lax.axis_index("zh").reshape(1).astype(jnp.int32), blocks)
    received = lax.all_to_all(outgoing, ("y", "zl"), split_axis=0, concat_axis=0, tiled=True)
    part = jnp.sum(received.reshape(slots, DS).astype(F32) * mixed, axis=1)
    part = part.reshape(EXPERTS, CAP)
    part = jnp.sum(lax.all_gather(part, "core", axis=0, tiled=False), axis=0)
    part = lax.all_to_all(
        jnp.broadcast_to(part[None], (X,) + part.shape), "x", split_axis=0, concat_axis=0, tiled=True
    )
    part = jnp.sum(part, axis=0)
    back = lax.all_to_all(
        part.reshape(EXPERTS, 1, CAP), ("y", "zl", "zh"), split_axis=0, concat_axis=0, tiled=True
    )
    back = back.reshape(Y, ZL, ZH, CAP).transpose(3, 0, 2, 1).reshape(CAP, EXPERTS)
    key, probs = plan(expert_ids, chosen_logits)
    return finish(back, key, probs, expert_ids, router_weight)


def solution(mesh):
    fine = Mesh(
        mesh.devices.reshape(X, CORES, Y, ZH, ZL), ("x", "core", "y", "zh", "zl")
    )
    return jax.shard_map(
        body,
        mesh=fine,
        in_specs=(
            P(EXPERT, None),
            P(EXPERT, None),
            P(EXPERT, None),
            P(EXPERT, HEAD, None),
            P(EXPERT, None, None, HEAD),
            P(HEAD, None),
        ),
        out_specs=(P(EXPERT, HEAD), P(EXPERT, None)),
        check_vma=False,
    )
```

```python
import jax
import jax.numpy as jnp
from jax import lax
from jax.experimental import pallas as pl
from jax.experimental.pallas import tpu as pltpu
from jax.sharding import Mesh, PartitionSpec as P

X, CORES, Y, ZH, ZL = 4, 2, 4, 4, 4
EXPERT = ("y", "zh", "zl")
HEAD = ("x", "core")
TOK = 256
CAP = 40
TOPK = 8
EXPERTS = 64
DS = 256
NEAR = Y * ZL
F32 = jnp.float32
BF16 = jnp.bfloat16


def select_kernel(zh_ref, blocks_ref, out_ref, picked):
    zh = zh_ref[0]
    j = lax.broadcasted_iota(jnp.int32, (NEAR, TOK), 0)
    expert = ((j // ZL) * (ZH * ZL) + zh * ZL + j % ZL).astype(F32)
    hits = []
    for b in range(ZH):
        ids = blocks_ref[b, TOK : TOK + 16, :].astype(F32)
        hit = jnp.zeros((NEAR, TOK), F32)
        for k in range(TOPK):
            hit = hit + (ids[k : k + 1, :] == expert).astype(F32)
        hits.append(hit)
    hits = jnp.concatenate(hits, axis=0)
    earlier = lax.broadcasted_iota(jnp.int32, (TOK, TOK), 0) < lax.broadcasted_iota(
        jnp.int32, (TOK, TOK), 1
    )
    before = jnp.dot(hits.astype(BF16), earlier.astype(BF16), preferred_element_type=F32)
    key = jnp.where(hits > 0, before, -1.0)
    slot = lax.broadcasted_iota(jnp.int32, (CAP, TOK), 0).astype(F32)
    for b in range(ZH):
        pick = jnp.concatenate(
            [(key[b * NEAR + e : b * NEAR + e + 1, :] == slot).astype(F32) for e in range(NEAR)],
            axis=0,
        )
        picked[b] = jnp.dot(
            pick.astype(BF16), blocks_ref[b, 0:TOK, :], preferred_element_type=F32
        )
    for e in range(NEAR):
        rows = [picked[b, e * CAP : (e + 1) * CAP, :] for b in range(ZH)]
        out_ref[e] = jnp.concatenate(rows, axis=0).astype(BF16)


def select_rows(zh, blocks):
    return pl.pallas_call(
        select_kernel,
        out_shape=jax.ShapeDtypeStruct((NEAR, ZH * CAP, DS), BF16),
        in_specs=[
            pl.BlockSpec(memory_space=pltpu.SMEM),
            pl.BlockSpec(memory_space=pltpu.VMEM),
        ],
        out_specs=pl.BlockSpec(memory_space=pltpu.VMEM),
        scratch_shapes=[pltpu.VMEM((ZH, NEAR * CAP, DS), F32)],
        compiler_params=pltpu.CompilerParams(vmem_limit_bytes=32 << 20),
    )(zh, blocks)


def exchange_kernel(hidden_ref, weight_ref, out_ref):
    slots = EXPERTS * CAP
    hidden = hidden_ref[...].astype(F32).T.astype(BF16)
    for i in range(X):
        out_ref[i, :, 0:slots] = hidden
        out_ref[i, :, slots:] = weight_ref[:, i * CORES * DS : (i + 1) * CORES * DS]


def exchange_blocks(hidden, weight):
    width = weight.shape[0]
    return pl.pallas_call(
        exchange_kernel,
        out_shape=jax.ShapeDtypeStruct((X, width, EXPERTS * CAP + CORES * DS), BF16),
        compiler_params=pltpu.CompilerParams(vmem_limit_bytes=32 << 20),
    )(hidden, weight)


def mix_kernel(core_ref, mine_ref, theirs_ref, out_ref):
    slots = EXPERTS * CAP
    first = core_ref[0] == 0
    weight = jnp.where(
        first, mine_ref[:, slots : slots + DS], mine_ref[:, slots + DS : slots + 2 * DS]
    )
    group = ZH * ZL * CAP
    contract = (((0,), (0,)), ((), ()))
    for y in range(Y):
        cols = slice(y * group, (y + 1) * group)
        mixed = lax.dot_general(
            mine_ref[:, cols], weight, contract, preferred_element_type=F32
        ) + lax.dot_general(
            theirs_ref[:, cols], theirs_ref[:, slots:], contract, preferred_element_type=F32
        )
        for zh in range(ZH):
            for zl in range(ZL):
                src, dst = (zh * ZL + zl) * CAP, y * group + (zl * ZH + zh) * CAP
                out_ref[dst : dst + CAP, :] = mixed[src : src + CAP, :]


def mix(core, mine, theirs):
    return pl.pallas_call(
        mix_kernel,
        out_shape=jax.ShapeDtypeStruct((EXPERTS * CAP, DS), F32),
        in_specs=[
            pl.BlockSpec(memory_space=pltpu.SMEM),
            pl.BlockSpec(memory_space=pltpu.VMEM),
            pl.BlockSpec(memory_space=pltpu.VMEM),
        ],
        out_specs=pl.BlockSpec(memory_space=pltpu.VMEM),
        compiler_params=pltpu.CompilerParams(vmem_limit_bytes=32 << 20),
    )(core, mine, theirs)


def value_kernel(rows_ref, mixed_ref, out_ref):
    own_lane = lax.broadcasted_iota(jnp.int32, (CAP, 128), 0) == lax.broadcasted_iota(
        jnp.int32, (CAP, 128), 1
    )
    for e in range(NEAR):
        rows = rows_ref[e].astype(F32) * mixed_ref[e * ZH * CAP : (e + 1) * ZH * CAP, :]
        sums = jnp.sum(rows[:, 0:128] + rows[:, 128:256], axis=1, keepdims=True)
        for b in range(ZH):
            lanes = jnp.where(own_lane, sums[b * CAP : (b + 1) * CAP, :], 0.0)
            out_ref[e * ZH + b] = jnp.sum(lanes, axis=0, keepdims=True)


def slot_sums(rows, mixed):
    return pl.pallas_call(
        value_kernel,
        out_shape=jax.ShapeDtypeStruct((EXPERTS, 1, 128), F32),
        compiler_params=pltpu.CompilerParams(vmem_limit_bytes=32 << 20),
    )(rows, mixed)


def plan_kernel(ids_ref, logits_ref, key_ref, probs_ref):
    ids = ids_ref[...]
    raised = jnp.exp(logits_ref[...])
    probs = raised / jnp.sum(raised, axis=0, keepdims=True)
    expert = lax.broadcasted_iota(jnp.int32, (EXPERTS, TOK), 0)
    hits = jnp.zeros((EXPERTS, TOK), F32)
    spread = jnp.zeros((EXPERTS, TOK), F32)
    for k in range(TOPK):
        mine = ids[k : k + 1, :] == expert
        hits = hits + mine.astype(F32)
        spread = spread + jnp.where(mine, probs[k : k + 1, :], 0.0)
    earlier = lax.broadcasted_iota(jnp.int32, (TOK, TOK), 0) < lax.broadcasted_iota(
        jnp.int32, (TOK, TOK), 1
    )
    before = jnp.dot(hits.astype(BF16), earlier.astype(BF16), preferred_element_type=F32)
    key_ref[...] = jnp.where(hits > 0, before, -1.0)
    probs_ref[...] = spread


def plan(ids, logits):
    shape = jax.ShapeDtypeStruct((EXPERTS, TOK), F32)
    return pl.pallas_call(plan_kernel, out_shape=(shape, shape))(ids, logits)


def final_kernel(back_ref, key_ref, probs_ref, ids_ref, router_ref, grad_ref, weight_ref, total):
    parts = back_ref[0, 0]
    for c in range(CORES):
        for i in range(X):
            if c or i:
                parts = parts + back_ref[c, i]
    parts = parts.reshape(EXPERTS, 128)
    for y in range(Y):
        for zh in range(ZH):
            for zl in range(ZL):
                src, dst = (y * ZL + zl) * ZH + zh, (y * ZH + zh) * ZL + zl
                total[dst : dst + 1, :] = parts[src : src + 1, :]
    back = total[...]
    key = key_ref[...]
    probs = probs_ref[...]
    dense = jnp.zeros((EXPERTS, TOK), F32)
    for c in range(CAP):
        dense = jnp.where(key == float(c), back[:, c : c + 1], dense)
    mean = jnp.sum(probs * dense, axis=0, keepdims=True)
    logit = (probs * (dense - mean)).astype(BF16)
    grad_ref[...] = lax.dot_general(
        logit, router_ref[...], (((0,), (0,)), ((), ())), preferred_element_type=F32
    ).astype(BF16)
    ids = ids_ref[...]
    expert = lax.broadcasted_iota(jnp.int32, (EXPERTS, TOK), 0)
    for k in range(TOPK):
        weight_ref[k : k + 1, :] = jnp.sum(
            jnp.where(ids[k : k + 1, :] == expert, dense, 0.0), axis=0, keepdims=True
        )


def finish(back, key, probs, ids, router):
    return pl.pallas_call(
        final_kernel,
        out_shape=(
            jax.ShapeDtypeStruct((TOK, DS), BF16),
            jax.ShapeDtypeStruct((TOPK, TOK), F32),
        ),
        scratch_shapes=[pltpu.VMEM((EXPERTS, 128), F32)],
    )(back, key, probs, ids, router)


def body(out_grad, expert_ids, chosen_logits, down_weight, saved_hidden, router_weight):
    x, core = lax.axis_index("x"), lax.axis_index("core")
    head = x * CORES + core
    width = down_weight.shape[1]
    slots = EXPERTS * CAP
    ids, logits = expert_ids.T, chosen_logits.T
    along = exchange_blocks(saved_hidden[0].reshape(slots, width), down_weight[0])
    along = lax.all_to_all(along, "x", split_axis=0, concat_axis=0, tiled=True)
    mine = along.reshape(X * width, slots + CORES * DS)
    weight_other = lax.dynamic_slice_in_dim(mine, slots + (1 - core) * DS, DS, axis=1)
    theirs = lax.ppermute(
        jnp.concatenate([mine[:, :slots], weight_other], axis=1), "core", [(0, 1), (1, 0)]
    )
    mixed = mix(core.reshape(1).astype(jnp.int32), mine, theirs)
    ids_late, logits, _ = lax.optimization_barrier((ids, logits, theirs))
    key, probs = plan(ids_late, logits)
    own = lax.dynamic_slice_in_dim(out_grad, head * DS, DS, axis=1)
    ids_rows = jnp.pad(ids.astype(BF16), ((0, 8), (0, 0)))
    blocks = lax.all_gather(jnp.concatenate([own, ids_rows], axis=0), "zh", axis=0, tiled=False)
    outgoing = select_rows(lax.axis_index("zh").reshape(1).astype(jnp.int32), blocks)
    received = lax.all_to_all(outgoing, ("y", "zl"), split_axis=0, concat_axis=0, tiled=True)
    received, mixed, key, probs = lax.optimization_barrier((received, mixed, key, probs))
    part = slot_sums(received, mixed)
    part = lax.all_to_all(part, ("y", "zl", "zh"), split_axis=0, concat_axis=0, tiled=True)
    part = lax.all_to_all(
        jnp.broadcast_to(part[None], (X,) + part.shape), "x", split_axis=0, concat_axis=0, tiled=True
    )
    part = lax.all_gather(part, "core", axis=0, tiled=False)
    grad, weight_grad = finish(part, key, probs, ids, router_weight.T)
    return grad, weight_grad.T


def solution(mesh):
    fine = Mesh(
        mesh.devices.reshape(X, CORES, Y, ZH, ZL), ("x", "core", "y", "zh", "zl")
    )
    return jax.shard_map(
        body,
        mesh=fine,
        in_specs=(
            P(EXPERT, None),
            P(EXPERT, None),
            P(EXPERT, None),
            P(EXPERT, HEAD, None),
            P(EXPERT, None, None, HEAD),
            P(HEAD, None),
        ),
        out_specs=(P(EXPERT, HEAD), P(EXPERT, None)),
        check_vma=False,
    )
```

```python
import jax
import jax.numpy as jnp
from jax import lax
from jax.experimental import pallas as pl
from jax.experimental.pallas import tpu as pltpu
from jax.sharding import Mesh, PartitionSpec as P

X, CORES, Y, ZH, ZL = 4, 2, 4, 4, 4
EXPERT = ("y", "zh", "zl")
HEAD = ("x", "core")
TOK = 256
CAP = 40
TOPK = 8
EXPERTS = 64
DS = 256
NEAR = Y * ZL
F32 = jnp.float32
NEAR_GROUPS = [
    [c * Y * ZH * ZL + y * ZH * ZL + (q * ZL + r + 2 * c) % (ZH * ZL) for y in range(Y) for r in range(ZL)]
    for c in range(CORES)
    for q in range(ZH)
]
BF16 = jnp.bfloat16


def select_kernel(base_ref, blocks_ref, out_ref, picked):
    base = base_ref[0]
    j = lax.broadcasted_iota(jnp.int32, (NEAR, TOK), 0)
    expert = ((j // ZL) * (ZH * ZL) + ((base + j % ZL) & (ZH * ZL - 1))).astype(F32)
    hits = []
    for b in range(ZH):
        ids = blocks_ref[b, TOK : TOK + 16, :].astype(F32)
        hit = jnp.zeros((NEAR, TOK), F32)
        for k in range(TOPK):
            hit = hit + (ids[k : k + 1, :] == expert).astype(F32)
        hits.append(hit)
    hits = jnp.concatenate(hits, axis=0)
    earlier = lax.broadcasted_iota(jnp.int32, (TOK, TOK), 0) < lax.broadcasted_iota(
        jnp.int32, (TOK, TOK), 1
    )
    before = jnp.dot(hits.astype(BF16), earlier.astype(BF16), preferred_element_type=F32)
    key = jnp.where(hits > 0, before, -1.0)
    slot = lax.broadcasted_iota(jnp.int32, (CAP, TOK), 0).astype(F32)
    for b in range(ZH):
        pick = jnp.concatenate(
            [(key[b * NEAR + e : b * NEAR + e + 1, :] == slot).astype(F32) for e in range(NEAR)],
            axis=0,
        )
        picked[b] = jnp.dot(
            pick.astype(BF16), blocks_ref[b, 0:TOK, :], preferred_element_type=F32
        )
    for e in range(NEAR):
        rows = [picked[b, e * CAP : (e + 1) * CAP, :] for b in range(ZH)]
        out_ref[e] = jnp.concatenate(rows, axis=0).astype(BF16)


def select_rows(base, blocks):
    return pl.pallas_call(
        select_kernel,
        out_shape=jax.ShapeDtypeStruct((NEAR, ZH * CAP, DS), BF16),
        in_specs=[
            pl.BlockSpec(memory_space=pltpu.SMEM),
            pl.BlockSpec(memory_space=pltpu.VMEM),
        ],
        out_specs=pl.BlockSpec(memory_space=pltpu.VMEM),
        scratch_shapes=[pltpu.VMEM((ZH, NEAR * CAP, DS), F32)],
        compiler_params=pltpu.CompilerParams(vmem_limit_bytes=16 << 20),
    )(base, blocks)


def exchange_kernel(hidden_hbm, weight_hbm, out_ref, hidden, weight, sems):
    slots = EXPERTS * CAP
    piece = slots // 4
    copies = [
        pltpu.make_async_copy(
            hidden_hbm.at[pl.ds(i * piece, piece)], hidden.at[pl.ds(i * piece, piece)], sems.at[i]
        )
        for i in range(4)
    ]
    copies.append(pltpu.make_async_copy(weight_hbm, weight, sems.at[4]))
    for copy in copies:
        copy.start()
    for i in range(4):
        copies[i].wait()
        rows = slice(i * piece, (i + 1) * piece)
        turned = hidden[rows, :].astype(F32).T.astype(BF16)
        for j in range(X):
            out_ref[j, :, rows] = turned
    copies[4].wait()
    for j in range(X):
        out_ref[j, :, slots:] = weight[:, j * CORES * DS : (j + 1) * CORES * DS]


def exchange_blocks(hidden, weight):
    width = weight.shape[0]
    return pl.pallas_call(
        exchange_kernel,
        out_shape=jax.ShapeDtypeStruct((X, width, EXPERTS * CAP + CORES * DS), BF16),
        in_specs=[pl.BlockSpec(memory_space=pl.ANY)] * 2,
        out_specs=pl.BlockSpec(memory_space=pltpu.VMEM),
        scratch_shapes=[
            pltpu.VMEM(hidden.shape, BF16),
            pltpu.VMEM(weight.shape, BF16),
            pltpu.SemaphoreType.DMA((5,)),
        ],
        compiler_params=pltpu.CompilerParams(vmem_limit_bytes=16 << 20),
    )(hidden, weight)


def mix_kernel(
    core_ref, mine_ref, theirs_ref, ids_ref, logits_ref, out_ref, key_ref, probs_ref
):
    plan(ids_ref[...], logits_ref[...], key_ref, probs_ref)
    slots = EXPERTS * CAP
    core = core_ref[0]
    weight = jnp.where(
        core == 0, mine_ref[:, slots : slots + DS], mine_ref[:, slots + DS : slots + 2 * DS]
    )
    group = ZH * ZL * CAP
    contract = (((0,), (0,)), ((), ()))
    for y in range(Y):
        cols = slice(y * group, (y + 1) * group)
        mixed = lax.dot_general(
            mine_ref[:, cols], weight, contract, preferred_element_type=F32
        ) + lax.dot_general(
            theirs_ref[:, cols], theirs_ref[:, slots:], contract, preferred_element_type=F32
        )
        for zl in range(ZL):
            place = zl ^ (2 * core)
            for zh in range(ZH):
                src = (zh * ZL + zl) * CAP
                dst = pl.multiple_of(y * group + (place * ZH + zh) * CAP, 8)
                out_ref[pl.ds(dst, CAP), :] = mixed[src : src + CAP, :]


def plan(ids, logits, key_ref, probs_ref):
    raised = jnp.exp(logits)
    probs = raised / jnp.sum(raised, axis=0, keepdims=True)
    expert = lax.broadcasted_iota(jnp.int32, (EXPERTS, TOK), 0)
    hits = jnp.zeros((EXPERTS, TOK), F32)
    spread = jnp.zeros((EXPERTS, TOK), F32)
    for k in range(TOPK):
        mine = ids[k : k + 1, :] == expert
        hits = hits + mine.astype(F32)
        spread = spread + jnp.where(mine, probs[k : k + 1, :], 0.0)
    earlier = lax.broadcasted_iota(jnp.int32, (TOK, TOK), 0) < lax.broadcasted_iota(
        jnp.int32, (TOK, TOK), 1
    )
    before = jnp.dot(hits.astype(BF16), earlier.astype(BF16), preferred_element_type=F32)
    key_ref[...] = jnp.where(hits > 0, before, -1.0)
    probs_ref[...] = spread


def mix(core, mine, theirs, ids, logits):
    table = jax.ShapeDtypeStruct((EXPERTS, TOK), F32)
    return pl.pallas_call(
        mix_kernel,
        out_shape=(jax.ShapeDtypeStruct((EXPERTS * CAP, DS), F32), table, table),
        in_specs=[pl.BlockSpec(memory_space=pltpu.SMEM)]
        + [pl.BlockSpec(memory_space=pltpu.VMEM)] * 4,
        out_specs=(pl.BlockSpec(memory_space=pltpu.VMEM),) * 3,
        compiler_params=pltpu.CompilerParams(vmem_limit_bytes=16 << 20),
    )(core, mine, theirs, ids, logits)


def value_kernel(core_ref, rows_ref, mixed_ref, out_ref):
    own_lane = lax.broadcasted_iota(jnp.int32, (CAP, 128), 0) == lax.broadcasted_iota(
        jnp.int32, (CAP, 128), 1
    )
    for e in range(NEAR):
        rows = rows_ref[e].astype(F32) * mixed_ref[e * ZH * CAP : (e + 1) * ZH * CAP, :]
        sums = jnp.sum(rows[:, 0:128] + rows[:, 128:256], axis=1, keepdims=True)
        for b in range(ZH):
            lanes = jnp.where(own_lane, sums[b * CAP : (b + 1) * CAP, :], 0.0)
            place = (e // ZL * ZH + b) * ZL + ((e % ZL) ^ (2 * core_ref[0]))
            out_ref[place] = jnp.sum(lanes, axis=0, keepdims=True)


def slot_sums(core, rows, mixed):
    return pl.pallas_call(
        value_kernel,
        out_shape=jax.ShapeDtypeStruct((EXPERTS, 1, 128), F32),
        in_specs=[pl.BlockSpec(memory_space=pltpu.SMEM)]
        + [pl.BlockSpec(memory_space=pltpu.VMEM)] * 2,
        out_specs=pl.BlockSpec(memory_space=pltpu.VMEM),
        compiler_params=pltpu.CompilerParams(vmem_limit_bytes=16 << 20),
    )(core, rows, mixed)


def final_kernel(back_ref, key_ref, probs_ref, ids_ref, router_ref, grad_ref, weight_ref):
    parts = back_ref[0, 0]
    for c in range(CORES):
        for i in range(X):
            if c or i:
                parts = parts + back_ref[c, i]
    back = parts.reshape(EXPERTS, 128)
    key = key_ref[...]
    probs = probs_ref[...]
    dense = jnp.zeros((EXPERTS, TOK), F32)
    for c in range(CAP):
        dense = jnp.where(key == float(c), back[:, c : c + 1], dense)
    mean = jnp.sum(probs * dense, axis=0, keepdims=True)
    logit = (probs * (dense - mean)).astype(BF16)
    grad_ref[...] = lax.dot_general(
        logit, router_ref[...], (((0,), (0,)), ((), ())), preferred_element_type=F32
    ).astype(BF16)
    ids = ids_ref[...]
    expert = lax.broadcasted_iota(jnp.int32, (EXPERTS, TOK), 0)
    for k in range(TOPK):
        weight_ref[k : k + 1, :] = jnp.sum(
            jnp.where(ids[k : k + 1, :] == expert, dense, 0.0), axis=0, keepdims=True
        )


def finish(back, key, probs, ids, router):
    return pl.pallas_call(
        final_kernel,
        out_shape=(
            jax.ShapeDtypeStruct((TOK, DS), BF16),
            jax.ShapeDtypeStruct((TOPK, TOK), F32),
        ),
    )(back, key, probs, ids, router)


def body(out_grad, expert_ids, chosen_logits, down_weight, saved_hidden, router_weight):
    x, core = lax.axis_index("x"), lax.axis_index("core")
    head = x * CORES + core
    width = down_weight.shape[1]
    slots = EXPERTS * CAP
    ids, logits = expert_ids.T, chosen_logits.T
    along = exchange_blocks(saved_hidden[0].reshape(slots, width), down_weight[0])
    along = lax.all_to_all(along, "x", split_axis=0, concat_axis=0, tiled=True)
    mine = along.reshape(X * width, slots + CORES * DS)
    weight_other = lax.dynamic_slice_in_dim(mine, slots + (1 - core) * DS, DS, axis=1)
    theirs = lax.ppermute(
        jnp.concatenate([mine[:, :slots], weight_other], axis=1), "core", [(0, 1), (1, 0)]
    )
    core_scalar = core.reshape(1).astype(jnp.int32)
    mixed, key, probs = mix(core_scalar, mine, theirs, ids, logits)
    own = lax.dynamic_slice_in_dim(out_grad, head * DS, DS, axis=1)
    ids_rows = jnp.pad(ids.astype(BF16), ((0, 8), (0, 0)))
    blocks = lax.all_gather(jnp.concatenate([own, ids_rows], axis=0), "zh", axis=0, tiled=False)
    z = lax.axis_index("zh") * ZL + lax.axis_index("zl")
    base = ((z - 2 * core) & (ZH * ZL - ZL)) + 2 * core
    outgoing = select_rows(base.reshape(1).astype(jnp.int32), blocks)
    received = lax.all_to_all(
        outgoing,
        ("core", "y", "zh", "zl"),
        split_axis=0,
        concat_axis=0,
        tiled=True,
        axis_index_groups=NEAR_GROUPS,
    )
    part = slot_sums(core_scalar, received, mixed)
    part = lax.all_to_all(part, EXPERT, split_axis=0, concat_axis=0, tiled=True)
    part = lax.all_to_all(
        jnp.broadcast_to(part[None], (X,) + part.shape), "x", split_axis=0, concat_axis=0, tiled=True
    )
    part = lax.all_gather(part, "core", axis=0, tiled=False)
    grad, weight_grad = finish(part, key, probs, ids, router_weight.T)
    return grad, weight_grad.T


def solution(mesh):
    fine = Mesh(
        mesh.devices.reshape(X, CORES, Y, ZH, ZL), ("x", "core", "y", "zh", "zl")
    )
    return jax.shard_map(
        body,
        mesh=fine,
        in_specs=(
            P(EXPERT, None),
            P(EXPERT, None),
            P(EXPERT, None),
            P(EXPERT, HEAD, None),
            P(EXPERT, None, None, HEAD),
            P(HEAD, None),
        ),
        out_specs=(P(EXPERT, HEAD), P(EXPERT, None)),
        check_vma=False,
    )
```

```python
import jax
import jax.numpy as jnp
from jax import lax
from jax.experimental import pallas as pl
from jax.experimental.pallas import tpu as pltpu
from jax.sharding import Mesh, PartitionSpec as P

X, CORES, Y, ZH, ZL = 4, 2, 4, 4, 4
EXPERT = ("y", "zh", "zl")
HEAD = ("x", "core")
TOK = 256
CAP = 40
TOPK = 8
EXPERTS = 64
DS = 256
NEAR = Y * ZL
F32 = jnp.float32
NEAR_GROUPS = [
    [c * Y * ZH * ZL + y * ZH * ZL + (q * ZL + r + 2 * c) % (ZH * ZL) for y in range(Y) for r in range(ZL)]
    for c in range(CORES)
    for q in range(ZH)
]
BF16 = jnp.bfloat16


def in_hbm(array):
    return pltpu.with_memory_space_constraint(array, pltpu.HBM)


def select_kernel(base_ref, blocks_ref, out_hbm, picked, rows_out, sems):
    base = base_ref[0]
    j = lax.broadcasted_iota(jnp.int32, (NEAR, TOK), 0)
    expert = ((j // ZL) * (ZH * ZL) + ((base + j % ZL) & (ZH * ZL - 1))).astype(F32)
    hits = []
    for b in range(ZH):
        ids = blocks_ref[b, TOK : TOK + 16, :].astype(F32)
        hit = jnp.zeros((NEAR, TOK), F32)
        for k in range(TOPK):
            hit = hit + (ids[k : k + 1, :] == expert).astype(F32)
        hits.append(hit)
    hits = jnp.concatenate(hits, axis=0)
    earlier = lax.broadcasted_iota(jnp.int32, (TOK, TOK), 0) < lax.broadcasted_iota(
        jnp.int32, (TOK, TOK), 1
    )
    before = jnp.dot(hits.astype(BF16), earlier.astype(BF16), preferred_element_type=F32)
    key = jnp.where(hits > 0, before, -1.0)
    slot = lax.broadcasted_iota(jnp.int32, (CAP, TOK), 0).astype(F32)
    for b in range(ZH):
        pick = jnp.concatenate(
            [(key[b * NEAR + e : b * NEAR + e + 1, :] == slot).astype(F32) for e in range(NEAR)],
            axis=0,
        )
        picked[b] = jnp.dot(
            pick.astype(BF16), blocks_ref[b, 0:TOK, :], preferred_element_type=F32
        )
    copies = []
    for y in range(Y):
        for e in range(y * ZL, (y + 1) * ZL):
            rows = [picked[b, e * CAP : (e + 1) * CAP, :] for b in range(ZH)]
            rows_out[e] = jnp.concatenate(rows, axis=0).astype(BF16)
        near = pl.ds(y * ZL, ZL)
        copies.append(pltpu.make_async_copy(rows_out.at[near], out_hbm.at[near], sems.at[y]))
        copies[-1].start()
    for copy in copies:
        copy.wait()


def select_rows(base, blocks):
    return pl.pallas_call(
        select_kernel,
        out_shape=pltpu.HBM((NEAR, ZH * CAP, DS), BF16),
        in_specs=[
            pl.BlockSpec(memory_space=pltpu.SMEM),
            pl.BlockSpec(memory_space=pltpu.VMEM),
        ],
        out_specs=pl.BlockSpec(memory_space=pltpu.HBM),
        scratch_shapes=[
            pltpu.VMEM((ZH, NEAR * CAP, DS), F32),
            pltpu.VMEM((NEAR, ZH * CAP, DS), BF16),
            pltpu.SemaphoreType.DMA((Y,)),
        ],
        compiler_params=pltpu.CompilerParams(vmem_limit_bytes=16 << 20),
    )(base, blocks)


def exchange_kernel(
    head_ref, ids_hbm, grad_hbm, hidden_hbm, weight_hbm, out_hbm, block_ref, ids_ref, hidden, turned, sems
):
    slots = EXPERTS * CAP
    piece = slots // 4
    pieces = [pl.ds(i * piece, piece) for i in range(4)]
    loads = [
        pltpu.make_async_copy(hidden_hbm.at[pieces[i]], hidden.at[pieces[i]], sems.at[i])
        for i in range(4)
    ]
    columns = pl.ds(pl.multiple_of(head_ref[0] * DS, DS), DS)
    others = [
        pltpu.make_async_copy(
            weight_hbm.at[:, pl.ds(j * CORES * DS, CORES * DS)],
            out_hbm.at[j, :, pl.ds(slots, CORES * DS)],
            sems.at[4 + j],
        )
        for j in range(X)
    ]
    others.append(
        pltpu.make_async_copy(grad_hbm.at[:, columns], block_ref.at[pl.ds(0, TOK)], sems.at[8])
    )
    load_ids = pltpu.make_async_copy(ids_hbm, ids_ref, sems.at[9])
    for copy in loads + others + [load_ids]:
        copy.start()
    load_ids.wait()
    ids = ids_ref[...].astype(F32)
    block_ref[TOK : TOK + 16, :] = jnp.concatenate([ids, jnp.zeros_like(ids)], axis=0).astype(BF16)
    for i in range(4):
        loads[i].wait()
        rows = slice(i * piece, (i + 1) * piece)
        turned[:, rows] = hidden[rows, :].astype(F32).T.astype(BF16)
        for j in range(X):
            copy = pltpu.make_async_copy(
                turned.at[:, pieces[i]], out_hbm.at[j, :, pieces[i]], sems.at[10 + i * X + j]
            )
            copy.start()
            others.append(copy)
    for copy in others:
        copy.wait()


def exchange_blocks(head, ids, grad, hidden, weight):
    width = weight.shape[0]
    far = pl.BlockSpec(memory_space=pltpu.HBM)
    return pl.pallas_call(
        exchange_kernel,
        out_shape=(
            pltpu.HBM((X, width, EXPERTS * CAP + CORES * DS), BF16),
            jax.ShapeDtypeStruct((TOK + 16, DS), BF16),
        ),
        in_specs=[
            pl.BlockSpec(memory_space=pltpu.SMEM),
            far,
            far,
            far,
            far,
        ],
        out_specs=(far, pl.BlockSpec(memory_space=pltpu.VMEM)),
        scratch_shapes=[
            pltpu.VMEM(ids.shape, jnp.int32),
            pltpu.VMEM(hidden.shape, BF16),
            pltpu.VMEM((width, EXPERTS * CAP), BF16),
            pltpu.SemaphoreType.DMA((10 + 4 * X,)),
        ],
        compiler_params=pltpu.CompilerParams(vmem_limit_bytes=16 << 20),
    )(head, in_hbm(ids), in_hbm(grad), in_hbm(hidden), in_hbm(weight))


def mix_kernel(
    core_ref, mine_ref, theirs_ref, ids_ref, logits_ref, out_hbm, key_ref, probs_ref, out_ref, sems
):
    plan(ids_ref[...], logits_ref[...], key_ref, probs_ref)
    slots = EXPERTS * CAP
    core = core_ref[0]
    weight = jnp.where(
        core == 0, mine_ref[:, slots : slots + DS], mine_ref[:, slots + DS : slots + 2 * DS]
    )
    group = ZH * ZL * CAP
    contract = (((0,), (0,)), ((), ()))
    copies = []
    for y in range(Y):
        cols = slice(y * group, (y + 1) * group)
        mixed = lax.dot_general(
            mine_ref[:, cols], weight, contract, preferred_element_type=F32
        ) + lax.dot_general(
            theirs_ref[:, cols], theirs_ref[:, slots:], contract, preferred_element_type=F32
        )
        for zl in range(ZL):
            place = zl ^ (2 * core)
            for zh in range(ZH):
                src = (zh * ZL + zl) * CAP
                dst = pl.multiple_of(y * group + (place * ZH + zh) * CAP, 8)
                out_ref[pl.ds(dst, CAP), :] = mixed[src : src + CAP, :]
        rows = pl.ds(y * group, group)
        copies.append(pltpu.make_async_copy(out_ref.at[rows], out_hbm.at[rows], sems.at[y]))
        copies[-1].start()
    for copy in copies:
        copy.wait()


def plan(ids, logits, key_ref, probs_ref):
    raised = jnp.exp(logits)
    probs = raised / jnp.sum(raised, axis=0, keepdims=True)
    expert = lax.broadcasted_iota(jnp.int32, (EXPERTS, TOK), 0)
    hits = jnp.zeros((EXPERTS, TOK), F32)
    spread = jnp.zeros((EXPERTS, TOK), F32)
    for k in range(TOPK):
        mine = ids[k : k + 1, :] == expert
        hits = hits + mine.astype(F32)
        spread = spread + jnp.where(mine, probs[k : k + 1, :], 0.0)
    earlier = lax.broadcasted_iota(jnp.int32, (TOK, TOK), 0) < lax.broadcasted_iota(
        jnp.int32, (TOK, TOK), 1
    )
    before = jnp.dot(hits.astype(BF16), earlier.astype(BF16), preferred_element_type=F32)
    key_ref[...] = jnp.where(hits > 0, before, -1.0)
    probs_ref[...] = spread


def mix(core, mine, theirs, ids, logits):
    table = jax.ShapeDtypeStruct((EXPERTS, TOK), F32)
    return pl.pallas_call(
        mix_kernel,
        out_shape=(pltpu.HBM((EXPERTS * CAP, DS), F32), table, table),
        in_specs=[pl.BlockSpec(memory_space=pltpu.SMEM)]
        + [pl.BlockSpec(memory_space=pltpu.VMEM)] * 4,
        out_specs=(pl.BlockSpec(memory_space=pltpu.HBM),) + (pl.BlockSpec(memory_space=pltpu.VMEM),) * 2,
        scratch_shapes=[pltpu.VMEM((EXPERTS * CAP, DS), F32), pltpu.SemaphoreType.DMA((Y,))],
        compiler_params=pltpu.CompilerParams(vmem_limit_bytes=16 << 20),
    )(core, mine, theirs, ids, logits)


def value_kernel(core_ref, rows_hbm, mixed_hbm, out_ref, rows_ref, mixed_ref, sems):
    steps = 8
    per = NEAR // steps
    copies = []
    for i in range(steps):
        near, slots = pl.ds(i * per, per), pl.ds(i * per * ZH * CAP, per * ZH * CAP)
        copies.append(
            (
                pltpu.make_async_copy(rows_hbm.at[near], rows_ref.at[near], sems.at[0, i]),
                pltpu.make_async_copy(mixed_hbm.at[slots], mixed_ref.at[slots], sems.at[1, i]),
            )
        )
    for pair in copies:
        for copy in pair:
            copy.start()
    own_lane = lax.broadcasted_iota(jnp.int32, (CAP, 128), 0) == lax.broadcasted_iota(
        jnp.int32, (CAP, 128), 1
    )
    for i in range(steps):
        for copy in copies[i]:
            copy.wait()
        for e in range(i * per, (i + 1) * per):
            rows = rows_ref[e].astype(F32) * mixed_ref[e * ZH * CAP : (e + 1) * ZH * CAP, :]
            sums = jnp.sum(rows[:, 0:128] + rows[:, 128:256], axis=1, keepdims=True)
            for b in range(ZH):
                lanes = jnp.where(own_lane, sums[b * CAP : (b + 1) * CAP, :], 0.0)
                place = (e // ZL * ZH + b) * ZL + ((e % ZL) ^ (2 * core_ref[0]))
                out_ref[place] = jnp.sum(lanes, axis=0, keepdims=True)


def slot_sums(core, rows, mixed):
    return pl.pallas_call(
        value_kernel,
        out_shape=jax.ShapeDtypeStruct((EXPERTS, 1, 128), F32),
        in_specs=[
            pl.BlockSpec(memory_space=pltpu.SMEM),
            pl.BlockSpec(memory_space=pltpu.HBM),
            pl.BlockSpec(memory_space=pltpu.HBM),
        ],
        out_specs=pl.BlockSpec(memory_space=pltpu.VMEM),
        scratch_shapes=[
            pltpu.VMEM(rows.shape, BF16),
            pltpu.VMEM(mixed.shape, F32),
            pltpu.SemaphoreType.DMA((2, 8)),
        ],
        compiler_params=pltpu.CompilerParams(vmem_limit_bytes=16 << 20),
    )(core, in_hbm(rows), in_hbm(mixed))


def final_kernel(
    parts_hbm, key_hbm, probs_hbm, ids_ref, router_hbm, grad_ref, weight_ref,
    parts_ref, key_ref, probs_ref, router_ref, total, sems,
):
    copies = [
        pltpu.make_async_copy(far, near, sems.at[i])
        for i, (far, near) in enumerate(
            [(parts_hbm, parts_ref), (key_hbm, key_ref), (probs_hbm, probs_ref), (router_hbm, router_ref)]
        )
    ]
    for copy in copies:
        copy.start()
    for copy in copies:
        copy.wait()
    parts = parts_ref[0, 0]
    for c in range(CORES):
        for i in range(X):
            if c or i:
                parts = parts + parts_ref[c, i]
    total[...] = parts.reshape(EXPERTS, 128)
    back = total[...]
    key = key_ref[...]
    probs = probs_ref[...]
    dense = jnp.zeros((EXPERTS, TOK), F32)
    for c in range(CAP):
        dense = jnp.where(key == float(c), back[:, c : c + 1], dense)
    mean = jnp.sum(probs * dense, axis=0, keepdims=True)
    logit = (probs * (dense - mean)).astype(BF16)
    grad_ref[...] = lax.dot_general(
        logit, router_ref[...], (((0,), (0,)), ((), ())), preferred_element_type=F32
    ).astype(BF16)
    ids = ids_ref[...]
    expert = lax.broadcasted_iota(jnp.int32, (EXPERTS, TOK), 0)
    for k in range(TOPK):
        weight_ref[k : k + 1, :] = jnp.sum(
            jnp.where(ids[k : k + 1, :] == expert, dense, 0.0), axis=0, keepdims=True
        )


def finish(parts, key, probs, ids, router):
    far, near = pl.BlockSpec(memory_space=pltpu.HBM), pl.BlockSpec(memory_space=pltpu.VMEM)
    return pl.pallas_call(
        final_kernel,
        out_shape=(
            jax.ShapeDtypeStruct((TOK, DS), BF16),
            jax.ShapeDtypeStruct((TOPK, TOK), F32),
        ),
        in_specs=[far, far, far, near, far],
        out_specs=(near, near),
        scratch_shapes=[
            pltpu.VMEM(parts.shape, F32),
            pltpu.VMEM(key.shape, F32),
            pltpu.VMEM(probs.shape, F32),
            pltpu.VMEM(router.shape, BF16),
            pltpu.VMEM((EXPERTS, 128), F32),
            pltpu.SemaphoreType.DMA((4,)),
        ],
        compiler_params=pltpu.CompilerParams(vmem_limit_bytes=16 << 20),
    )(in_hbm(parts), in_hbm(key), in_hbm(probs), ids, in_hbm(router))


def body(out_grad, expert_ids, chosen_logits, down_weight, saved_hidden, router_weight):
    x, core = lax.axis_index("x"), lax.axis_index("core")
    head = x * CORES + core
    width = down_weight.shape[1]
    slots = EXPERTS * CAP
    ids, logits = expert_ids.T, chosen_logits.T
    along, block = exchange_blocks(
        head.reshape(1).astype(jnp.int32),
        ids,
        out_grad,
        saved_hidden[0].reshape(slots, width),
        down_weight[0],
    )
    along = lax.all_to_all(along, "x", split_axis=0, concat_axis=0, tiled=True)
    mine = along.reshape(X * width, slots + CORES * DS)
    weight_other = lax.dynamic_slice_in_dim(mine, slots + (1 - core) * DS, DS, axis=1)
    theirs = lax.ppermute(
        jnp.concatenate([mine[:, :slots], weight_other], axis=1), "core", [(0, 1), (1, 0)]
    )
    core_scalar = core.reshape(1).astype(jnp.int32)
    mixed, key, probs = mix(core_scalar, mine, theirs, ids, logits)
    blocks = lax.all_gather(block, "zh", axis=0, tiled=False)
    z = lax.axis_index("zh") * ZL + lax.axis_index("zl")
    base = ((z - 2 * core) & (ZH * ZL - ZL)) + 2 * core
    outgoing = select_rows(base.reshape(1).astype(jnp.int32), blocks)
    received = lax.all_to_all(
        outgoing,
        ("core", "y", "zh", "zl"),
        split_axis=0,
        concat_axis=0,
        tiled=True,
        axis_index_groups=NEAR_GROUPS,
    )
    part = slot_sums(core_scalar, received, mixed)
    part = lax.all_to_all(part, EXPERT, split_axis=0, concat_axis=0, tiled=True)
    part = lax.all_to_all(
        jnp.broadcast_to(part[None], (X,) + part.shape), "x", split_axis=0, concat_axis=0, tiled=True
    )
    part = lax.all_gather(part, "core", axis=0, tiled=False)
    grad, weight_grad = finish(part, key, probs, ids, router_weight.T)
    return grad, weight_grad.T


def solution(mesh):
    fine = Mesh(
        mesh.devices.reshape(X, CORES, Y, ZH, ZL), ("x", "core", "y", "zh", "zl")
    )
    return jax.shard_map(
        body,
        mesh=fine,
        in_specs=(
            P(EXPERT, None),
            P(EXPERT, None),
            P(EXPERT, None),
            P(EXPERT, HEAD, None),
            P(EXPERT, None, None, HEAD),
            P(HEAD, None),
        ),
        out_specs=(P(EXPERT, HEAD), P(EXPERT, None)),
        check_vma=False,
    )
```

```python
import jax
import jax.numpy as jnp
from jax import lax
from jax.experimental import pallas as pl
from jax.experimental.pallas import tpu as pltpu
from jax.sharding import Mesh, PartitionSpec as P

X, CORES, Y, ZH, ZL = 4, 2, 4, 4, 4
EXPERT = ("y", "zh", "zl")
HEAD = ("x", "core")
TOK = 256
CAP = 40
TOPK = 8
EXPERTS = 64
DS = 256
NEAR = Y * ZL
F32 = jnp.float32
NEAR_GROUPS = [
    [c * Y * ZH * ZL + y * ZH * ZL + (q * ZL + r + 2 * c) % (ZH * ZL) for y in range(Y) for r in range(ZL)]
    for c in range(CORES)
    for q in range(ZH)
]
BF16 = jnp.bfloat16


def in_hbm(array):
    return pltpu.with_memory_space_constraint(array, pltpu.HBM)


def select_kernel(base_ref, blocks_ref, out_hbm, picked, rows_out, sems):
    base = base_ref[0]
    j = lax.broadcasted_iota(jnp.int32, (NEAR, TOK), 0)
    expert = ((j // ZL) * (ZH * ZL) + ((base + j % ZL) & (ZH * ZL - 1))).astype(F32)
    hits = []
    for b in range(ZH):
        ids = blocks_ref[b, TOK : TOK + 16, :].astype(F32)
        hit = jnp.zeros((NEAR, TOK), F32)
        for k in range(TOPK):
            hit = hit + (ids[k : k + 1, :] == expert).astype(F32)
        hits.append(hit)
    hits = jnp.concatenate(hits, axis=0)
    earlier = lax.broadcasted_iota(jnp.int32, (TOK, TOK), 0) < lax.broadcasted_iota(
        jnp.int32, (TOK, TOK), 1
    )
    before = jnp.dot(hits.astype(BF16), earlier.astype(BF16), preferred_element_type=F32)
    key = jnp.where(hits > 0, before, -1.0)
    slot = lax.broadcasted_iota(jnp.int32, (CAP, TOK), 0).astype(F32)
    for b in range(ZH):
        pick = jnp.concatenate(
            [(key[b * NEAR + e : b * NEAR + e + 1, :] == slot).astype(F32) for e in range(NEAR)],
            axis=0,
        )
        picked[b] = jnp.dot(
            pick.astype(BF16), blocks_ref[b, 0:TOK, :], preferred_element_type=F32
        )
    copies = []
    for y in range(Y):
        for e in range(y * ZL, (y + 1) * ZL):
            rows = [picked[b, e * CAP : (e + 1) * CAP, :] for b in range(ZH)]
            rows_out[e] = jnp.concatenate(rows, axis=0).astype(BF16)
        near = pl.ds(y * ZL, ZL)
        copies.append(pltpu.make_async_copy(rows_out.at[near], out_hbm.at[near], sems.at[y]))
        copies[-1].start()
    for copy in copies:
        copy.wait()


def select_rows(base, blocks):
    return pl.pallas_call(
        select_kernel,
        out_shape=pltpu.HBM((NEAR, ZH * CAP, DS), BF16),
        in_specs=[
            pl.BlockSpec(memory_space=pltpu.SMEM),
            pl.BlockSpec(memory_space=pltpu.VMEM),
        ],
        out_specs=pl.BlockSpec(memory_space=pltpu.HBM),
        scratch_shapes=[
            pltpu.VMEM((ZH, NEAR * CAP, DS), F32),
            pltpu.VMEM((NEAR, ZH * CAP, DS), BF16),
            pltpu.SemaphoreType.DMA((Y,)),
        ],
        compiler_params=pltpu.CompilerParams(vmem_limit_bytes=16 << 20),
    )(base, blocks)


def exchange_kernel(
    head_ref, ids_hbm, grad_hbm, hidden_hbm, weight_hbm, out_hbm, block_ref, ids_ref, hidden, weight, turned, sems
):
    slots = EXPERTS * CAP
    piece = slots // 4
    pieces = [pl.ds(i * piece, piece) for i in range(4)]
    loads = [
        pltpu.make_async_copy(hidden_hbm.at[pieces[i]], hidden.at[pieces[i]], sems.at[i])
        for i in range(4)
    ]
    columns = pl.ds(pl.multiple_of(head_ref[0] * DS, DS), DS)
    load_weight = pltpu.make_async_copy(weight_hbm, weight, sems.at[10])
    load_ids = pltpu.make_async_copy(ids_hbm, ids_ref, sems.at[9])
    load_grad = pltpu.make_async_copy(
        grad_hbm.at[:, columns], block_ref.at[pl.ds(0, TOK)], sems.at[8]
    )
    for copy in loads + [load_weight, load_ids, load_grad]:
        copy.start()
    others = [load_grad]
    load_ids.wait()
    ids = ids_ref[...].astype(F32)
    block_ref[TOK : TOK + 16, :] = jnp.concatenate([ids, jnp.zeros_like(ids)], axis=0).astype(BF16)
    for i in range(4):
        loads[i].wait()
        rows = slice(i * piece, (i + 1) * piece)
        turned[:, rows] = hidden[rows, :].astype(F32).T.astype(BF16)
        for j in range(X):
            copy = pltpu.make_async_copy(
                turned.at[:, pieces[i]], out_hbm.at[j, :, pieces[i]], sems.at[11 + i * X + j]
            )
            copy.start()
            others.append(copy)
    load_weight.wait()
    for j in range(X):
        copy = pltpu.make_async_copy(
            weight.at[:, pl.ds(j * CORES * DS, CORES * DS)],
            out_hbm.at[j, :, pl.ds(slots, CORES * DS)],
            sems.at[4 + j],
        )
        copy.start()
        others.append(copy)
    for copy in others:
        copy.wait()


def exchange_blocks(head, ids, grad, hidden, weight):
    width = weight.shape[0]
    far = pl.BlockSpec(memory_space=pltpu.HBM)
    return pl.pallas_call(
        exchange_kernel,
        out_shape=(
            pltpu.HBM((X, width, EXPERTS * CAP + CORES * DS), BF16),
            jax.ShapeDtypeStruct((TOK + 16, DS), BF16),
        ),
        in_specs=[
            pl.BlockSpec(memory_space=pltpu.SMEM),
            far,
            far,
            far,
            far,
        ],
        out_specs=(far, pl.BlockSpec(memory_space=pltpu.VMEM)),
        scratch_shapes=[
            pltpu.VMEM(ids.shape, jnp.int32),
            pltpu.VMEM(hidden.shape, BF16),
            pltpu.VMEM(weight.shape, BF16),
            pltpu.VMEM((width, EXPERTS * CAP), BF16),
            pltpu.SemaphoreType.DMA((11 + 4 * X,)),
        ],
        compiler_params=pltpu.CompilerParams(vmem_limit_bytes=16 << 20),
    )(head, in_hbm(ids), in_hbm(grad), in_hbm(hidden), in_hbm(weight))


def mix_kernel(
    core_ref, mine_ref, theirs_ref, ids_ref, logits_ref, out_hbm, key_ref, probs_ref, out_ref, sems
):
    plan(ids_ref[...], logits_ref[...], key_ref, probs_ref)
    slots = EXPERTS * CAP
    core = core_ref[0]
    weight = jnp.where(
        core == 0, mine_ref[:, slots : slots + DS], mine_ref[:, slots + DS : slots + 2 * DS]
    )
    group = ZH * ZL * CAP
    contract = (((0,), (0,)), ((), ()))
    copies = []
    for y in range(Y):
        cols = slice(y * group, (y + 1) * group)
        mixed = lax.dot_general(
            mine_ref[:, cols], weight, contract, preferred_element_type=F32
        ) + lax.dot_general(
            theirs_ref[:, cols], theirs_ref[:, slots:], contract, preferred_element_type=F32
        )
        for zl in range(ZL):
            place = zl ^ (2 * core)
            for zh in range(ZH):
                src = (zh * ZL + zl) * CAP
                dst = pl.multiple_of(y * group + (place * ZH + zh) * CAP, 8)
                out_ref[pl.ds(dst, CAP), :] = mixed[src : src + CAP, :]
        rows = pl.ds(y * group, group)
        copies.append(pltpu.make_async_copy(out_ref.at[rows], out_hbm.at[rows], sems.at[y]))
        copies[-1].start()
    for copy in copies:
        copy.wait()


def plan(ids, logits, key_ref, probs_ref):
    raised = jnp.exp(logits)
    probs = raised / jnp.sum(raised, axis=0, keepdims=True)
    expert = lax.broadcasted_iota(jnp.int32, (EXPERTS, TOK), 0)
    hits = jnp.zeros((EXPERTS, TOK), F32)
    spread = jnp.zeros((EXPERTS, TOK), F32)
    for k in range(TOPK):
        mine = ids[k : k + 1, :] == expert
        hits = hits + mine.astype(F32)
        spread = spread + jnp.where(mine, probs[k : k + 1, :], 0.0)
    earlier = lax.broadcasted_iota(jnp.int32, (TOK, TOK), 0) < lax.broadcasted_iota(
        jnp.int32, (TOK, TOK), 1
    )
    before = jnp.dot(hits.astype(BF16), earlier.astype(BF16), preferred_element_type=F32)
    key_ref[...] = jnp.where(hits > 0, before, -1.0)
    probs_ref[...] = spread


def mix(core, mine, theirs, ids, logits):
    table = jax.ShapeDtypeStruct((EXPERTS, TOK), F32)
    return pl.pallas_call(
        mix_kernel,
        out_shape=(pltpu.HBM((EXPERTS * CAP, DS), F32), table, table),
        in_specs=[pl.BlockSpec(memory_space=pltpu.SMEM)]
        + [pl.BlockSpec(memory_space=pltpu.VMEM)] * 4,
        out_specs=(pl.BlockSpec(memory_space=pltpu.HBM),) + (pl.BlockSpec(memory_space=pltpu.VMEM),) * 2,
        scratch_shapes=[pltpu.VMEM((EXPERTS * CAP, DS), F32), pltpu.SemaphoreType.DMA((Y,))],
        compiler_params=pltpu.CompilerParams(vmem_limit_bytes=16 << 20),
    )(core, mine, theirs, ids, logits)


def value_kernel(core_ref, rows_hbm, mixed_hbm, out_ref, rows_ref, mixed_ref, sems):
    steps = 8
    per = NEAR // steps
    copies = []
    for i in range(steps):
        near, slots = pl.ds(i * per, per), pl.ds(i * per * ZH * CAP, per * ZH * CAP)
        copies.append(
            (
                pltpu.make_async_copy(rows_hbm.at[near], rows_ref.at[near], sems.at[0, i]),
                pltpu.make_async_copy(mixed_hbm.at[slots], mixed_ref.at[slots], sems.at[1, i]),
            )
        )
    for pair in copies:
        for copy in pair:
            copy.start()
    own_lane = lax.broadcasted_iota(jnp.int32, (CAP, 128), 0) == lax.broadcasted_iota(
        jnp.int32, (CAP, 128), 1
    )
    for i in range(steps):
        for copy in copies[i]:
            copy.wait()
        for e in range(i * per, (i + 1) * per):
            rows = rows_ref[e].astype(F32) * mixed_ref[e * ZH * CAP : (e + 1) * ZH * CAP, :]
            sums = jnp.sum(rows[:, 0:128] + rows[:, 128:256], axis=1, keepdims=True)
            for b in range(ZH):
                lanes = jnp.where(own_lane, sums[b * CAP : (b + 1) * CAP, :], 0.0)
                place = (e // ZL * ZH + b) * ZL + ((e % ZL) ^ (2 * core_ref[0]))
                out_ref[place] = jnp.sum(lanes, axis=0, keepdims=True)


def slot_sums(core, rows, mixed):
    return pl.pallas_call(
        value_kernel,
        out_shape=jax.ShapeDtypeStruct((EXPERTS, 1, 128), F32),
        in_specs=[
            pl.BlockSpec(memory_space=pltpu.SMEM),
            pl.BlockSpec(memory_space=pltpu.HBM),
            pl.BlockSpec(memory_space=pltpu.HBM),
        ],
        out_specs=pl.BlockSpec(memory_space=pltpu.VMEM),
        scratch_shapes=[
            pltpu.VMEM(rows.shape, BF16),
            pltpu.VMEM(mixed.shape, F32),
            pltpu.SemaphoreType.DMA((2, 8)),
        ],
        compiler_params=pltpu.CompilerParams(vmem_limit_bytes=16 << 20),
    )(core, in_hbm(rows), in_hbm(mixed))


def final_kernel(
    parts_hbm, key_hbm, probs_hbm, ids_ref, router_hbm, grad_ref, weight_ref,
    parts_ref, key_ref, probs_ref, router_ref, total, sems,
):
    copies = [
        pltpu.make_async_copy(far, near, sems.at[i])
        for i, (far, near) in enumerate(
            [(parts_hbm, parts_ref), (key_hbm, key_ref), (probs_hbm, probs_ref), (router_hbm, router_ref)]
        )
    ]
    for copy in copies:
        copy.start()
    for copy in copies:
        copy.wait()
    parts = parts_ref[0]
    for i in range(1, X):
        parts = parts + parts_ref[i]
    total[...] = parts.reshape(EXPERTS, 128)
    back = total[...]
    key = key_ref[...]
    probs = probs_ref[...]
    dense = jnp.zeros((EXPERTS, TOK), F32)
    for c in range(CAP):
        dense = jnp.where(key == float(c), back[:, c : c + 1], dense)
    mean = jnp.sum(probs * dense, axis=0, keepdims=True)
    logit = (probs * (dense - mean)).astype(BF16)
    grad_ref[...] = lax.dot_general(
        logit, router_ref[...], (((0,), (0,)), ((), ())), preferred_element_type=F32
    ).astype(BF16)
    ids = ids_ref[...]
    expert = lax.broadcasted_iota(jnp.int32, (EXPERTS, TOK), 0)
    for k in range(TOPK):
        weight_ref[k : k + 1, :] = jnp.sum(
            jnp.where(ids[k : k + 1, :] == expert, dense, 0.0), axis=0, keepdims=True
        )


def finish(parts, key, probs, ids, router):
    far, near = pl.BlockSpec(memory_space=pltpu.HBM), pl.BlockSpec(memory_space=pltpu.VMEM)
    return pl.pallas_call(
        final_kernel,
        out_shape=(
            jax.ShapeDtypeStruct((TOK, DS), BF16),
            jax.ShapeDtypeStruct((TOPK, TOK), F32),
        ),
        in_specs=[far, far, far, near, far],
        out_specs=(near, near),
        scratch_shapes=[
            pltpu.VMEM(parts.shape, F32),
            pltpu.VMEM(key.shape, F32),
            pltpu.VMEM(probs.shape, F32),
            pltpu.VMEM(router.shape, BF16),
            pltpu.VMEM((EXPERTS, 128), F32),
            pltpu.SemaphoreType.DMA((4,)),
        ],
        compiler_params=pltpu.CompilerParams(vmem_limit_bytes=16 << 20),
    )(in_hbm(parts), in_hbm(key), in_hbm(probs), ids, in_hbm(router))


def body(out_grad, expert_ids, chosen_logits, down_weight, saved_hidden, router_weight):
    x, core = lax.axis_index("x"), lax.axis_index("core")
    head = x * CORES + core
    width = down_weight.shape[1]
    slots = EXPERTS * CAP
    ids, logits = expert_ids.T, chosen_logits.T
    along, block = exchange_blocks(
        head.reshape(1).astype(jnp.int32),
        ids,
        out_grad,
        saved_hidden[0].reshape(slots, width),
        down_weight[0],
    )
    along = lax.all_to_all(along, "x", split_axis=0, concat_axis=0, tiled=True)
    mine = along.reshape(X * width, slots + CORES * DS)
    weight_other = lax.dynamic_slice_in_dim(mine, slots + (1 - core) * DS, DS, axis=1)
    theirs = lax.ppermute(
        jnp.concatenate([mine[:, :slots], weight_other], axis=1), "core", [(0, 1), (1, 0)]
    )
    core_scalar = core.reshape(1).astype(jnp.int32)
    mixed, key, probs = mix(core_scalar, mine, theirs, ids, logits)
    blocks = lax.all_gather(block, "zh", axis=0, tiled=False)
    z = lax.axis_index("zh") * ZL + lax.axis_index("zl")
    base = ((z - 2 * core) & (ZH * ZL - ZL)) + 2 * core
    outgoing = select_rows(base.reshape(1).astype(jnp.int32), blocks)
    received = lax.all_to_all(
        outgoing,
        ("core", "y", "zh", "zl"),
        split_axis=0,
        concat_axis=0,
        tiled=True,
        axis_index_groups=NEAR_GROUPS,
    )
    part = slot_sums(core_scalar, received, mixed)
    part = jnp.sum(lax.all_gather(part, "core", axis=0, tiled=False), axis=0)
    part = jnp.broadcast_to(part[None], (X,) + part.shape).reshape(X * EXPERTS, 1, 128)
    part = lax.all_to_all(part, ("x",) + EXPERT, split_axis=0, concat_axis=0, tiled=True)
    part = part.reshape(X, EXPERTS, 1, 128)
    grad, weight_grad = finish(part, key, probs, ids, router_weight.T)
    return grad, weight_grad.T


def solution(mesh):
    fine = Mesh(
        mesh.devices.reshape(X, CORES, Y, ZH, ZL), ("x", "core", "y", "zh", "zl")
    )
    return jax.shard_map(
        body,
        mesh=fine,
        in_specs=(
            P(EXPERT, None),
            P(EXPERT, None),
            P(EXPERT, None),
            P(EXPERT, HEAD, None),
            P(EXPERT, None, None, HEAD),
            P(HEAD, None),
        ),
        out_specs=(P(EXPERT, HEAD), P(EXPERT, None)),
        check_vma=False,
    )
```

```python
import jax
import jax.numpy as jnp
from jax import lax
from jax.experimental import pallas as pl
from jax.experimental.pallas import tpu as pltpu
from jax.sharding import Mesh, PartitionSpec as P

X, CORES, Y, ZH, ZL = 4, 2, 4, 4, 4
EXPERT = ("y", "zh", "zl")
HEAD = ("x", "core")
TOK = 256
CAP = 40
TOPK = 8
EXPERTS = 64
DS = 256
NEAR = Y * ZL
F32 = jnp.float32
NEAR_GROUPS = [
    [c * Y * ZH * ZL + y * ZH * ZL + (q * ZL + r + 2 * c) % (ZH * ZL) for y in range(Y) for r in range(ZL)]
    for c in range(CORES)
    for q in range(ZH)
]
BF16 = jnp.bfloat16


def in_vmem(array):
    return pltpu.with_memory_space_constraint(array, pltpu.VMEM)


def in_hbm(array):
    return pltpu.with_memory_space_constraint(array, pltpu.HBM)


def select_kernel(base_ref, blocks_ref, out_hbm, picked, rows_out, sems):
    base = base_ref[0]
    j = lax.broadcasted_iota(jnp.int32, (NEAR, TOK), 0)
    expert = ((j // ZL) * (ZH * ZL) + ((base + j % ZL) & (ZH * ZL - 1))).astype(F32)
    hits = []
    for b in range(ZH):
        ids = blocks_ref[b, TOK : TOK + 16, :].astype(F32)
        hit = jnp.zeros((NEAR, TOK), F32)
        for k in range(TOPK):
            hit = hit + (ids[k : k + 1, :] == expert).astype(F32)
        hits.append(hit)
    hits = jnp.concatenate(hits, axis=0)
    earlier = lax.broadcasted_iota(jnp.int32, (TOK, TOK), 0) < lax.broadcasted_iota(
        jnp.int32, (TOK, TOK), 1
    )
    before = jnp.dot(hits.astype(BF16), earlier.astype(BF16), preferred_element_type=F32)
    key = jnp.where(hits > 0, before, -1.0)
    slot = lax.broadcasted_iota(jnp.int32, (CAP, TOK), 0).astype(F32)
    copies = []
    for y in range(Y):
        for b in range(ZH):
            first = b * NEAR + y * ZL
            pick = jnp.concatenate(
                [(key[e : e + 1, :] == slot).astype(F32) for e in range(first, first + ZL)], axis=0
            )
            picked[b] = jnp.dot(
                pick.astype(BF16), blocks_ref[b, 0:TOK, :], preferred_element_type=F32
            )
        for e in range(ZL):
            rows = [picked[b, e * CAP : (e + 1) * CAP, :] for b in range(ZH)]
            rows_out[y * ZL + e] = jnp.concatenate(rows, axis=0).astype(BF16)
        near = pl.ds(y * ZL, ZL)
        copies.append(pltpu.make_async_copy(rows_out.at[near], out_hbm.at[near], sems.at[y]))
        copies[-1].start()
    for copy in copies:
        copy.wait()


def select_rows(base, blocks):
    return pl.pallas_call(
        select_kernel,
        out_shape=pltpu.HBM((NEAR, ZH * CAP, DS), BF16),
        in_specs=[
            pl.BlockSpec(memory_space=pltpu.SMEM),
            pl.BlockSpec(memory_space=pltpu.VMEM),
        ],
        out_specs=pl.BlockSpec(memory_space=pltpu.HBM),
        scratch_shapes=[
            pltpu.VMEM((ZH, ZL * CAP, DS), F32),
            pltpu.VMEM((NEAR, ZH * CAP, DS), BF16),
            pltpu.SemaphoreType.DMA((Y,)),
        ],
        compiler_params=pltpu.CompilerParams(vmem_limit_bytes=16 << 20),
    )(base, blocks)


def exchange_kernel(
    head_ref, ids_hbm, grad_hbm, hidden_hbm, weight_hbm, out_hbm, block_ref, ids_ref, hidden, weight, turned, sems
):
    slots = EXPERTS * CAP
    piece = slots // 4
    pieces = [pl.ds(i * piece, piece) for i in range(4)]
    loads = [
        pltpu.make_async_copy(hidden_hbm.at[pieces[i]], hidden.at[pieces[i]], sems.at[i])
        for i in range(4)
    ]
    columns = pl.ds(pl.multiple_of(head_ref[0] * DS, DS), DS)
    load_weight = pltpu.make_async_copy(weight_hbm, weight, sems.at[10])
    load_ids = pltpu.make_async_copy(ids_hbm, ids_ref, sems.at[9])
    load_grad = pltpu.make_async_copy(
        grad_hbm.at[:, columns], block_ref.at[pl.ds(0, TOK)], sems.at[8]
    )
    for copy in [load_weight] + loads + [load_ids, load_grad]:
        copy.start()
    others = [load_grad]
    load_ids.wait()
    ids = ids_ref[...].astype(F32)
    block_ref[TOK : TOK + 16, :] = jnp.concatenate([ids, jnp.zeros_like(ids)], axis=0).astype(BF16)
    load_weight.wait()
    for j in range(X):
        copy = pltpu.make_async_copy(
            weight.at[:, pl.ds(j * CORES * DS, CORES * DS)],
            out_hbm.at[j, :, pl.ds(slots, CORES * DS)],
            sems.at[4 + j],
        )
        copy.start()
        others.append(copy)
    for i in range(4):
        loads[i].wait()
        rows = slice(i * piece, (i + 1) * piece)
        turned[:, rows] = hidden[rows, :].astype(F32).T.astype(BF16)
        for j in range(X):
            copy = pltpu.make_async_copy(
                turned.at[:, pieces[i]], out_hbm.at[j, :, pieces[i]], sems.at[11 + i * X + j]
            )
            copy.start()
            others.append(copy)
    for copy in others:
        copy.wait()


def exchange_blocks(head, ids, grad, hidden, weight):
    width = weight.shape[0]
    far = pl.BlockSpec(memory_space=pltpu.HBM)
    return pl.pallas_call(
        exchange_kernel,
        out_shape=(
            pltpu.HBM((X, width, EXPERTS * CAP + CORES * DS), BF16),
            jax.ShapeDtypeStruct((TOK + 16, DS), BF16),
        ),
        in_specs=[
            pl.BlockSpec(memory_space=pltpu.SMEM),
            far,
            far,
            far,
            far,
        ],
        out_specs=(far, pl.BlockSpec(memory_space=pltpu.VMEM)),
        scratch_shapes=[
            pltpu.VMEM(ids.shape, jnp.int32),
            pltpu.VMEM(hidden.shape, BF16),
            pltpu.VMEM(weight.shape, BF16),
            pltpu.VMEM((width, EXPERTS * CAP), BF16),
            pltpu.SemaphoreType.DMA((11 + 4 * X,)),
        ],
        compiler_params=pltpu.CompilerParams(vmem_limit_bytes=16 << 20),
    )(head, in_hbm(ids), in_hbm(grad), in_hbm(hidden), in_hbm(weight))


def mix_kernel(
    core_ref, mine_ref, theirs_ref, ids_ref, logits_ref, out_hbm, key_ref, probs_ref, out_ref, rounded, sems
):
    plan(ids_ref[...], logits_ref[...], key_ref, probs_ref)
    slots = EXPERTS * CAP
    core = core_ref[0]
    weight = jnp.where(
        core == 0, mine_ref[:, slots : slots + DS], mine_ref[:, slots + DS : slots + 2 * DS]
    )
    group = ZH * ZL * CAP
    contract = (((0,), (0,)), ((), ()))
    copies = []
    for y in range(Y):
        cols = slice(y * group, (y + 1) * group)
        mixed = lax.dot_general(
            mine_ref[:, cols], weight, contract, preferred_element_type=F32
        ) + lax.dot_general(
            theirs_ref[:, cols], theirs_ref[:, slots:], contract, preferred_element_type=F32
        )
        for zl in range(ZL):
            place = zl ^ (2 * core)
            for zh in range(ZH):
                src = (zh * ZL + zl) * CAP
                dst = pl.multiple_of(y * group + (place * ZH + zh) * CAP, 8)
                out_ref[pl.ds(dst, CAP), :] = mixed[src : src + CAP, :]
        rows = pl.ds(y * group, group)
        rounded[rows, :] = out_ref[rows, :].astype(BF16)
        copies.append(pltpu.make_async_copy(rounded.at[rows], out_hbm.at[rows], sems.at[y]))
        copies[-1].start()
    for copy in copies:
        copy.wait()


def plan(ids, logits, key_ref, probs_ref):
    raised = jnp.exp(logits)
    probs = raised / jnp.sum(raised, axis=0, keepdims=True)
    expert = lax.broadcasted_iota(jnp.int32, (EXPERTS, TOK), 0)
    hits = jnp.zeros((EXPERTS, TOK), F32)
    spread = jnp.zeros((EXPERTS, TOK), F32)
    for k in range(TOPK):
        mine = ids[k : k + 1, :] == expert
        hits = hits + mine.astype(F32)
        spread = spread + jnp.where(mine, probs[k : k + 1, :], 0.0)
    earlier = lax.broadcasted_iota(jnp.int32, (TOK, TOK), 0) < lax.broadcasted_iota(
        jnp.int32, (TOK, TOK), 1
    )
    before = jnp.dot(hits.astype(BF16), earlier.astype(BF16), preferred_element_type=F32)
    key_ref[...] = jnp.where(hits > 0, before, -1.0)
    probs_ref[...] = spread


def mix(core, mine, theirs, ids, logits):
    table = pltpu.VMEM((EXPERTS, TOK), F32)
    return pl.pallas_call(
        mix_kernel,
        out_shape=(pltpu.HBM((EXPERTS * CAP, DS), BF16), table, table),
        in_specs=[pl.BlockSpec(memory_space=pltpu.SMEM)]
        + [pl.BlockSpec(memory_space=pltpu.VMEM)] * 4,
        out_specs=(pl.BlockSpec(memory_space=pltpu.HBM),) + (pl.BlockSpec(memory_space=pltpu.VMEM),) * 2,
        scratch_shapes=[
            pltpu.VMEM((EXPERTS * CAP, DS), F32),
            pltpu.VMEM((EXPERTS * CAP, DS), BF16),
            pltpu.SemaphoreType.DMA((Y,)),
        ],
        compiler_params=pltpu.CompilerParams(vmem_limit_bytes=16 << 20),
    )(core, mine, theirs, ids, logits)


def value_kernel(core_ref, rows_hbm, mixed_hbm, out_ref, rows_ref, mixed_ref, sems):
    steps = 4
    per = NEAR // steps
    copies = []
    for i in range(steps):
        near, slots = pl.ds(i * per, per), pl.ds(i * per * ZH * CAP, per * ZH * CAP)
        copies.append(
            (
                pltpu.make_async_copy(rows_hbm.at[near], rows_ref.at[near], sems.at[0, i]),
                pltpu.make_async_copy(mixed_hbm.at[slots], mixed_ref.at[slots], sems.at[1, i]),
            )
        )
    for pair in copies:
        for copy in pair:
            copy.start()
    own_lane = lax.broadcasted_iota(jnp.int32, (CAP, 128), 0) == lax.broadcasted_iota(
        jnp.int32, (CAP, 128), 1
    )
    for i in range(steps):
        for copy in copies[i]:
            copy.wait()
        for e in range(i * per, (i + 1) * per):
            rows = rows_ref[e].astype(F32) * mixed_ref[
                e * ZH * CAP : (e + 1) * ZH * CAP, :
            ].astype(F32)
            sums = jnp.sum(rows[:, 0:128] + rows[:, 128:256], axis=1, keepdims=True)
            for b in range(ZH):
                lanes = jnp.where(own_lane, sums[b * CAP : (b + 1) * CAP, :], 0.0)
                place = (e // ZL * ZH + b) * ZL + ((e % ZL) ^ (2 * core_ref[0]))
                out_ref[place] = jnp.sum(lanes, axis=0, keepdims=True)


def slot_sums(core, rows, mixed):
    return pl.pallas_call(
        value_kernel,
        out_shape=jax.ShapeDtypeStruct((EXPERTS, 1, 128), F32),
        in_specs=[
            pl.BlockSpec(memory_space=pltpu.SMEM),
            pl.BlockSpec(memory_space=pltpu.HBM),
            pl.BlockSpec(memory_space=pltpu.HBM),
        ],
        out_specs=pl.BlockSpec(memory_space=pltpu.VMEM),
        scratch_shapes=[
            pltpu.VMEM(rows.shape, BF16),
            pltpu.VMEM(mixed.shape, BF16),
            pltpu.SemaphoreType.DMA((2, 4)),
        ],
        compiler_params=pltpu.CompilerParams(vmem_limit_bytes=16 << 20),
    )(core, in_hbm(rows), in_hbm(mixed))


def final_kernel(
    parts_hbm, key_ref, probs_ref, ids_ref, router_hbm, grad_ref, weight_ref,
    parts_ref, router_ref, total, sems,
):
    copies = [
        pltpu.make_async_copy(far, near, sems.at[i])
        for i, (far, near) in enumerate(
            [(parts_hbm, parts_ref), (router_hbm, router_ref)]
        )
    ]
    for copy in copies:
        copy.start()
    for copy in copies:
        copy.wait()
    parts = parts_ref[0]
    for i in range(1, X):
        parts = parts + parts_ref[i]
    total[...] = parts.reshape(EXPERTS, 128)
    back = total[...]
    key = key_ref[...]
    probs = probs_ref[...]
    dense = jnp.zeros((EXPERTS, TOK), F32)
    for c in range(CAP):
        dense = jnp.where(key == float(c), back[:, c : c + 1], dense)
    mean = jnp.sum(probs * dense, axis=0, keepdims=True)
    logit = (probs * (dense - mean)).astype(BF16)
    grad_ref[...] = lax.dot_general(
        logit, router_ref[...], (((0,), (0,)), ((), ())), preferred_element_type=F32
    ).astype(BF16)
    ids = ids_ref[...]
    expert = lax.broadcasted_iota(jnp.int32, (EXPERTS, TOK), 0)
    for k in range(TOPK):
        weight_ref[k : k + 1, :] = jnp.sum(
            jnp.where(ids[k : k + 1, :] == expert, dense, 0.0), axis=0, keepdims=True
        )


def finish(parts, key, probs, ids, router):
    far, near = pl.BlockSpec(memory_space=pltpu.HBM), pl.BlockSpec(memory_space=pltpu.VMEM)
    return pl.pallas_call(
        final_kernel,
        out_shape=(
            jax.ShapeDtypeStruct((TOK, DS), BF16),
            jax.ShapeDtypeStruct((TOPK, TOK), F32),
        ),
        in_specs=[far, near, near, near, far],
        out_specs=(near, near),
        scratch_shapes=[
            pltpu.VMEM(parts.shape, F32),
            pltpu.VMEM(router.shape, BF16),
            pltpu.VMEM((EXPERTS, 128), F32),
            pltpu.SemaphoreType.DMA((2,)),
        ],
        compiler_params=pltpu.CompilerParams(vmem_limit_bytes=16 << 20),
    )(in_hbm(parts), in_vmem(key), in_vmem(probs), ids, in_hbm(router))


def body(out_grad, expert_ids, chosen_logits, down_weight, saved_hidden, router_weight):
    x, core = lax.axis_index("x"), lax.axis_index("core")
    head = x * CORES + core
    width = down_weight.shape[1]
    slots = EXPERTS * CAP
    ids, logits = expert_ids.T, chosen_logits.T
    along, block = exchange_blocks(
        head.reshape(1).astype(jnp.int32),
        ids,
        out_grad,
        saved_hidden[0].reshape(slots, width),
        down_weight[0],
    )
    along = lax.all_to_all(along, "x", split_axis=0, concat_axis=0, tiled=True)
    mine = along.reshape(X * width, slots + CORES * DS)
    weight_other = lax.dynamic_slice_in_dim(mine, slots + (1 - core) * DS, DS, axis=1)
    theirs = lax.ppermute(
        jnp.concatenate([mine[:, :slots], weight_other], axis=1), "core", [(0, 1), (1, 0)]
    )
    core_scalar = core.reshape(1).astype(jnp.int32)
    mixed, key, probs = mix(core_scalar, mine, theirs, ids, logits)
    blocks = lax.all_gather(block, "zh", axis=0, tiled=False)
    z = lax.axis_index("zh") * ZL + lax.axis_index("zl")
    base = ((z - 2 * core) & (ZH * ZL - ZL)) + 2 * core
    outgoing = select_rows(base.reshape(1).astype(jnp.int32), blocks)
    received = lax.all_to_all(
        outgoing,
        ("core", "y", "zh", "zl"),
        split_axis=0,
        concat_axis=0,
        tiled=True,
        axis_index_groups=NEAR_GROUPS,
    )
    part = slot_sums(core_scalar, received, mixed)
    part = jnp.sum(lax.all_gather(part, "core", axis=0, tiled=False), axis=0)
    part = jnp.broadcast_to(part[None], (X,) + part.shape).reshape(X * EXPERTS, 1, 128)
    part = lax.all_to_all(part, ("x",) + EXPERT, split_axis=0, concat_axis=0, tiled=True)
    part = part.reshape(X, EXPERTS, 1, 128)
    grad, weight_grad = finish(part, key, probs, ids, router_weight.T)
    return grad, weight_grad.T


def solution(mesh):
    fine = Mesh(
        mesh.devices.reshape(X, CORES, Y, ZH, ZL), ("x", "core", "y", "zh", "zl")
    )
    return jax.shard_map(
        body,
        mesh=fine,
        in_specs=(
            P(EXPERT, None),
            P(EXPERT, None),
            P(EXPERT, None),
            P(EXPERT, HEAD, None),
            P(EXPERT, None, None, HEAD),
            P(HEAD, None),
        ),
        out_specs=(P(EXPERT, HEAD), P(EXPERT, None)),
        check_vma=False,
    )
```

```python
import jax
import jax.numpy as jnp
from jax import lax
from jax.experimental import pallas as pl
from jax.experimental.pallas import tpu as pltpu
from jax.sharding import Mesh, PartitionSpec as P

X, CORES, Y, ZH, ZL = 4, 2, 4, 4, 4
EXPERT = ("y", "zh", "zl")
HEAD = ("x", "core")
TOK = 256
CAP = 40
TOPK = 8
EXPERTS = 64
DS = 256
NEAR = Y * ZL
F32 = jnp.float32
FAR_GROUPS = [[c * ZH + (b + c) % ZH for b in range(ZH)] for c in range(CORES)]
NEAR_GROUPS = [
    [c * Y * ZH * ZL + y * ZH * ZL + (q * ZL + r + 2 * c) % (ZH * ZL) for y in range(Y) for r in range(ZL)]
    for c in range(CORES)
    for q in range(ZH)
]
BF16 = jnp.bfloat16


def in_vmem(array):
    return pltpu.with_memory_space_constraint(array, pltpu.VMEM)


def in_hbm(array):
    return pltpu.with_memory_space_constraint(array, pltpu.HBM)


def select_kernel(base_ref, blocks_ref, out_hbm, picked, rows_out, sems):
    base, core = base_ref[0], base_ref[1]
    j = lax.broadcasted_iota(jnp.int32, (NEAR, TOK), 0)
    expert = ((j // ZL) * (ZH * ZL) + ((base + j % ZL) & (ZH * ZL - 1))).astype(F32)
    hits = []
    for b in range(ZH):
        ids = blocks_ref[b, TOK : TOK + 16, :].astype(F32)
        hit = jnp.zeros((NEAR, TOK), F32)
        for k in range(TOPK):
            hit = hit + (ids[k : k + 1, :] == expert).astype(F32)
        hits.append(hit)
    hits = jnp.concatenate(hits, axis=0)
    earlier = lax.broadcasted_iota(jnp.int32, (TOK, TOK), 0) < lax.broadcasted_iota(
        jnp.int32, (TOK, TOK), 1
    )
    before = jnp.dot(hits.astype(BF16), earlier.astype(BF16), preferred_element_type=F32)
    key = jnp.where(hits > 0, before, -1.0)
    slot = lax.broadcasted_iota(jnp.int32, (CAP, TOK), 0).astype(F32)
    copies = []
    for y in range(Y):
        for b in range(ZH):
            first = b * NEAR + y * ZL
            pick = jnp.concatenate(
                [(key[e : e + 1, :] == slot).astype(F32) for e in range(first, first + ZL)], axis=0
            )
            picked[(b + core) & (ZH - 1)] = jnp.dot(
                pick.astype(BF16), blocks_ref[b, 0:TOK, :], preferred_element_type=F32
            )
        for e in range(ZL):
            rows = [picked[b, e * CAP : (e + 1) * CAP, :] for b in range(ZH)]
            rows_out[y * ZL + e] = jnp.concatenate(rows, axis=0).astype(BF16)
        near = pl.ds(y * ZL, ZL)
        copies.append(pltpu.make_async_copy(rows_out.at[near], out_hbm.at[near], sems.at[y]))
        copies[-1].start()
    for copy in copies:
        copy.wait()


def select_rows(base, blocks):
    return pl.pallas_call(
        select_kernel,
        out_shape=pltpu.HBM((NEAR, ZH * CAP, DS), BF16),
        in_specs=[
            pl.BlockSpec(memory_space=pltpu.SMEM),
            pl.BlockSpec(memory_space=pltpu.VMEM),
        ],
        out_specs=pl.BlockSpec(memory_space=pltpu.HBM),
        scratch_shapes=[
            pltpu.VMEM((ZH, ZL * CAP, DS), F32),
            pltpu.VMEM((NEAR, ZH * CAP, DS), BF16),
            pltpu.SemaphoreType.DMA((Y,)),
        ],
        compiler_params=pltpu.CompilerParams(vmem_limit_bytes=16 << 20),
    )(base, blocks)


def exchange_kernel(
    head_ref, ids_hbm, grad_hbm, hidden_hbm, weight_hbm, out_hbm, block_ref, ids_ref, hidden, weight, turned, sems
):
    slots = EXPERTS * CAP
    piece = slots // 4
    pieces = [pl.ds(i * piece, piece) for i in range(4)]
    loads = [
        pltpu.make_async_copy(hidden_hbm.at[pieces[i]], hidden.at[pieces[i]], sems.at[i])
        for i in range(4)
    ]
    columns = pl.ds(pl.multiple_of(head_ref[0] * DS, DS), DS)
    load_weight = pltpu.make_async_copy(weight_hbm, weight, sems.at[10])
    load_ids = pltpu.make_async_copy(ids_hbm, ids_ref, sems.at[9])
    load_grad = pltpu.make_async_copy(
        grad_hbm.at[:, columns], block_ref.at[pl.ds(0, TOK)], sems.at[8]
    )
    for copy in [load_weight] + loads + [load_ids, load_grad]:
        copy.start()
    others = [load_grad]
    load_ids.wait()
    ids = ids_ref[...].astype(F32)
    block_ref[TOK : TOK + 16, :] = jnp.concatenate([ids, jnp.zeros_like(ids)], axis=0).astype(BF16)
    load_weight.wait()
    for j in range(X):
        copy = pltpu.make_async_copy(
            weight.at[:, pl.ds(j * CORES * DS, CORES * DS)],
            out_hbm.at[j, :, pl.ds(slots, CORES * DS)],
            sems.at[4 + j],
        )
        copy.start()
        others.append(copy)
    for i in range(4):
        loads[i].wait()
        rows = slice(i * piece, (i + 1) * piece)
        turned[:, rows] = hidden[rows, :].astype(F32).T.astype(BF16)
        for j in range(X):
            copy = pltpu.make_async_copy(
                turned.at[:, pieces[i]], out_hbm.at[j, :, pieces[i]], sems.at[11 + i * X + j]
            )
            copy.start()
            others.append(copy)
    for copy in others:
        copy.wait()


def exchange_blocks(head, ids, grad, hidden, weight):
    width = weight.shape[0]
    far = pl.BlockSpec(memory_space=pltpu.HBM)
    return pl.pallas_call(
        exchange_kernel,
        out_shape=(
            pltpu.HBM((X, width, EXPERTS * CAP + CORES * DS), BF16),
            jax.ShapeDtypeStruct((TOK + 16, DS), BF16),
        ),
        in_specs=[
            pl.BlockSpec(memory_space=pltpu.SMEM),
            far,
            far,
            far,
            far,
        ],
        out_specs=(far, pl.BlockSpec(memory_space=pltpu.VMEM)),
        scratch_shapes=[
            pltpu.VMEM(ids.shape, jnp.int32),
            pltpu.VMEM(hidden.shape, BF16),
            pltpu.VMEM(weight.shape, BF16),
            pltpu.VMEM((width, EXPERTS * CAP), BF16),
            pltpu.SemaphoreType.DMA((11 + 4 * X,)),
        ],
        compiler_params=pltpu.CompilerParams(vmem_limit_bytes=16 << 20),
    )(head, in_hbm(ids), in_hbm(grad), in_hbm(hidden), in_hbm(weight))


def mix_kernel(
    core_ref, mine_ref, theirs_ref, ids_ref, logits_ref, out_hbm, key_ref, probs_ref, out_ref, rounded, sems
):
    plan(ids_ref[...], logits_ref[...], key_ref, probs_ref)
    slots = EXPERTS * CAP
    core = core_ref[0]
    weight = jnp.where(
        core == 0, mine_ref[:, slots : slots + DS], mine_ref[:, slots + DS : slots + 2 * DS]
    )
    group = ZH * ZL * CAP
    contract = (((0,), (0,)), ((), ()))
    copies = []
    for y in range(Y):
        cols = slice(y * group, (y + 1) * group)
        mixed = lax.dot_general(
            mine_ref[:, cols], weight, contract, preferred_element_type=F32
        ) + lax.dot_general(
            theirs_ref[:, cols], theirs_ref[:, slots:], contract, preferred_element_type=F32
        )
        for zl in range(ZL):
            place = zl ^ (2 * core)
            for zh in range(ZH):
                src = (zh * ZL + zl) * CAP
                dst = pl.multiple_of(y * group + (place * ZH + zh) * CAP, 8)
                out_ref[pl.ds(dst, CAP), :] = mixed[src : src + CAP, :]
        rows = pl.ds(y * group, group)
        rounded[rows, :] = out_ref[rows, :].astype(BF16)
        copies.append(pltpu.make_async_copy(rounded.at[rows], out_hbm.at[rows], sems.at[y]))
        copies[-1].start()
    for copy in copies:
        copy.wait()


def plan(ids, logits, key_ref, probs_ref):
    raised = jnp.exp(logits)
    probs = raised / jnp.sum(raised, axis=0, keepdims=True)
    expert = lax.broadcasted_iota(jnp.int32, (EXPERTS, TOK), 0)
    hits = jnp.zeros((EXPERTS, TOK), F32)
    spread = jnp.zeros((EXPERTS, TOK), F32)
    for k in range(TOPK):
        mine = ids[k : k + 1, :] == expert
        hits = hits + mine.astype(F32)
        spread = spread + jnp.where(mine, probs[k : k + 1, :], 0.0)
    earlier = lax.broadcasted_iota(jnp.int32, (TOK, TOK), 0) < lax.broadcasted_iota(
        jnp.int32, (TOK, TOK), 1
    )
    before = jnp.dot(hits.astype(BF16), earlier.astype(BF16), preferred_element_type=F32)
    key_ref[...] = jnp.where(hits > 0, before, -1.0)
    probs_ref[...] = spread


def mix(core, mine, theirs, ids, logits):
    table = pltpu.VMEM((EXPERTS, TOK), F32)
    return pl.pallas_call(
        mix_kernel,
        out_shape=(pltpu.HBM((EXPERTS * CAP, DS), BF16), table, table),
        in_specs=[pl.BlockSpec(memory_space=pltpu.SMEM)]
        + [pl.BlockSpec(memory_space=pltpu.VMEM)] * 4,
        out_specs=(pl.BlockSpec(memory_space=pltpu.HBM),) + (pl.BlockSpec(memory_space=pltpu.VMEM),) * 2,
        scratch_shapes=[
            pltpu.VMEM((EXPERTS * CAP, DS), F32),
            pltpu.VMEM((EXPERTS * CAP, DS), BF16),
            pltpu.SemaphoreType.DMA((Y,)),
        ],
        compiler_params=pltpu.CompilerParams(vmem_limit_bytes=16 << 20),
    )(core, mine, theirs, ids, logits)


def value_kernel(core_ref, rows_hbm, mixed_hbm, out_ref, rows_ref, mixed_ref, sems):
    steps = 4
    per = NEAR // steps
    copies = []
    for i in range(steps):
        near, slots = pl.ds(i * per, per), pl.ds(i * per * ZH * CAP, per * ZH * CAP)
        copies.append(
            (
                pltpu.make_async_copy(rows_hbm.at[near], rows_ref.at[near], sems.at[0, i]),
                pltpu.make_async_copy(mixed_hbm.at[slots], mixed_ref.at[slots], sems.at[1, i]),
            )
        )
    for pair in copies:
        for copy in pair:
            copy.start()
    own_lane = lax.broadcasted_iota(jnp.int32, (CAP, 128), 0) == lax.broadcasted_iota(
        jnp.int32, (CAP, 128), 1
    )
    for i in range(steps):
        for copy in copies[i]:
            copy.wait()
        for e in range(i * per, (i + 1) * per):
            rows = rows_ref[e].astype(F32) * mixed_ref[
                e * ZH * CAP : (e + 1) * ZH * CAP, :
            ].astype(F32)
            sums = jnp.sum(rows[:, 0:128] + rows[:, 128:256], axis=1, keepdims=True)
            for b in range(ZH):
                lanes = jnp.where(own_lane, sums[b * CAP : (b + 1) * CAP, :], 0.0)
                place = (e // ZL * ZH + b) * ZL + ((e % ZL) ^ (2 * core_ref[0]))
                out_ref[place] = jnp.sum(lanes, axis=0, keepdims=True)


def slot_sums(core, rows, mixed):
    return pl.pallas_call(
        value_kernel,
        out_shape=jax.ShapeDtypeStruct((EXPERTS, 1, 128), F32),
        in_specs=[
            pl.BlockSpec(memory_space=pltpu.SMEM),
            pl.BlockSpec(memory_space=pltpu.HBM),
            pl.BlockSpec(memory_space=pltpu.HBM),
        ],
        out_specs=pl.BlockSpec(memory_space=pltpu.VMEM),
        scratch_shapes=[
            pltpu.VMEM(rows.shape, BF16),
            pltpu.VMEM(mixed.shape, BF16),
            pltpu.SemaphoreType.DMA((2, 4)),
        ],
        compiler_params=pltpu.CompilerParams(vmem_limit_bytes=16 << 20),
    )(core, in_hbm(rows), in_hbm(mixed))


def final_kernel(
    parts_ref, key_ref, probs_ref, ids_ref, router_hbm, grad_ref, weight_ref,
    router_ref, total, sem,
):
    load_router = pltpu.make_async_copy(router_hbm, router_ref, sem)
    load_router.start()
    parts = parts_ref[0]
    for i in range(1, X):
        parts = parts + parts_ref[i]
    total[...] = parts.reshape(EXPERTS, 128)
    back = total[...]
    key = key_ref[...]
    probs = probs_ref[...]
    dense = jnp.zeros((EXPERTS, TOK), F32)
    for c in range(CAP):
        dense = jnp.where(key == float(c), back[:, c : c + 1], dense)
    mean = jnp.sum(probs * dense, axis=0, keepdims=True)
    logit = (probs * (dense - mean)).astype(BF16)
    load_router.wait()
    grad_ref[...] = lax.dot_general(
        logit, router_ref[...], (((0,), (0,)), ((), ())), preferred_element_type=F32
    ).astype(BF16)
    ids = ids_ref[...]
    expert = lax.broadcasted_iota(jnp.int32, (EXPERTS, TOK), 0)
    for k in range(TOPK):
        weight_ref[k : k + 1, :] = jnp.sum(
            jnp.where(ids[k : k + 1, :] == expert, dense, 0.0), axis=0, keepdims=True
        )


def finish(parts, key, probs, ids, router):
    far, near = pl.BlockSpec(memory_space=pltpu.HBM), pl.BlockSpec(memory_space=pltpu.VMEM)
    return pl.pallas_call(
        final_kernel,
        out_shape=(
            jax.ShapeDtypeStruct((TOK, DS), BF16),
            jax.ShapeDtypeStruct((TOPK, TOK), F32),
        ),
        in_specs=[near, near, near, near, far],
        out_specs=(near, near),
        scratch_shapes=[
            pltpu.VMEM(router.shape, BF16),
            pltpu.VMEM((EXPERTS, 128), F32),
            pltpu.SemaphoreType.DMA(()),
        ],
        compiler_params=pltpu.CompilerParams(vmem_limit_bytes=16 << 20),
    )(in_vmem(parts), in_vmem(key), in_vmem(probs), ids, in_hbm(router))


def body(out_grad, expert_ids, chosen_logits, down_weight, saved_hidden, router_weight):
    x, core = lax.axis_index("x"), lax.axis_index("core")
    head = x * CORES + core
    width = down_weight.shape[1]
    slots = EXPERTS * CAP
    ids, logits = expert_ids.T, chosen_logits.T
    along, block = exchange_blocks(
        head.reshape(1).astype(jnp.int32),
        ids,
        out_grad,
        saved_hidden[0].reshape(slots, width),
        down_weight[0],
    )
    along = lax.all_to_all(along, "x", split_axis=0, concat_axis=0, tiled=True)
    mine = along.reshape(X * width, slots + CORES * DS)
    weight_other = lax.dynamic_slice_in_dim(mine, slots + (1 - core) * DS, DS, axis=1)
    theirs = lax.ppermute(
        jnp.concatenate([mine[:, :slots], weight_other], axis=1), "core", [(0, 1), (1, 0)]
    )
    core_scalar = core.reshape(1).astype(jnp.int32)
    mixed, key, probs = mix(core_scalar, mine, theirs, ids, logits)
    blocks = lax.all_gather(
        block, ("core", "zh"), axis=0, tiled=False, axis_index_groups=FAR_GROUPS
    )
    z = lax.axis_index("zh") * ZL + lax.axis_index("zl")
    base = ((z - 2 * core) & (ZH * ZL - ZL)) + 2 * core
    outgoing = select_rows(jnp.stack([base, core]).astype(jnp.int32), blocks)
    received = lax.all_to_all(
        outgoing,
        ("core", "y", "zh", "zl"),
        split_axis=0,
        concat_axis=0,
        tiled=True,
        axis_index_groups=NEAR_GROUPS,
    )
    part = slot_sums(core_scalar, received, mixed)
    part = jnp.sum(lax.all_gather(part, "core", axis=0, tiled=False), axis=0)
    part = jnp.broadcast_to(part[None], (X,) + part.shape).reshape(X * EXPERTS, 1, 128)
    part = lax.all_to_all(part, ("x",) + EXPERT, split_axis=0, concat_axis=0, tiled=True)
    part = part.reshape(X, EXPERTS, 1, 128)
    grad, weight_grad = finish(part, key, probs, ids, router_weight.T)
    return grad, weight_grad.T


def solution(mesh):
    fine = Mesh(
        mesh.devices.reshape(X, CORES, Y, ZH, ZL), ("x", "core", "y", "zh", "zl")
    )
    return jax.shard_map(
        body,
        mesh=fine,
        in_specs=(
            P(EXPERT, None),
            P(EXPERT, None),
            P(EXPERT, None),
            P(EXPERT, HEAD, None),
            P(EXPERT, None, None, HEAD),
            P(HEAD, None),
        ),
        out_specs=(P(EXPERT, HEAD), P(EXPERT, None)),
        check_vma=False,
    )
```

```python
import jax
import jax.numpy as jnp
from jax import lax
from jax.experimental import pallas as pl
from jax.experimental.pallas import tpu as pltpu
from jax.sharding import Mesh, PartitionSpec as P

X, CORES, Y, ZH, ZL = 4, 2, 4, 4, 4
EXPERT = ("y", "zh", "zl")
HEAD = ("x", "core")
TOK = 256
CAP = 40
TOPK = 8
EXPERTS = 64
DS = 256
NEAR = Y * ZL
F32 = jnp.float32
NEAR_GROUPS = [
    [c * Y * ZH * ZL + y * ZH * ZL + (q * ZL + r + 2 * c) % (ZH * ZL) for y in range(Y) for r in range(ZL)]
    for c in range(CORES)
    for q in range(ZH)
]
BF16 = jnp.bfloat16


def in_vmem(array):
    return pltpu.with_memory_space_constraint(array, pltpu.VMEM)


def in_hbm(array):
    return pltpu.with_memory_space_constraint(array, pltpu.HBM)


def select_kernel(base_ref, blocks_ref, out_hbm, picked, rows_out, sems):
    base = base_ref[0]
    j = lax.broadcasted_iota(jnp.int32, (NEAR, TOK), 0)
    expert = ((j // ZL) * (ZH * ZL) + ((base + j % ZL) & (ZH * ZL - 1))).astype(F32)
    hits = []
    for b in range(ZH):
        ids = blocks_ref[b, TOK : TOK + 16, :].astype(F32)
        hit = jnp.zeros((NEAR, TOK), F32)
        for k in range(TOPK):
            hit = hit + (ids[k : k + 1, :] == expert).astype(F32)
        hits.append(hit)
    hits = jnp.concatenate(hits, axis=0)
    earlier = lax.broadcasted_iota(jnp.int32, (TOK, TOK), 0) < lax.broadcasted_iota(
        jnp.int32, (TOK, TOK), 1
    )
    before = jnp.dot(hits.astype(BF16), earlier.astype(BF16), preferred_element_type=F32)
    key = jnp.where(hits > 0, before, -1.0)
    slot = lax.broadcasted_iota(jnp.int32, (CAP, TOK), 0).astype(F32)
    copies = []
    for y in range(Y):
        for b in range(ZH):
            first = b * NEAR + y * ZL
            pick = jnp.concatenate(
                [(key[e : e + 1, :] == slot).astype(F32) for e in range(first, first + ZL)], axis=0
            )
            picked[b] = jnp.dot(
                pick.astype(BF16), blocks_ref[b, 0:TOK, :], preferred_element_type=F32
            )
        for e in range(ZL):
            rows = [picked[b, e * CAP : (e + 1) * CAP, :] for b in range(ZH)]
            rows_out[y * ZL + e] = jnp.concatenate(rows, axis=0).astype(BF16)
        near = pl.ds(y * ZL, ZL)
        copies.append(pltpu.make_async_copy(rows_out.at[near], out_hbm.at[near], sems.at[y]))
        copies[-1].start()
    for copy in copies:
        copy.wait()


def select_rows(base, blocks):
    return pl.pallas_call(
        select_kernel,
        out_shape=pltpu.HBM((NEAR, ZH * CAP, DS), BF16),
        in_specs=[
            pl.BlockSpec(memory_space=pltpu.SMEM),
            pl.BlockSpec(memory_space=pltpu.VMEM),
        ],
        out_specs=pl.BlockSpec(memory_space=pltpu.HBM),
        scratch_shapes=[
            pltpu.VMEM((ZH, ZL * CAP, DS), F32),
            pltpu.VMEM((NEAR, ZH * CAP, DS), BF16),
            pltpu.SemaphoreType.DMA((Y,)),
        ],
        compiler_params=pltpu.CompilerParams(vmem_limit_bytes=16 << 20),
    )(base, blocks)


def exchange_kernel(
    head_ref, ids_hbm, grad_hbm, hidden_hbm, weight_hbm, out_hbm, block_ref, ids_ref, hidden, weight, turned, sems
):
    slots = EXPERTS * CAP
    piece = slots // 4
    pieces = [pl.ds(i * piece, piece) for i in range(4)]
    loads = [
        pltpu.make_async_copy(hidden_hbm.at[pieces[i]], hidden.at[pieces[i]], sems.at[i])
        for i in range(4)
    ]
    columns = pl.ds(pl.multiple_of(head_ref[0] * DS, DS), DS)
    load_weight = pltpu.make_async_copy(weight_hbm, weight, sems.at[10])
    load_ids = pltpu.make_async_copy(ids_hbm, ids_ref, sems.at[9])
    load_grad = pltpu.make_async_copy(
        grad_hbm.at[:, columns], block_ref.at[pl.ds(0, TOK)], sems.at[8]
    )
    for copy in [load_weight] + loads + [load_ids, load_grad]:
        copy.start()
    others = [load_grad]
    load_ids.wait()
    ids = ids_ref[...].astype(F32)
    block_ref[TOK : TOK + 16, :] = jnp.concatenate([ids, jnp.zeros_like(ids)], axis=0).astype(BF16)
    load_weight.wait()
    for j in range(X):
        copy = pltpu.make_async_copy(
            weight.at[:, pl.ds(j * CORES * DS, CORES * DS)],
            out_hbm.at[j, :, pl.ds(slots, CORES * DS)],
            sems.at[4 + j],
        )
        copy.start()
        others.append(copy)
    for i in range(4):
        loads[i].wait()
        rows = slice(i * piece, (i + 1) * piece)
        turned[:, rows] = hidden[rows, :].astype(F32).T.astype(BF16)
        for j in range(X):
            copy = pltpu.make_async_copy(
                turned.at[:, pieces[i]], out_hbm.at[j, :, pieces[i]], sems.at[11 + i * X + j]
            )
            copy.start()
            others.append(copy)
    for copy in others:
        copy.wait()


def exchange_blocks(head, ids, grad, hidden, weight):
    width = weight.shape[0]
    far = pl.BlockSpec(memory_space=pltpu.HBM)
    return pl.pallas_call(
        exchange_kernel,
        out_shape=(
            pltpu.HBM((X, width, EXPERTS * CAP + CORES * DS), BF16),
            jax.ShapeDtypeStruct((TOK + 16, DS), BF16),
        ),
        in_specs=[
            pl.BlockSpec(memory_space=pltpu.SMEM),
            far,
            far,
            far,
            far,
        ],
        out_specs=(far, pl.BlockSpec(memory_space=pltpu.VMEM)),
        scratch_shapes=[
            pltpu.VMEM(ids.shape, jnp.int32),
            pltpu.VMEM(hidden.shape, BF16),
            pltpu.VMEM(weight.shape, BF16),
            pltpu.VMEM((width, EXPERTS * CAP), BF16),
            pltpu.SemaphoreType.DMA((11 + 4 * X,)),
        ],
        compiler_params=pltpu.CompilerParams(vmem_limit_bytes=16 << 20),
    )(head, in_hbm(ids), in_hbm(grad), in_hbm(hidden), in_hbm(weight))


def mix_kernel(
    core_ref, mine_ref, theirs_ref, ids_ref, logits_ref, out_hbm, key_ref, probs_ref, out_ref, rounded, sems
):
    plan(ids_ref[...], logits_ref[...], key_ref, probs_ref)
    slots = EXPERTS * CAP
    core = core_ref[0]
    weight = jnp.where(
        core == 0, mine_ref[:, slots : slots + DS], mine_ref[:, slots + DS : slots + 2 * DS]
    )
    group = ZH * ZL * CAP
    contract = (((0,), (0,)), ((), ()))
    copies = []
    for y in range(Y):
        cols = slice(y * group, (y + 1) * group)
        mixed = lax.dot_general(
            mine_ref[:, cols], weight, contract, preferred_element_type=F32
        ) + lax.dot_general(
            theirs_ref[:, cols], theirs_ref[:, slots:], contract, preferred_element_type=F32
        )
        for zl in range(ZL):
            place = zl ^ (2 * core)
            for zh in range(ZH):
                src = (zh * ZL + zl) * CAP
                dst = pl.multiple_of(y * group + (place * ZH + zh) * CAP, 8)
                out_ref[pl.ds(dst, CAP), :] = mixed[src : src + CAP, :]
        rows = pl.ds(y * group, group)
        rounded[rows, :] = out_ref[rows, :].astype(BF16)
        copies.append(pltpu.make_async_copy(rounded.at[rows], out_hbm.at[rows], sems.at[y]))
        copies[-1].start()
    for copy in copies:
        copy.wait()


def plan(ids, logits, key_ref, probs_ref):
    raised = jnp.exp(logits)
    probs = raised / jnp.sum(raised, axis=0, keepdims=True)
    expert = lax.broadcasted_iota(jnp.int32, (EXPERTS, TOK), 0)
    hits = jnp.zeros((EXPERTS, TOK), F32)
    spread = jnp.zeros((EXPERTS, TOK), F32)
    for k in range(TOPK):
        mine = ids[k : k + 1, :] == expert
        hits = hits + mine.astype(F32)
        spread = spread + jnp.where(mine, probs[k : k + 1, :], 0.0)
    earlier = lax.broadcasted_iota(jnp.int32, (TOK, TOK), 0) < lax.broadcasted_iota(
        jnp.int32, (TOK, TOK), 1
    )
    before = jnp.dot(hits.astype(BF16), earlier.astype(BF16), preferred_element_type=F32)
    key_ref[...] = jnp.where(hits > 0, before, -1.0)
    probs_ref[...] = spread


def mix(core, mine, theirs, ids, logits):
    table = pltpu.VMEM((EXPERTS, TOK), F32)
    return pl.pallas_call(
        mix_kernel,
        out_shape=(pltpu.HBM((EXPERTS * CAP, DS), BF16), table, table),
        in_specs=[pl.BlockSpec(memory_space=pltpu.SMEM)]
        + [pl.BlockSpec(memory_space=pltpu.VMEM)] * 4,
        out_specs=(pl.BlockSpec(memory_space=pltpu.HBM),) + (pl.BlockSpec(memory_space=pltpu.VMEM),) * 2,
        scratch_shapes=[
            pltpu.VMEM((EXPERTS * CAP, DS), F32),
            pltpu.VMEM((EXPERTS * CAP, DS), BF16),
            pltpu.SemaphoreType.DMA((Y,)),
        ],
        compiler_params=pltpu.CompilerParams(vmem_limit_bytes=16 << 20),
    )(core, mine, theirs, ids, logits)


def value_kernel(core_ref, rows_hbm, mixed_hbm, out_ref, rows_ref, mixed_ref, sems):
    steps = 4
    per = NEAR // steps
    copies = []
    for i in range(steps):
        near, slots = pl.ds(i * per, per), pl.ds(i * per * ZH * CAP, per * ZH * CAP)
        copies.append(
            (
                pltpu.make_async_copy(rows_hbm.at[near], rows_ref.at[near], sems.at[0, i]),
                pltpu.make_async_copy(mixed_hbm.at[slots], mixed_ref.at[slots], sems.at[1, i]),
            )
        )
    for pair in copies:
        for copy in pair:
            copy.start()
    own_lane = lax.broadcasted_iota(jnp.int32, (CAP, 128), 0) == lax.broadcasted_iota(
        jnp.int32, (CAP, 128), 1
    )
    for i in range(steps):
        for copy in copies[i]:
            copy.wait()
        for e in range(i * per, (i + 1) * per):
            rows = rows_ref[e].astype(F32) * mixed_ref[
                e * ZH * CAP : (e + 1) * ZH * CAP, :
            ].astype(F32)
            sums = jnp.sum(rows[:, 0:128] + rows[:, 128:256], axis=1, keepdims=True)
            for b in range(ZH):
                lanes = jnp.where(own_lane, sums[b * CAP : (b + 1) * CAP, :], 0.0)
                place = (e // ZL * ZH + b) * ZL + ((e % ZL) ^ (2 * core_ref[0]))
                out_ref[place] = jnp.sum(lanes, axis=0, keepdims=True)


def slot_sums(core, rows, mixed):
    return pl.pallas_call(
        value_kernel,
        out_shape=jax.ShapeDtypeStruct((EXPERTS, 1, 128), F32),
        in_specs=[
            pl.BlockSpec(memory_space=pltpu.SMEM),
            pl.BlockSpec(memory_space=pltpu.HBM),
            pl.BlockSpec(memory_space=pltpu.HBM),
        ],
        out_specs=pl.BlockSpec(memory_space=pltpu.VMEM),
        scratch_shapes=[
            pltpu.VMEM(rows.shape, BF16),
            pltpu.VMEM(mixed.shape, BF16),
            pltpu.SemaphoreType.DMA((2, 4)),
        ],
        compiler_params=pltpu.CompilerParams(vmem_limit_bytes=16 << 20),
    )(core, in_hbm(rows), in_hbm(mixed))


def head_sum_kernel(parts_ref, out_ref):
    for y in range(Y):
        total = parts_ref[0, y]
        for i in range(1, X * CORES):
            total = total + parts_ref[i, y]
        for z in range(ZH * ZL):
            out_ref[z, :, y * 128 : (y + 1) * 128] = total[z : z + 1, :]


def head_sums(parts):
    return pl.pallas_call(
        head_sum_kernel,
        out_shape=jax.ShapeDtypeStruct((ZH * ZL, 1, Y * 128), F32),
    )(in_vmem(parts))


def final_kernel(
    parts_ref, key_ref, probs_ref, ids_ref, router_hbm, grad_ref, weight_ref,
    router_ref, total, sem,
):
    load_router = pltpu.make_async_copy(router_hbm, router_ref, sem)
    load_router.start()
    for y in range(Y):
        total[y * ZH * ZL : (y + 1) * ZH * ZL, :] = parts_ref[:, 0, y * 128 : (y + 1) * 128]
    back = total[...]
    key = key_ref[...]
    probs = probs_ref[...]
    dense = jnp.zeros((EXPERTS, TOK), F32)
    for c in range(CAP):
        dense = jnp.where(key == float(c), back[:, c : c + 1], dense)
    mean = jnp.sum(probs * dense, axis=0, keepdims=True)
    logit = (probs * (dense - mean)).astype(BF16)
    load_router.wait()
    grad_ref[...] = lax.dot_general(
        logit, router_ref[...], (((0,), (0,)), ((), ())), preferred_element_type=F32
    ).astype(BF16)
    ids = ids_ref[...]
    expert = lax.broadcasted_iota(jnp.int32, (EXPERTS, TOK), 0)
    for k in range(TOPK):
        weight_ref[k : k + 1, :] = jnp.sum(
            jnp.where(ids[k : k + 1, :] == expert, dense, 0.0), axis=0, keepdims=True
        )


def finish(parts, key, probs, ids, router):
    far, near = pl.BlockSpec(memory_space=pltpu.HBM), pl.BlockSpec(memory_space=pltpu.VMEM)
    return pl.pallas_call(
        final_kernel,
        out_shape=(
            jax.ShapeDtypeStruct((TOK, DS), BF16),
            jax.ShapeDtypeStruct((TOPK, TOK), F32),
        ),
        in_specs=[near, near, near, near, far],
        out_specs=(near, near),
        scratch_shapes=[
            pltpu.VMEM(router.shape, BF16),
            pltpu.VMEM((EXPERTS, 128), F32),
            pltpu.SemaphoreType.DMA(()),
        ],
        compiler_params=pltpu.CompilerParams(vmem_limit_bytes=16 << 20),
    )(in_vmem(parts), in_vmem(key), in_vmem(probs), ids, in_hbm(router))


def body(out_grad, expert_ids, chosen_logits, down_weight, saved_hidden, router_weight):
    x, core = lax.axis_index("x"), lax.axis_index("core")
    head = x * CORES + core
    width = down_weight.shape[1]
    slots = EXPERTS * CAP
    ids, logits = expert_ids.T, chosen_logits.T
    along, block = exchange_blocks(
        head.reshape(1).astype(jnp.int32),
        ids,
        out_grad,
        saved_hidden[0].reshape(slots, width),
        down_weight[0],
    )
    along = lax.all_to_all(along, "x", split_axis=0, concat_axis=0, tiled=True)
    mine = along.reshape(X * width, slots + CORES * DS)
    weight_other = lax.dynamic_slice_in_dim(mine, slots + (1 - core) * DS, DS, axis=1)
    theirs = lax.ppermute(
        jnp.concatenate([mine[:, :slots], weight_other], axis=1), "core", [(0, 1), (1, 0)]
    )
    core_scalar = core.reshape(1).astype(jnp.int32)
    mixed, key, probs = mix(core_scalar, mine, theirs, ids, logits)
    blocks = lax.all_gather(block, "zh", axis=0, tiled=False)
    z = lax.axis_index("zh") * ZL + lax.axis_index("zl")
    base = ((z - 2 * core) & (ZH * ZL - ZL)) + 2 * core
    outgoing = select_rows(base.reshape(1).astype(jnp.int32), blocks)
    received = lax.all_to_all(
        outgoing,
        ("core", "y", "zh", "zl"),
        split_axis=0,
        concat_axis=0,
        tiled=True,
        axis_index_groups=NEAR_GROUPS,
    )
    part = slot_sums(core_scalar, received, mixed)
    part = part.reshape(1, Y, ZH * ZL, 128)
    part = jnp.broadcast_to(part, (X * CORES,) + part.shape[1:])
    part = lax.all_to_all(
        part.reshape(X * CORES * Y, ZH * ZL, 128),
        ("x", "core", "y"),
        split_axis=0,
        concat_axis=0,
        tiled=True,
    )
    part = head_sums(part.reshape(X * CORES, Y, ZH * ZL, 128))
    part = lax.all_to_all(part, ("zh", "zl"), split_axis=0, concat_axis=0, tiled=True)
    grad, weight_grad = finish(part, key, probs, ids, router_weight.T)
    return grad, weight_grad.T


def solution(mesh):
    fine = Mesh(
        mesh.devices.reshape(X, CORES, Y, ZH, ZL), ("x", "core", "y", "zh", "zl")
    )
    return jax.shard_map(
        body,
        mesh=fine,
        in_specs=(
            P(EXPERT, None),
            P(EXPERT, None),
            P(EXPERT, None),
            P(EXPERT, HEAD, None),
            P(EXPERT, None, None, HEAD),
            P(HEAD, None),
        ),
        out_specs=(P(EXPERT, HEAD), P(EXPERT, None)),
        check_vma=False,
    )
```

```python
import jax
import jax.numpy as jnp
from jax import lax
from jax.experimental import pallas as pl
from jax.experimental.pallas import tpu as pltpu
from jax.sharding import Mesh, PartitionSpec as P

X, CORES, Y, ZH, ZL = 4, 2, 4, 4, 4
EXPERT = ("y", "zh", "zl")
HEAD = ("x", "core")
TOK = 256
CAP = 40
TOPK = 8
EXPERTS = 64
DS = 256
NEAR = Y * ZL
F32 = jnp.float32
NEAR_GROUPS = [
    [c * Y * ZH * ZL + y * ZH * ZL + (q * ZL + r + 2 * c) % (ZH * ZL) for y in range(Y) for r in range(ZL)]
    for c in range(CORES)
    for q in range(ZH)
]
BF16 = jnp.bfloat16


def in_vmem(array):
    return pltpu.with_memory_space_constraint(array, pltpu.VMEM)


def in_hbm(array):
    return pltpu.with_memory_space_constraint(array, pltpu.HBM)


def select_kernel(base_ref, blocks_ref, out_hbm, picked, rows_out, sems):
    base = base_ref[0]
    j = lax.broadcasted_iota(jnp.int32, (NEAR, TOK), 0)
    expert = ((j // ZL) * (ZH * ZL) + ((base + j % ZL) & (ZH * ZL - 1))).astype(F32)
    hits = []
    for b in range(ZH):
        ids = blocks_ref[b, TOK : TOK + 16, :].astype(F32)
        hit = jnp.zeros((NEAR, TOK), F32)
        for k in range(TOPK):
            hit = hit + (ids[k : k + 1, :] == expert).astype(F32)
        hits.append(hit)
    hits = jnp.concatenate(hits, axis=0)
    earlier = lax.broadcasted_iota(jnp.int32, (TOK, TOK), 0) < lax.broadcasted_iota(
        jnp.int32, (TOK, TOK), 1
    )
    before = jnp.dot(hits.astype(BF16), earlier.astype(BF16), preferred_element_type=F32)
    key = jnp.where(hits > 0, before, -1.0)
    slot = lax.broadcasted_iota(jnp.int32, (CAP, TOK), 0).astype(F32)
    copies = []
    for y in range(Y):
        for b in range(ZH):
            first = b * NEAR + y * ZL
            pick = jnp.concatenate(
                [(key[e : e + 1, :] == slot).astype(F32) for e in range(first, first + ZL)], axis=0
            )
            picked[b] = jnp.dot(
                pick.astype(BF16), blocks_ref[b, 0:TOK, :], preferred_element_type=F32
            )
        for e in range(ZL):
            rows = [picked[b, e * CAP : (e + 1) * CAP, :] for b in range(ZH)]
            rows_out[y * ZL + e] = jnp.concatenate(rows, axis=0).astype(BF16)
        near = pl.ds(y * ZL, ZL)
        copies.append(pltpu.make_async_copy(rows_out.at[near], out_hbm.at[near], sems.at[y]))
        copies[-1].start()
    for copy in copies:
        copy.wait()


def select_rows(base, blocks):
    return pl.pallas_call(
        select_kernel,
        out_shape=pltpu.HBM((NEAR, ZH * CAP, DS), BF16),
        in_specs=[
            pl.BlockSpec(memory_space=pltpu.SMEM),
            pl.BlockSpec(memory_space=pltpu.VMEM),
        ],
        out_specs=pl.BlockSpec(memory_space=pltpu.HBM),
        scratch_shapes=[
            pltpu.VMEM((ZH, ZL * CAP, DS), F32),
            pltpu.VMEM((NEAR, ZH * CAP, DS), BF16),
            pltpu.SemaphoreType.DMA((Y,)),
        ],
        compiler_params=pltpu.CompilerParams(vmem_limit_bytes=16 << 20),
    )(base, blocks)


def exchange_kernel(
    head_ref, ids_hbm, grad_hbm, hidden_hbm, weight_hbm, out_hbm, block_ref, ids_ref, hidden, weight, turned, sems
):
    slots = EXPERTS * CAP
    piece = slots // 4
    pieces = [pl.ds(i * piece, piece) for i in range(4)]
    loads = [
        pltpu.make_async_copy(hidden_hbm.at[pieces[i]], hidden.at[pieces[i]], sems.at[i])
        for i in range(4)
    ]
    columns = pl.ds(pl.multiple_of(head_ref[0] * DS, DS), DS)
    load_weight = pltpu.make_async_copy(weight_hbm, weight, sems.at[10])
    load_ids = pltpu.make_async_copy(ids_hbm, ids_ref, sems.at[9])
    load_grad = pltpu.make_async_copy(
        grad_hbm.at[:, columns], block_ref.at[pl.ds(0, TOK)], sems.at[8]
    )
    for copy in [load_weight] + loads + [load_ids, load_grad]:
        copy.start()
    others = [load_grad]
    load_ids.wait()
    ids = ids_ref[...].astype(F32)
    block_ref[TOK : TOK + 16, :] = jnp.concatenate([ids, jnp.zeros_like(ids)], axis=0).astype(BF16)
    load_weight.wait()
    for j in range(X):
        copy = pltpu.make_async_copy(
            weight.at[:, pl.ds(j * CORES * DS, CORES * DS)],
            out_hbm.at[j, :, pl.ds(slots, CORES * DS)],
            sems.at[4 + j],
        )
        copy.start()
        others.append(copy)
    for i in range(4):
        loads[i].wait()
        rows = slice(i * piece, (i + 1) * piece)
        turned[:, rows] = hidden[rows, :].astype(F32).T.astype(BF16)
        for j in range(X):
            copy = pltpu.make_async_copy(
                turned.at[:, pieces[i]], out_hbm.at[j, :, pieces[i]], sems.at[11 + i * X + j]
            )
            copy.start()
            others.append(copy)
    for copy in others:
        copy.wait()


def exchange_blocks(head, ids, grad, hidden, weight):
    width = weight.shape[0]
    far = pl.BlockSpec(memory_space=pltpu.HBM)
    return pl.pallas_call(
        exchange_kernel,
        out_shape=(
            pltpu.HBM((X, width, EXPERTS * CAP + CORES * DS), BF16),
            jax.ShapeDtypeStruct((TOK + 16, DS), BF16),
        ),
        in_specs=[
            pl.BlockSpec(memory_space=pltpu.SMEM),
            far,
            far,
            far,
            far,
        ],
        out_specs=(far, pl.BlockSpec(memory_space=pltpu.VMEM)),
        scratch_shapes=[
            pltpu.VMEM(ids.shape, jnp.int32),
            pltpu.VMEM(hidden.shape, BF16),
            pltpu.VMEM(weight.shape, BF16),
            pltpu.VMEM((width, EXPERTS * CAP), BF16),
            pltpu.SemaphoreType.DMA((11 + 4 * X,)),
        ],
        compiler_params=pltpu.CompilerParams(vmem_limit_bytes=16 << 20),
    )(head, in_hbm(ids), in_hbm(grad), in_hbm(hidden), in_hbm(weight))


def mix_kernel(
    core_ref, mine_ref, theirs_ref, ids_ref, logits_ref, out_hbm, key_ref, probs_ref, out_ref, rounded, sems
):
    plan(ids_ref[...], logits_ref[...], key_ref, probs_ref)
    slots = EXPERTS * CAP
    core = core_ref[0]
    weight = jnp.where(
        core == 0, mine_ref[:, slots : slots + DS], mine_ref[:, slots + DS : slots + 2 * DS]
    )
    group = ZH * ZL * CAP
    contract = (((0,), (0,)), ((), ()))
    copies = []
    for y in range(Y):
        cols = slice(y * group, (y + 1) * group)
        mixed = lax.dot_general(
            mine_ref[:, cols], weight, contract, preferred_element_type=F32
        ) + lax.dot_general(
            theirs_ref[:, cols], theirs_ref[:, slots:], contract, preferred_element_type=F32
        )
        for zl in range(ZL):
            place = zl ^ (2 * core)
            for zh in range(ZH):
                src = (zh * ZL + zl) * CAP
                dst = pl.multiple_of(y * group + (place * ZH + zh) * CAP, 8)
                out_ref[pl.ds(dst, CAP), :] = mixed[src : src + CAP, :]
        rows = pl.ds(y * group, group)
        rounded[rows, :] = out_ref[rows, :].astype(BF16)
        copies.append(pltpu.make_async_copy(rounded.at[rows], out_hbm.at[rows], sems.at[y]))
        copies[-1].start()
    for copy in copies:
        copy.wait()


def plan(ids, logits, key_ref, probs_ref):
    raised = jnp.exp(logits)
    probs = raised / jnp.sum(raised, axis=0, keepdims=True)
    expert = lax.broadcasted_iota(jnp.int32, (EXPERTS, TOK), 0)
    hits = jnp.zeros((EXPERTS, TOK), F32)
    spread = jnp.zeros((EXPERTS, TOK), F32)
    for k in range(TOPK):
        mine = ids[k : k + 1, :] == expert
        hits = hits + mine.astype(F32)
        spread = spread + jnp.where(mine, probs[k : k + 1, :], 0.0)
    earlier = lax.broadcasted_iota(jnp.int32, (TOK, TOK), 0) < lax.broadcasted_iota(
        jnp.int32, (TOK, TOK), 1
    )
    before = jnp.dot(hits.astype(BF16), earlier.astype(BF16), preferred_element_type=F32)
    key_ref[...] = jnp.where(hits > 0, before, -1.0)
    probs_ref[...] = spread


def mix(core, mine, theirs, ids, logits):
    table = pltpu.VMEM((EXPERTS, TOK), F32)
    return pl.pallas_call(
        mix_kernel,
        out_shape=(pltpu.HBM((EXPERTS * CAP, DS), BF16), table, table),
        in_specs=[pl.BlockSpec(memory_space=pltpu.SMEM)]
        + [pl.BlockSpec(memory_space=pltpu.VMEM)] * 4,
        out_specs=(pl.BlockSpec(memory_space=pltpu.HBM),) + (pl.BlockSpec(memory_space=pltpu.VMEM),) * 2,
        scratch_shapes=[
            pltpu.VMEM((EXPERTS * CAP, DS), F32),
            pltpu.VMEM((EXPERTS * CAP, DS), BF16),
            pltpu.SemaphoreType.DMA((Y,)),
        ],
        compiler_params=pltpu.CompilerParams(vmem_limit_bytes=16 << 20),
    )(core, mine, theirs, ids, logits)


def value_kernel(core_ref, rows_hbm, mixed_hbm, out_ref, rows_ref, mixed_ref, sems):
    steps = 4
    per = NEAR // steps
    copies = []
    for i in range(steps):
        near, slots = pl.ds(i * per, per), pl.ds(i * per * ZH * CAP, per * ZH * CAP)
        copies.append(
            (
                pltpu.make_async_copy(rows_hbm.at[near], rows_ref.at[near], sems.at[0, i]),
                pltpu.make_async_copy(mixed_hbm.at[slots], mixed_ref.at[slots], sems.at[1, i]),
            )
        )
    for pair in copies:
        for copy in pair:
            copy.start()
    slot = lax.broadcasted_iota(jnp.int32, (CAP, 128), 0)
    lane = lax.broadcasted_iota(jnp.int32, (CAP, 128), 1)
    own_lane = (lane == slot, lane == slot + 64)
    for i in range(steps):
        for copy in copies[i]:
            copy.wait()
        for e in range(i * per, (i + 1) * per, 2):
            sums = []
            for odd in range(2):
                rows = rows_ref[e + odd].astype(F32) * mixed_ref[
                    (e + odd) * ZH * CAP : (e + odd + 1) * ZH * CAP, :
                ].astype(F32)
                sums.append(jnp.sum(rows[:, 0:128] + rows[:, 128:256], axis=1, keepdims=True))
            for b in range(ZH):
                slots = slice(b * CAP, (b + 1) * CAP)
                lanes = jnp.where(own_lane[0], sums[0][slots, :], 0.0) + jnp.where(
                    own_lane[1], sums[1][slots, :], 0.0
                )
                place = (e // ZL * ZH + b) * 2 + ((e % ZL // 2) ^ core_ref[0])
                out_ref[place] = jnp.sum(lanes, axis=0, keepdims=True)


def slot_sums(core, rows, mixed):
    return pl.pallas_call(
        value_kernel,
        out_shape=jax.ShapeDtypeStruct((EXPERTS // 2, 1, 128), F32),
        in_specs=[
            pl.BlockSpec(memory_space=pltpu.SMEM),
            pl.BlockSpec(memory_space=pltpu.HBM),
            pl.BlockSpec(memory_space=pltpu.HBM),
        ],
        out_specs=pl.BlockSpec(memory_space=pltpu.VMEM),
        scratch_shapes=[
            pltpu.VMEM(rows.shape, BF16),
            pltpu.VMEM(mixed.shape, BF16),
            pltpu.SemaphoreType.DMA((2, 4)),
        ],
        compiler_params=pltpu.CompilerParams(vmem_limit_bytes=16 << 20),
    )(core, in_hbm(rows), in_hbm(mixed))


def head_sum_kernel(parts_ref, out_ref):
    for y in range(Y):
        total = parts_ref[0, y]
        for i in range(1, X * CORES):
            total = total + parts_ref[i, y]
        turned = pltpu.roll(total, 64, 1)
        for z in range(0, ZH * ZL, 2):
            out_ref[z, :, y * 128 : (y + 1) * 128] = total[z // 2 : z // 2 + 1, :]
            out_ref[z + 1, :, y * 128 : (y + 1) * 128] = turned[z // 2 : z // 2 + 1, :]


def head_sums(parts):
    return pl.pallas_call(
        head_sum_kernel,
        out_shape=jax.ShapeDtypeStruct((ZH * ZL, 1, Y * 128), F32),
    )(in_vmem(parts))


def final_kernel(
    parts_ref, key_ref, probs_ref, ids_ref, router_hbm, grad_ref, weight_ref,
    router_ref, total, sem,
):
    load_router = pltpu.make_async_copy(router_hbm, router_ref, sem)
    load_router.start()
    for y in range(Y):
        total[y * ZH * ZL : (y + 1) * ZH * ZL, :] = parts_ref[:, 0, y * 128 : (y + 1) * 128]
    back = total[...]
    key = key_ref[...]
    probs = probs_ref[...]
    dense = jnp.zeros((EXPERTS, TOK), F32)
    for c in range(CAP):
        dense = jnp.where(key == float(c), back[:, c : c + 1], dense)
    mean = jnp.sum(probs * dense, axis=0, keepdims=True)
    logit = (probs * (dense - mean)).astype(BF16)
    load_router.wait()
    grad_ref[...] = lax.dot_general(
        logit, router_ref[...], (((0,), (0,)), ((), ())), preferred_element_type=F32
    ).astype(BF16)
    ids = ids_ref[...]
    expert = lax.broadcasted_iota(jnp.int32, (EXPERTS, TOK), 0)
    for k in range(TOPK):
        weight_ref[k : k + 1, :] = jnp.sum(
            jnp.where(ids[k : k + 1, :] == expert, dense, 0.0), axis=0, keepdims=True
        )


def finish(parts, key, probs, ids, router):
    far, near = pl.BlockSpec(memory_space=pltpu.HBM), pl.BlockSpec(memory_space=pltpu.VMEM)
    return pl.pallas_call(
        final_kernel,
        out_shape=(
            jax.ShapeDtypeStruct((TOK, DS), BF16),
            jax.ShapeDtypeStruct((TOPK, TOK), F32),
        ),
        in_specs=[near, near, near, near, far],
        out_specs=(near, near),
        scratch_shapes=[
            pltpu.VMEM(router.shape, BF16),
            pltpu.VMEM((EXPERTS, 128), F32),
            pltpu.SemaphoreType.DMA(()),
        ],
        compiler_params=pltpu.CompilerParams(vmem_limit_bytes=16 << 20),
    )(in_vmem(parts), in_vmem(key), in_vmem(probs), ids, in_hbm(router))


def body(out_grad, expert_ids, chosen_logits, down_weight, saved_hidden, router_weight):
    x, core = lax.axis_index("x"), lax.axis_index("core")
    head = x * CORES + core
    width = down_weight.shape[1]
    slots = EXPERTS * CAP
    ids, logits = expert_ids.T, chosen_logits.T
    along, block = exchange_blocks(
        head.reshape(1).astype(jnp.int32),
        ids,
        out_grad,
        saved_hidden[0].reshape(slots, width),
        down_weight[0],
    )
    along = lax.all_to_all(along, "x", split_axis=0, concat_axis=0, tiled=True)
    mine = along.reshape(X * width, slots + CORES * DS)
    weight_other = lax.dynamic_slice_in_dim(mine, slots + (1 - core) * DS, DS, axis=1)
    theirs = lax.ppermute(
        jnp.concatenate([mine[:, :slots], weight_other], axis=1), "core", [(0, 1), (1, 0)]
    )
    core_scalar = core.reshape(1).astype(jnp.int32)
    mixed, key, probs = mix(core_scalar, mine, theirs, ids, logits)
    blocks = lax.all_gather(block, "zh", axis=0, tiled=False)
    z = lax.axis_index("zh") * ZL + lax.axis_index("zl")
    base = ((z - 2 * core) & (ZH * ZL - ZL)) + 2 * core
    outgoing = select_rows(base.reshape(1).astype(jnp.int32), blocks)
    received = lax.all_to_all(
        outgoing,
        ("core", "y", "zh", "zl"),
        split_axis=0,
        concat_axis=0,
        tiled=True,
        axis_index_groups=NEAR_GROUPS,
    )
    part = slot_sums(core_scalar, received, mixed)
    rows = ZH * ZL // 2
    part = jnp.broadcast_to(part.reshape(1, Y, rows, 128), (X * CORES, Y, rows, 128))
    part = lax.all_to_all(
        part.reshape(X * CORES * Y, rows, 128),
        ("x", "core", "y"),
        split_axis=0,
        concat_axis=0,
        tiled=True,
    )
    part = head_sums(part.reshape(X * CORES, Y, rows, 128))
    part = lax.all_to_all(part, ("zh", "zl"), split_axis=0, concat_axis=0, tiled=True)
    grad, weight_grad = finish(part, key, probs, ids, router_weight.T)
    return grad, weight_grad.T


def solution(mesh):
    fine = Mesh(
        mesh.devices.reshape(X, CORES, Y, ZH, ZL), ("x", "core", "y", "zh", "zl")
    )
    return jax.shard_map(
        body,
        mesh=fine,
        in_specs=(
            P(EXPERT, None),
            P(EXPERT, None),
            P(EXPERT, None),
            P(EXPERT, HEAD, None),
            P(EXPERT, None, None, HEAD),
            P(HEAD, None),
        ),
        out_specs=(P(EXPERT, HEAD), P(EXPERT, None)),
        check_vma=False,
    )
```

```python
import jax
import jax.numpy as jnp
from jax import lax
from jax.experimental import pallas as pl
from jax.experimental.pallas import tpu as pltpu
from jax.sharding import Mesh, PartitionSpec as P

X, CORES, Y, ZH, ZL = 4, 2, 4, 4, 4
EXPERT = ("y", "zh", "zl")
HEAD = ("x", "core")
TOK = 256
CAP = 40
TOPK = 8
EXPERTS = 64
DS = 256
NEAR = Y * ZL
F32 = jnp.float32
NEAR_GROUPS = [
    [c * Y * ZH * ZL + y * ZH * ZL + (q * ZL + r + 2 * c) % (ZH * ZL) for y in range(Y) for r in range(ZL)]
    for c in range(CORES)
    for q in range(ZH)
]
BF16 = jnp.bfloat16


def in_vmem(array):
    return pltpu.with_memory_space_constraint(array, pltpu.VMEM)


def in_hbm(array):
    return pltpu.with_memory_space_constraint(array, pltpu.HBM)


def select_kernel(base_ref, block0, block1, block2, block3, out_hbm, picked, rows_out, sems):
    base = base_ref[0]
    blocks = (block0, block1, block2, block3)
    j = lax.broadcasted_iota(jnp.int32, (NEAR, TOK), 0)
    expert = ((j // ZL) * (ZH * ZL) + ((base + j % ZL) & (ZH * ZL - 1))).astype(F32)
    hits = []
    for b in range(ZH):
        ids = blocks[b][TOK : TOK + 16, :].astype(F32)
        hit = jnp.zeros((NEAR, TOK), F32)
        for k in range(TOPK):
            hit = hit + (ids[k : k + 1, :] == expert).astype(F32)
        hits.append(hit)
    hits = jnp.concatenate(hits, axis=0)
    earlier = lax.broadcasted_iota(jnp.int32, (TOK, TOK), 0) < lax.broadcasted_iota(
        jnp.int32, (TOK, TOK), 1
    )
    before = jnp.dot(hits.astype(BF16), earlier.astype(BF16), preferred_element_type=F32)
    key = jnp.where(hits > 0, before, -1.0)
    slot = lax.broadcasted_iota(jnp.int32, (CAP, TOK), 0).astype(F32)
    copies = []
    for y in range(Y):
        for b in range(ZH):
            first = b * NEAR + y * ZL
            pick = jnp.concatenate(
                [(key[e : e + 1, :] == slot).astype(F32) for e in range(first, first + ZL)], axis=0
            )
            picked[b] = jnp.dot(
                pick.astype(BF16), blocks[b][0:TOK, :], preferred_element_type=F32
            )
        for e in range(ZL):
            rows = [picked[b, e * CAP : (e + 1) * CAP, :] for b in range(ZH)]
            rows_out[y * ZL + e] = jnp.concatenate(rows, axis=0).astype(BF16)
        near = pl.ds(y * ZL, ZL)
        copies.append(pltpu.make_async_copy(rows_out.at[near], out_hbm.at[near], sems.at[y]))
        copies[-1].start()
    for copy in copies:
        copy.wait()


def select_rows(base, blocks):
    return pl.pallas_call(
        select_kernel,
        out_shape=pltpu.HBM((NEAR, ZH * CAP, DS), BF16),
        in_specs=[
            pl.BlockSpec(memory_space=pltpu.SMEM),
        ]
        + [pl.BlockSpec(memory_space=pltpu.VMEM)] * ZH,
        out_specs=pl.BlockSpec(memory_space=pltpu.HBM),
        scratch_shapes=[
            pltpu.VMEM((ZH, ZL * CAP, DS), F32),
            pltpu.VMEM((NEAR, ZH * CAP, DS), BF16),
            pltpu.SemaphoreType.DMA((Y,)),
        ],
        compiler_params=pltpu.CompilerParams(vmem_limit_bytes=16 << 20),
    )(base, *blocks)


def exchange_kernel(
    head_ref, ids_hbm, grad_hbm, hidden_hbm, weight_hbm, out_hbm, block_ref, ids_ref, hidden, weight, turned, sems
):
    slots = EXPERTS * CAP
    piece = slots // 4
    pieces = [pl.ds(i * piece, piece) for i in range(4)]
    loads = [
        pltpu.make_async_copy(hidden_hbm.at[pieces[i]], hidden.at[pieces[i]], sems.at[i])
        for i in range(4)
    ]
    columns = pl.ds(pl.multiple_of(head_ref[0] * DS, DS), DS)
    load_weight = pltpu.make_async_copy(weight_hbm, weight, sems.at[10])
    load_ids = pltpu.make_async_copy(ids_hbm, ids_ref, sems.at[9])
    load_grad = pltpu.make_async_copy(
        grad_hbm.at[:, columns], block_ref.at[pl.ds(0, TOK)], sems.at[8]
    )
    for copy in [load_weight] + loads + [load_ids, load_grad]:
        copy.start()
    others = [load_grad]
    load_ids.wait()
    ids = ids_ref[...].astype(F32)
    block_ref[TOK : TOK + 16, :] = jnp.concatenate([ids, jnp.zeros_like(ids)], axis=0).astype(BF16)
    load_weight.wait()
    for j in range(X):
        copy = pltpu.make_async_copy(
            weight.at[:, pl.ds(j * CORES * DS, CORES * DS)],
            out_hbm.at[j, :, pl.ds(slots, CORES * DS)],
            sems.at[4 + j],
        )
        copy.start()
        others.append(copy)
    for i in range(4):
        loads[i].wait()
        rows = slice(i * piece, (i + 1) * piece)
        turned[:, rows] = hidden[rows, :].astype(F32).T.astype(BF16)
        for j in range(X):
            copy = pltpu.make_async_copy(
                turned.at[:, pieces[i]], out_hbm.at[j, :, pieces[i]], sems.at[11 + i * X + j]
            )
            copy.start()
            others.append(copy)
    for copy in others:
        copy.wait()


def exchange_blocks(head, ids, grad, hidden, weight):
    width = weight.shape[0]
    far = pl.BlockSpec(memory_space=pltpu.HBM)
    return pl.pallas_call(
        exchange_kernel,
        out_shape=(
            pltpu.HBM((X, width, EXPERTS * CAP + CORES * DS), BF16),
            jax.ShapeDtypeStruct((TOK + 16, DS), BF16),
        ),
        in_specs=[
            pl.BlockSpec(memory_space=pltpu.SMEM),
            far,
            far,
            far,
            far,
        ],
        out_specs=(far, pl.BlockSpec(memory_space=pltpu.VMEM)),
        scratch_shapes=[
            pltpu.VMEM(ids.shape, jnp.int32),
            pltpu.VMEM(hidden.shape, BF16),
            pltpu.VMEM(weight.shape, BF16),
            pltpu.VMEM((width, EXPERTS * CAP), BF16),
            pltpu.SemaphoreType.DMA((11 + 4 * X,)),
        ],
        compiler_params=pltpu.CompilerParams(vmem_limit_bytes=16 << 20),
    )(head, in_hbm(ids), in_hbm(grad), in_hbm(hidden), in_hbm(weight))


def mix_kernel(
    core_ref, mine_ref, theirs_ref, ids_ref, logits_ref, out_hbm, key_ref, probs_ref, out_ref, rounded, sems
):
    plan(ids_ref[...], logits_ref[...], key_ref, probs_ref)
    slots = EXPERTS * CAP
    core, base = core_ref[0], core_ref[1]
    weight = jnp.where(
        core == 0, mine_ref[:, slots : slots + DS], mine_ref[:, slots + DS : slots + 2 * DS]
    )
    group = ZH * ZL * CAP
    contract = (((0,), (0,)), ((), ()))
    copies = []
    for y in range(Y):
        cols = slice(y * group, (y + 1) * group)
        mixed = lax.dot_general(
            mine_ref[:, cols], weight, contract, preferred_element_type=F32
        ) + lax.dot_general(
            theirs_ref[:, cols], theirs_ref[:, slots:], contract, preferred_element_type=F32
        )
        for zl in range(ZL):
            place = zl ^ (2 * core)
            node = ((base + place) & (ZH * ZL - 1)) >> 2
            for zh in range(ZH):
                src = (zh * ZL + zl) * CAP
                back = (node - zh) & (ZH - 1)
                dst = pl.multiple_of(y * group + (place * ZH + back) * CAP, 8)
                out_ref[pl.ds(dst, CAP), :] = mixed[src : src + CAP, :]
        rows = pl.ds(y * group, group)
        rounded[rows, :] = out_ref[rows, :].astype(BF16)
        copies.append(pltpu.make_async_copy(rounded.at[rows], out_hbm.at[rows], sems.at[y]))
        copies[-1].start()
    for copy in copies:
        copy.wait()


def plan(ids, logits, key_ref, probs_ref):
    raised = jnp.exp(logits)
    probs = raised / jnp.sum(raised, axis=0, keepdims=True)
    expert = lax.broadcasted_iota(jnp.int32, (EXPERTS, TOK), 0)
    hits = jnp.zeros((EXPERTS, TOK), F32)
    spread = jnp.zeros((EXPERTS, TOK), F32)
    for k in range(TOPK):
        mine = ids[k : k + 1, :] == expert
        hits = hits + mine.astype(F32)
        spread = spread + jnp.where(mine, probs[k : k + 1, :], 0.0)
    earlier = lax.broadcasted_iota(jnp.int32, (TOK, TOK), 0) < lax.broadcasted_iota(
        jnp.int32, (TOK, TOK), 1
    )
    before = jnp.dot(hits.astype(BF16), earlier.astype(BF16), preferred_element_type=F32)
    key_ref[...] = jnp.where(hits > 0, before, -1.0)
    probs_ref[...] = spread


def mix(core, mine, theirs, ids, logits):
    table = pltpu.VMEM((EXPERTS, TOK), F32)
    return pl.pallas_call(
        mix_kernel,
        out_shape=(pltpu.HBM((EXPERTS * CAP, DS), BF16), table, table),
        in_specs=[pl.BlockSpec(memory_space=pltpu.SMEM)]
        + [pl.BlockSpec(memory_space=pltpu.VMEM)] * 4,
        out_specs=(pl.BlockSpec(memory_space=pltpu.HBM),) + (pl.BlockSpec(memory_space=pltpu.VMEM),) * 2,
        scratch_shapes=[
            pltpu.VMEM((EXPERTS * CAP, DS), F32),
            pltpu.VMEM((EXPERTS * CAP, DS), BF16),
            pltpu.SemaphoreType.DMA((Y,)),
        ],
        compiler_params=pltpu.CompilerParams(vmem_limit_bytes=16 << 20),
    )(core, mine, theirs, ids, logits)


def value_kernel(core_ref, rows_hbm, mixed_hbm, out_ref, rows_ref, mixed_ref, sems):
    steps = 4
    per = NEAR // steps
    copies = []
    for i in range(steps):
        near, slots = pl.ds(i * per, per), pl.ds(i * per * ZH * CAP, per * ZH * CAP)
        copies.append(
            (
                pltpu.make_async_copy(rows_hbm.at[near], rows_ref.at[near], sems.at[0, i]),
                pltpu.make_async_copy(mixed_hbm.at[slots], mixed_ref.at[slots], sems.at[1, i]),
            )
        )
    for pair in copies:
        for copy in pair:
            copy.start()
    slot = lax.broadcasted_iota(jnp.int32, (CAP, 128), 0)
    lane = lax.broadcasted_iota(jnp.int32, (CAP, 128), 1)
    own_lane = (lane == slot, lane == slot + 64)
    for i in range(steps):
        for copy in copies[i]:
            copy.wait()
        for e in range(i * per, (i + 1) * per, 2):
            sums = []
            for odd in range(2):
                rows = rows_ref[e + odd].astype(F32) * mixed_ref[
                    (e + odd) * ZH * CAP : (e + odd + 1) * ZH * CAP, :
                ].astype(F32)
                sums.append(jnp.sum(rows[:, 0:128] + rows[:, 128:256], axis=1, keepdims=True))
            for b in range(ZH):
                slots = slice(b * CAP, (b + 1) * CAP)
                lanes = jnp.where(own_lane[0], sums[0][slots, :], 0.0) + jnp.where(
                    own_lane[1], sums[1][slots, :], 0.0
                )
                pair = (e % ZL // 2) ^ core_ref[0]
                node = ((core_ref[1] + e % ZL) & (ZH * ZL - 1)) >> 2
                place = (e // ZL * ZH + ((node - b) & (ZH - 1))) * 2 + pair
                out_ref[place] = jnp.sum(lanes, axis=0, keepdims=True)


def slot_sums(core, rows, mixed):
    return pl.pallas_call(
        value_kernel,
        out_shape=jax.ShapeDtypeStruct((EXPERTS // 2, 1, 128), F32),
        in_specs=[
            pl.BlockSpec(memory_space=pltpu.SMEM),
            pl.BlockSpec(memory_space=pltpu.HBM),
            pl.BlockSpec(memory_space=pltpu.HBM),
        ],
        out_specs=pl.BlockSpec(memory_space=pltpu.VMEM),
        scratch_shapes=[
            pltpu.VMEM(rows.shape, BF16),
            pltpu.VMEM(mixed.shape, BF16),
            pltpu.SemaphoreType.DMA((2, 4)),
        ],
        compiler_params=pltpu.CompilerParams(vmem_limit_bytes=16 << 20),
    )(core, in_hbm(rows), in_hbm(mixed))


def head_sum_kernel(parts_ref, out_ref):
    for y in range(Y):
        total = parts_ref[0, y]
        for i in range(1, X * CORES):
            total = total + parts_ref[i, y]
        turned = pltpu.roll(total, 64, 1)
        for z in range(0, ZH * ZL, 2):
            out_ref[z, :, y * 128 : (y + 1) * 128] = total[z // 2 : z // 2 + 1, :]
            out_ref[z + 1, :, y * 128 : (y + 1) * 128] = turned[z // 2 : z // 2 + 1, :]


def head_sums(parts):
    return pl.pallas_call(
        head_sum_kernel,
        out_shape=jax.ShapeDtypeStruct((ZH * ZL, 1, Y * 128), F32),
    )(in_vmem(parts))


def final_kernel(
    parts_ref, key_ref, probs_ref, ids_ref, router_hbm, grad_ref, weight_ref,
    router_ref, total, sem,
):
    load_router = pltpu.make_async_copy(router_hbm, router_ref, sem)
    load_router.start()
    for y in range(Y):
        total[y * ZH * ZL : (y + 1) * ZH * ZL, :] = parts_ref[:, 0, y * 128 : (y + 1) * 128]
    back = total[...]
    key = key_ref[...]
    probs = probs_ref[...]
    dense = jnp.zeros((EXPERTS, TOK), F32)
    for c in range(CAP):
        dense = jnp.where(key == float(c), back[:, c : c + 1], dense)
    mean = jnp.sum(probs * dense, axis=0, keepdims=True)
    logit = (probs * (dense - mean)).astype(BF16)
    load_router.wait()
    grad_ref[...] = lax.dot_general(
        logit, router_ref[...], (((0,), (0,)), ((), ())), preferred_element_type=F32
    ).astype(BF16)
    ids = ids_ref[...]
    expert = lax.broadcasted_iota(jnp.int32, (EXPERTS, TOK), 0)
    for k in range(TOPK):
        weight_ref[k : k + 1, :] = jnp.sum(
            jnp.where(ids[k : k + 1, :] == expert, dense, 0.0), axis=0, keepdims=True
        )


def finish(parts, key, probs, ids, router):
    far, near = pl.BlockSpec(memory_space=pltpu.HBM), pl.BlockSpec(memory_space=pltpu.VMEM)
    return pl.pallas_call(
        final_kernel,
        out_shape=(
            jax.ShapeDtypeStruct((TOK, DS), BF16),
            jax.ShapeDtypeStruct((TOPK, TOK), F32),
        ),
        in_specs=[near, near, near, near, far],
        out_specs=(near, near),
        scratch_shapes=[
            pltpu.VMEM(router.shape, BF16),
            pltpu.VMEM((EXPERTS, 128), F32),
            pltpu.SemaphoreType.DMA(()),
        ],
        compiler_params=pltpu.CompilerParams(vmem_limit_bytes=16 << 20),
    )(in_vmem(parts), in_vmem(key), in_vmem(probs), ids, in_hbm(router))


def body(out_grad, expert_ids, chosen_logits, down_weight, saved_hidden, router_weight):
    x, core = lax.axis_index("x"), lax.axis_index("core")
    head = x * CORES + core
    width = down_weight.shape[1]
    slots = EXPERTS * CAP
    ids, logits = expert_ids.T, chosen_logits.T
    along, block = exchange_blocks(
        head.reshape(1).astype(jnp.int32),
        ids,
        out_grad,
        saved_hidden[0].reshape(slots, width),
        down_weight[0],
    )
    along = lax.all_to_all(along, "x", split_axis=0, concat_axis=0, tiled=True)
    mine = along.reshape(X * width, slots + CORES * DS)
    weight_other = lax.dynamic_slice_in_dim(mine, slots + (1 - core) * DS, DS, axis=1)
    theirs = lax.ppermute(
        jnp.concatenate([mine[:, :slots], weight_other], axis=1), "core", [(0, 1), (1, 0)]
    )
    z = lax.axis_index("zh") * ZL + lax.axis_index("zl")
    base = ((z - 2 * core) & (ZH * ZL - ZL)) + 2 * core
    place = jnp.stack([core, base]).astype(jnp.int32)
    mixed, key, probs = mix(place, mine, theirs, ids, logits)
    blocks = [block] + [
        lax.ppermute(block, "zh", [(i, (i + k) % ZH) for i in range(ZH)]) for k in range(1, ZH)
    ]
    outgoing = select_rows(base.reshape(1).astype(jnp.int32), blocks)
    received = lax.all_to_all(
        outgoing,
        ("core", "y", "zh", "zl"),
        split_axis=0,
        concat_axis=0,
        tiled=True,
        axis_index_groups=NEAR_GROUPS,
    )
    part = slot_sums(place, received, mixed)
    rows = ZH * ZL // 2
    part = jnp.broadcast_to(part.reshape(1, Y, rows, 128), (X * CORES, Y, rows, 128))
    part = lax.all_to_all(
        part.reshape(X * CORES * Y, rows, 128),
        ("x", "core", "y"),
        split_axis=0,
        concat_axis=0,
        tiled=True,
    )
    part = head_sums(part.reshape(X * CORES, Y, rows, 128))
    part = lax.all_to_all(part, ("zh", "zl"), split_axis=0, concat_axis=0, tiled=True)
    grad, weight_grad = finish(part, key, probs, ids, router_weight.T)
    return grad, weight_grad.T


def solution(mesh):
    fine = Mesh(
        mesh.devices.reshape(X, CORES, Y, ZH, ZL), ("x", "core", "y", "zh", "zl")
    )
    return jax.shard_map(
        body,
        mesh=fine,
        in_specs=(
            P(EXPERT, None),
            P(EXPERT, None),
            P(EXPERT, None),
            P(EXPERT, HEAD, None),
            P(EXPERT, None, None, HEAD),
            P(HEAD, None),
        ),
        out_specs=(P(EXPERT, HEAD), P(EXPERT, None)),
        check_vma=False,
    )
```

```python
import jax
import jax.numpy as jnp
from jax import lax
from jax.experimental import pallas as pl
from jax.experimental.pallas import tpu as pltpu
from jax.sharding import Mesh, PartitionSpec as P

X, CORES, Y, ZH, ZL = 4, 2, 4, 4, 4
EXPERT = ("y", "zh", "zl")
HEAD = ("x", "core")
TOK = 256
CAP = 40
TOPK = 8
EXPERTS = 64
DS = 256
NEAR = Y * ZL
F32 = jnp.float32
NEAR_GROUPS = [
    [c * Y * ZH * ZL + y * ZH * ZL + (q * ZL + r + 2 * c) % (ZH * ZL) for r in range(ZL) for y in range(Y)]
    for c in range(CORES)
    for q in range(ZH)
]
BF16 = jnp.bfloat16


def in_vmem(array):
    return pltpu.with_memory_space_constraint(array, pltpu.VMEM)


def in_hbm(array):
    return pltpu.with_memory_space_constraint(array, pltpu.HBM)


def select_kernel(base_ref, blocks_ref, out_hbm, picked, rows_out, sems):
    base = base_ref[0]
    j = lax.broadcasted_iota(jnp.int32, (NEAR, TOK), 0)
    expert = ((j % Y) * (ZH * ZL) + ((base + j // Y) & (ZH * ZL - 1))).astype(F32)
    hits = []
    for b in range(ZH):
        ids = blocks_ref[b, TOK : TOK + 16, :].astype(F32)
        hit = jnp.zeros((NEAR, TOK), F32)
        for k in range(TOPK):
            hit = hit + (ids[k : k + 1, :] == expert).astype(F32)
        hits.append(hit)
    hits = jnp.concatenate(hits, axis=0)
    earlier = lax.broadcasted_iota(jnp.int32, (TOK, TOK), 0) < lax.broadcasted_iota(
        jnp.int32, (TOK, TOK), 1
    )
    before = jnp.dot(hits.astype(BF16), earlier.astype(BF16), preferred_element_type=F32)
    key = jnp.where(hits > 0, before, -1.0)
    slot = lax.broadcasted_iota(jnp.int32, (CAP, TOK), 0).astype(F32)
    copies = []
    for y in range(Y):
        for b in range(ZH):
            first = b * NEAR + y * ZL
            pick = jnp.concatenate(
                [(key[e : e + 1, :] == slot).astype(F32) for e in range(first, first + ZL)], axis=0
            )
            picked[b] = jnp.dot(
                pick.astype(BF16), blocks_ref[b, 0:TOK, :], preferred_element_type=F32
            )
        for e in range(ZL):
            rows = [picked[b, e * CAP : (e + 1) * CAP, :] for b in range(ZH)]
            rows_out[y * ZL + e] = jnp.concatenate(rows, axis=0).astype(BF16)
        near = pl.ds(y * ZL, ZL)
        copies.append(pltpu.make_async_copy(rows_out.at[near], out_hbm.at[near], sems.at[y]))
        copies[-1].start()
    for copy in copies:
        copy.wait()


def select_rows(base, blocks):
    return pl.pallas_call(
        select_kernel,
        out_shape=pltpu.HBM((NEAR, ZH * CAP, DS), BF16),
        in_specs=[
            pl.BlockSpec(memory_space=pltpu.SMEM),
            pl.BlockSpec(memory_space=pltpu.VMEM),
        ],
        out_specs=pl.BlockSpec(memory_space=pltpu.HBM),
        scratch_shapes=[
            pltpu.VMEM((ZH, ZL * CAP, DS), F32),
            pltpu.VMEM((NEAR, ZH * CAP, DS), BF16),
            pltpu.SemaphoreType.DMA((Y,)),
        ],
        compiler_params=pltpu.CompilerParams(vmem_limit_bytes=16 << 20),
    )(base, blocks)


def exchange_kernel(
    head_ref, ids_hbm, grad_hbm, hidden_hbm, weight_hbm, out_hbm, block_ref, ids_ref, hidden, weight, turned, sems
):
    slots = EXPERTS * CAP
    piece = slots // 4
    pieces = [pl.ds(i * piece, piece) for i in range(4)]
    loads = [
        pltpu.make_async_copy(hidden_hbm.at[pieces[i]], hidden.at[pieces[i]], sems.at[i])
        for i in range(4)
    ]
    columns = pl.ds(pl.multiple_of(head_ref[0] * DS, DS), DS)
    load_weight = pltpu.make_async_copy(weight_hbm, weight, sems.at[10])
    load_ids = pltpu.make_async_copy(ids_hbm, ids_ref, sems.at[9])
    load_grad = pltpu.make_async_copy(
        grad_hbm.at[:, columns], block_ref.at[pl.ds(0, TOK)], sems.at[8]
    )
    for copy in [load_weight] + loads + [load_ids, load_grad]:
        copy.start()
    others = [load_grad]
    load_ids.wait()
    ids = ids_ref[...].astype(F32)
    block_ref[TOK : TOK + 16, :] = jnp.concatenate([ids, jnp.zeros_like(ids)], axis=0).astype(BF16)
    load_weight.wait()
    for j in range(X):
        copy = pltpu.make_async_copy(
            weight.at[:, pl.ds(j * CORES * DS, CORES * DS)],
            out_hbm.at[j, :, pl.ds(slots, CORES * DS)],
            sems.at[4 + j],
        )
        copy.start()
        others.append(copy)
    for i in range(4):
        loads[i].wait()
        rows = slice(i * piece, (i + 1) * piece)
        turned[:, rows] = hidden[rows, :].astype(F32).T.astype(BF16)
        for j in range(X):
            copy = pltpu.make_async_copy(
                turned.at[:, pieces[i]], out_hbm.at[j, :, pieces[i]], sems.at[11 + i * X + j]
            )
            copy.start()
            others.append(copy)
    for copy in others:
        copy.wait()


def exchange_blocks(head, ids, grad, hidden, weight):
    width = weight.shape[0]
    far = pl.BlockSpec(memory_space=pltpu.HBM)
    return pl.pallas_call(
        exchange_kernel,
        out_shape=(
            pltpu.HBM((X, width, EXPERTS * CAP + CORES * DS), BF16),
            jax.ShapeDtypeStruct((TOK + 16, DS), BF16),
        ),
        in_specs=[
            pl.BlockSpec(memory_space=pltpu.SMEM),
            far,
            far,
            far,
            far,
        ],
        out_specs=(far, pl.BlockSpec(memory_space=pltpu.VMEM)),
        scratch_shapes=[
            pltpu.VMEM(ids.shape, jnp.int32),
            pltpu.VMEM(hidden.shape, BF16),
            pltpu.VMEM(weight.shape, BF16),
            pltpu.VMEM((width, EXPERTS * CAP), BF16),
            pltpu.SemaphoreType.DMA((11 + 4 * X,)),
        ],
        compiler_params=pltpu.CompilerParams(vmem_limit_bytes=16 << 20),
    )(head, in_hbm(ids), in_hbm(grad), in_hbm(hidden), in_hbm(weight))


def mix_kernel(
    core_ref, mine_ref, theirs_ref, ids_ref, logits_ref, out_hbm, key_ref, probs_ref, out_ref, rounded, sems
):
    plan(ids_ref[...], logits_ref[...], key_ref, probs_ref)
    slots = EXPERTS * CAP
    core = core_ref[0]
    weight = jnp.where(
        core == 0, mine_ref[:, slots : slots + DS], mine_ref[:, slots + DS : slots + 2 * DS]
    )
    group = ZH * ZL * CAP
    contract = (((0,), (0,)), ((), ()))
    copies = []
    for y in range(Y):
        cols = slice(y * group, (y + 1) * group)
        mixed = lax.dot_general(
            mine_ref[:, cols], weight, contract, preferred_element_type=F32
        ) + lax.dot_general(
            theirs_ref[:, cols], theirs_ref[:, slots:], contract, preferred_element_type=F32
        )
        for zl in range(ZL):
            place = zl ^ (2 * core)
            for zh in range(ZH):
                src = (zh * ZL + zl) * CAP
                dst = pl.multiple_of(((place * Y + y) * ZH + zh) * CAP, 8)
                out_ref[pl.ds(dst, CAP), :] = mixed[src : src + CAP, :]
    for y in range(Y):
        rows = pl.ds(y * group, group)
        rounded[rows, :] = out_ref[rows, :].astype(BF16)
        copies.append(pltpu.make_async_copy(rounded.at[rows], out_hbm.at[rows], sems.at[y]))
        copies[-1].start()
    for copy in copies:
        copy.wait()


def plan(ids, logits, key_ref, probs_ref):
    raised = jnp.exp(logits)
    probs = raised / jnp.sum(raised, axis=0, keepdims=True)
    expert = lax.broadcasted_iota(jnp.int32, (EXPERTS, TOK), 0)
    hits = jnp.zeros((EXPERTS, TOK), F32)
    spread = jnp.zeros((EXPERTS, TOK), F32)
    for k in range(TOPK):
        mine = ids[k : k + 1, :] == expert
        hits = hits + mine.astype(F32)
        spread = spread + jnp.where(mine, probs[k : k + 1, :], 0.0)
    earlier = lax.broadcasted_iota(jnp.int32, (TOK, TOK), 0) < lax.broadcasted_iota(
        jnp.int32, (TOK, TOK), 1
    )
    before = jnp.dot(hits.astype(BF16), earlier.astype(BF16), preferred_element_type=F32)
    key_ref[...] = jnp.where(hits > 0, before, -1.0)
    probs_ref[...] = spread


def mix(core, mine, theirs, ids, logits):
    table = pltpu.VMEM((EXPERTS, TOK), F32)
    return pl.pallas_call(
        mix_kernel,
        out_shape=(pltpu.HBM((EXPERTS * CAP, DS), BF16), table, table),
        in_specs=[pl.BlockSpec(memory_space=pltpu.SMEM)]
        + [pl.BlockSpec(memory_space=pltpu.VMEM)] * 4,
        out_specs=(pl.BlockSpec(memory_space=pltpu.HBM),) + (pl.BlockSpec(memory_space=pltpu.VMEM),) * 2,
        scratch_shapes=[
            pltpu.VMEM((EXPERTS * CAP, DS), F32),
            pltpu.VMEM((EXPERTS * CAP, DS), BF16),
            pltpu.SemaphoreType.DMA((Y,)),
        ],
        compiler_params=pltpu.CompilerParams(vmem_limit_bytes=16 << 20),
    )(core, mine, theirs, ids, logits)


def value_kernel(core_ref, rows_hbm, mixed_hbm, out_ref, rows_ref, mixed_ref, sems):
    steps = ZL
    per = NEAR // steps
    copies = []
    for i in range(steps):
        near, slots = pl.ds(i * per, per), pl.ds(i * per * ZH * CAP, per * ZH * CAP)
        copies.append(
            (
                pltpu.make_async_copy(rows_hbm.at[near], rows_ref.at[near], sems.at[0, i]),
                pltpu.make_async_copy(mixed_hbm.at[slots], mixed_ref.at[slots], sems.at[1, i]),
            )
        )
    for pair in copies:
        for copy in pair:
            copy.start()
    slot = lax.broadcasted_iota(jnp.int32, (CAP, 128), 0)
    lane = lax.broadcasted_iota(jnp.int32, (CAP, 128), 1)
    own_lane = (lane == slot, lane == slot + 64)
    for pair in range(ZL // 2):
        for copy in copies[2 * pair] + copies[2 * pair + 1]:
            copy.wait()
        for y in range(Y):
            sums = []
            for r in (2 * pair, 2 * pair + 1):
                e = r * Y + y
                rows = rows_ref[e].astype(F32) * mixed_ref[
                    e * ZH * CAP : (e + 1) * ZH * CAP, :
                ].astype(F32)
                sums.append(jnp.sum(rows[:, 0:128] + rows[:, 128:256], axis=1, keepdims=True))
            for b in range(ZH):
                slots = slice(b * CAP, (b + 1) * CAP)
                lanes = jnp.where(own_lane[0], sums[0][slots, :], 0.0) + jnp.where(
                    own_lane[1], sums[1][slots, :], 0.0
                )
                place = (y * ZH + b) * 2 + (pair ^ core_ref[0])
                out_ref[place] = jnp.sum(lanes, axis=0, keepdims=True)


def slot_sums(core, rows, mixed):
    return pl.pallas_call(
        value_kernel,
        out_shape=jax.ShapeDtypeStruct((EXPERTS // 2, 1, 128), F32),
        in_specs=[
            pl.BlockSpec(memory_space=pltpu.SMEM),
            pl.BlockSpec(memory_space=pltpu.HBM),
            pl.BlockSpec(memory_space=pltpu.HBM),
        ],
        out_specs=pl.BlockSpec(memory_space=pltpu.VMEM),
        scratch_shapes=[
            pltpu.VMEM(rows.shape, BF16),
            pltpu.VMEM(mixed.shape, BF16),
            pltpu.SemaphoreType.DMA((2, 4)),
        ],
        compiler_params=pltpu.CompilerParams(vmem_limit_bytes=16 << 20),
    )(core, in_hbm(rows), in_hbm(mixed))


def head_sum_kernel(parts_ref, out_ref):
    for y in range(Y):
        total = parts_ref[0, y]
        for i in range(1, X * CORES):
            total = total + parts_ref[i, y]
        turned = pltpu.roll(total, 64, 1)
        for z in range(0, ZH * ZL, 2):
            out_ref[z, :, y * 128 : (y + 1) * 128] = total[z // 2 : z // 2 + 1, :]
            out_ref[z + 1, :, y * 128 : (y + 1) * 128] = turned[z // 2 : z // 2 + 1, :]


def head_sums(parts):
    return pl.pallas_call(
        head_sum_kernel,
        out_shape=jax.ShapeDtypeStruct((ZH * ZL, 1, Y * 128), F32),
    )(in_vmem(parts))


def final_kernel(
    parts_ref, key_ref, probs_ref, ids_ref, router_hbm, grad_ref, weight_ref,
    router_ref, total, sem,
):
    load_router = pltpu.make_async_copy(router_hbm, router_ref, sem)
    load_router.start()
    for y in range(Y):
        total[y * ZH * ZL : (y + 1) * ZH * ZL, :] = parts_ref[:, 0, y * 128 : (y + 1) * 128]
    back = total[...]
    key = key_ref[...]
    probs = probs_ref[...]
    dense = jnp.zeros((EXPERTS, TOK), F32)
    for c in range(CAP):
        dense = jnp.where(key == float(c), back[:, c : c + 1], dense)
    mean = jnp.sum(probs * dense, axis=0, keepdims=True)
    logit = (probs * (dense - mean)).astype(BF16)
    load_router.wait()
    grad_ref[...] = lax.dot_general(
        logit, router_ref[...], (((0,), (0,)), ((), ())), preferred_element_type=F32
    ).astype(BF16)
    ids = ids_ref[...]
    expert = lax.broadcasted_iota(jnp.int32, (EXPERTS, TOK), 0)
    for k in range(TOPK):
        weight_ref[k : k + 1, :] = jnp.sum(
            jnp.where(ids[k : k + 1, :] == expert, dense, 0.0), axis=0, keepdims=True
        )


def finish(parts, key, probs, ids, router):
    far, near = pl.BlockSpec(memory_space=pltpu.HBM), pl.BlockSpec(memory_space=pltpu.VMEM)
    return pl.pallas_call(
        final_kernel,
        out_shape=(
            jax.ShapeDtypeStruct((TOK, DS), BF16),
            jax.ShapeDtypeStruct((TOPK, TOK), F32),
        ),
        in_specs=[near, near, near, near, far],
        out_specs=(near, near),
        scratch_shapes=[
            pltpu.VMEM(router.shape, BF16),
            pltpu.VMEM((EXPERTS, 128), F32),
            pltpu.SemaphoreType.DMA(()),
        ],
        compiler_params=pltpu.CompilerParams(vmem_limit_bytes=16 << 20),
    )(in_vmem(parts), in_vmem(key), in_vmem(probs), ids, in_hbm(router))


def body(out_grad, expert_ids, chosen_logits, down_weight, saved_hidden, router_weight):
    x, core = lax.axis_index("x"), lax.axis_index("core")
    head = x * CORES + core
    width = down_weight.shape[1]
    slots = EXPERTS * CAP
    ids, logits = expert_ids.T, chosen_logits.T
    along, block = exchange_blocks(
        head.reshape(1).astype(jnp.int32),
        ids,
        out_grad,
        saved_hidden[0].reshape(slots, width),
        down_weight[0],
    )
    along = lax.all_to_all(along, "x", split_axis=0, concat_axis=0, tiled=True)
    mine = along.reshape(X * width, slots + CORES * DS)
    weight_other = lax.dynamic_slice_in_dim(mine, slots + (1 - core) * DS, DS, axis=1)
    theirs = lax.ppermute(
        jnp.concatenate([mine[:, :slots], weight_other], axis=1), "core", [(0, 1), (1, 0)]
    )
    core_scalar = core.reshape(1).astype(jnp.int32)
    mixed, key, probs = mix(core_scalar, mine, theirs, ids, logits)
    blocks = lax.all_gather(block, "zh", axis=0, tiled=False)
    z = lax.axis_index("zh") * ZL + lax.axis_index("zl")
    base = ((z - 2 * core) & (ZH * ZL - ZL)) + 2 * core
    outgoing = select_rows(base.reshape(1).astype(jnp.int32), blocks)
    received = lax.all_to_all(
        outgoing,
        ("core", "y", "zh", "zl"),
        split_axis=0,
        concat_axis=0,
        tiled=True,
        axis_index_groups=NEAR_GROUPS,
    )
    part = slot_sums(core_scalar, received, mixed)
    rows = ZH * ZL // 2
    part = jnp.broadcast_to(part.reshape(1, Y, rows, 128), (X * CORES, Y, rows, 128))
    part = lax.all_to_all(
        part.reshape(X * CORES * Y, rows, 128),
        ("x", "core", "y"),
        split_axis=0,
        concat_axis=0,
        tiled=True,
    )
    part = head_sums(part.reshape(X * CORES, Y, rows, 128))
    part = lax.all_to_all(part, ("zh", "zl"), split_axis=0, concat_axis=0, tiled=True)
    grad, weight_grad = finish(part, key, probs, ids, router_weight.T)
    return grad, weight_grad.T


def solution(mesh):
    fine = Mesh(
        mesh.devices.reshape(X, CORES, Y, ZH, ZL), ("x", "core", "y", "zh", "zl")
    )
    return jax.shard_map(
        body,
        mesh=fine,
        in_specs=(
            P(EXPERT, None),
            P(EXPERT, None),
            P(EXPERT, None),
            P(EXPERT, HEAD, None),
            P(EXPERT, None, None, HEAD),
            P(HEAD, None),
        ),
        out_specs=(P(EXPERT, HEAD), P(EXPERT, None)),
        check_vma=False,
    )
```

```python
import jax
import jax.numpy as jnp
from jax import lax
from jax.experimental import pallas as pl
from jax.experimental.pallas import tpu as pltpu
from jax.sharding import Mesh, PartitionSpec as P

X, CORES, Y, ZH, ZL = 4, 2, 4, 4, 4
EXPERT = ("y", "zh", "zl")
HEAD = ("x", "core")
TOK = 256
CAP = 40
TOPK = 8
EXPERTS = 64
DS = 256
NEAR = Y * ZL
F32 = jnp.float32
NEAR_GROUPS = [
    [c * Y * ZH * ZL + y * ZH * ZL + (q * ZL + r + 2 * c) % (ZH * ZL) for y in range(Y) for r in range(ZL)]
    for c in range(CORES)
    for q in range(ZH)
]
BF16 = jnp.bfloat16


def in_vmem(array):
    return pltpu.with_memory_space_constraint(array, pltpu.VMEM)


def in_hbm(array):
    return pltpu.with_memory_space_constraint(array, pltpu.HBM)


def select_kernel(base_ref, blocks_ref, out_hbm, picked, rows_out, sems):
    base = base_ref[0]
    j = lax.broadcasted_iota(jnp.int32, (NEAR, TOK), 0)
    expert = ((j // ZL) * (ZH * ZL) + ((base + j % ZL) & (ZH * ZL - 1))).astype(F32)
    hits = []
    for b in range(ZH):
        ids = blocks_ref[b, TOK : TOK + 16, :].astype(F32)
        hit = jnp.zeros((NEAR, TOK), F32)
        for k in range(TOPK):
            hit = hit + (ids[k : k + 1, :] == expert).astype(F32)
        hits.append(hit)
    hits = jnp.concatenate(hits, axis=0)
    earlier = lax.broadcasted_iota(jnp.int32, (TOK, TOK), 0) < lax.broadcasted_iota(
        jnp.int32, (TOK, TOK), 1
    )
    before = jnp.dot(hits.astype(BF16), earlier.astype(BF16), preferred_element_type=F32)
    key = jnp.where(hits > 0, before, -1.0)
    slot = lax.broadcasted_iota(jnp.int32, (CAP, TOK), 0).astype(F32)
    copies = []
    for y in range(Y):
        for b in range(ZH):
            first = b * NEAR + y * ZL
            pick = jnp.concatenate(
                [(key[e : e + 1, :] == slot).astype(F32) for e in range(first, first + ZL)], axis=0
            )
            picked[b] = jnp.dot(
                pick.astype(BF16), blocks_ref[b, 0:TOK, :], preferred_element_type=F32
            )
        for e in range(ZL):
            rows = [picked[b, e * CAP : (e + 1) * CAP, :] for b in range(ZH)]
            rows_out[y * ZL + e] = jnp.concatenate(rows, axis=0).astype(BF16)
        near = pl.ds(y * ZL, ZL)
        copies.append(pltpu.make_async_copy(rows_out.at[near], out_hbm.at[near], sems.at[y]))
        copies[-1].start()
    for copy in copies:
        copy.wait()


def select_rows(base, blocks):
    return pl.pallas_call(
        select_kernel,
        out_shape=pltpu.HBM((NEAR, ZH * CAP, DS), BF16),
        in_specs=[
            pl.BlockSpec(memory_space=pltpu.SMEM),
            pl.BlockSpec(memory_space=pltpu.VMEM),
        ],
        out_specs=pl.BlockSpec(memory_space=pltpu.HBM),
        scratch_shapes=[
            pltpu.VMEM((ZH, ZL * CAP, DS), F32),
            pltpu.VMEM((NEAR, ZH * CAP, DS), BF16),
            pltpu.SemaphoreType.DMA((Y,)),
        ],
        compiler_params=pltpu.CompilerParams(vmem_limit_bytes=16 << 20),
    )(base, blocks)


def exchange_kernel(
    head_ref, ids_hbm, grad_hbm, hidden_hbm, weight_hbm, out_hbm, block_ref, ids_ref, hidden, weight, turned, sems
):
    slots = EXPERTS * CAP
    piece = slots // 4
    pieces = [pl.ds(i * piece, piece) for i in range(4)]
    loads = [
        pltpu.make_async_copy(hidden_hbm.at[pieces[i]], hidden.at[pieces[i]], sems.at[i])
        for i in range(4)
    ]
    columns = pl.ds(pl.multiple_of(head_ref[0] * DS, DS), DS)
    load_weight = pltpu.make_async_copy(weight_hbm, weight, sems.at[10])
    load_ids = pltpu.make_async_copy(ids_hbm, ids_ref, sems.at[9])
    load_grad = pltpu.make_async_copy(
        grad_hbm.at[:, columns], block_ref.at[pl.ds(0, TOK)], sems.at[8]
    )
    for copy in [load_weight] + loads + [load_ids, load_grad]:
        copy.start()
    others = [load_grad]
    load_ids.wait()
    ids = ids_ref[...].astype(F32)
    block_ref[TOK : TOK + 16, :] = jnp.concatenate([ids, jnp.zeros_like(ids)], axis=0).astype(BF16)
    load_weight.wait()
    for j in range(X):
        copy = pltpu.make_async_copy(
            weight.at[:, pl.ds(j * CORES * DS, CORES * DS)],
            out_hbm.at[j, :, pl.ds(slots, CORES * DS)],
            sems.at[4 + j],
        )
        copy.start()
        others.append(copy)
    for i in range(4):
        loads[i].wait()
        rows = slice(i * piece, (i + 1) * piece)
        turned[:, rows] = hidden[rows, :].astype(F32).T.astype(BF16)
        for j in range(X):
            copy = pltpu.make_async_copy(
                turned.at[:, pieces[i]], out_hbm.at[j, :, pieces[i]], sems.at[11 + i * X + j]
            )
            copy.start()
            others.append(copy)
    for copy in others:
        copy.wait()


def exchange_blocks(head, ids, grad, hidden, weight):
    width = weight.shape[0]
    far = pl.BlockSpec(memory_space=pltpu.HBM)
    return pl.pallas_call(
        exchange_kernel,
        out_shape=(
            pltpu.HBM((X, width, EXPERTS * CAP + CORES * DS), BF16),
            jax.ShapeDtypeStruct((TOK + 16, DS), BF16),
        ),
        in_specs=[
            pl.BlockSpec(memory_space=pltpu.SMEM),
            far,
            far,
            far,
            far,
        ],
        out_specs=(far, pl.BlockSpec(memory_space=pltpu.VMEM)),
        scratch_shapes=[
            pltpu.VMEM(ids.shape, jnp.int32),
            pltpu.VMEM(hidden.shape, BF16),
            pltpu.VMEM(weight.shape, BF16),
            pltpu.VMEM((width, EXPERTS * CAP), BF16),
            pltpu.SemaphoreType.DMA((11 + 4 * X,)),
        ],
        compiler_params=pltpu.CompilerParams(vmem_limit_bytes=16 << 20),
    )(head, in_hbm(ids), in_hbm(grad), in_hbm(hidden), in_hbm(weight))


def mix_kernel(
    core_ref, mine_ref, theirs_ref, ids_ref, logits_ref, out_hbm, key_ref, probs_ref, out_ref, rounded, sems
):
    plan(ids_ref[...], logits_ref[...], key_ref, probs_ref)
    slots = EXPERTS * CAP
    core = core_ref[0]
    weight = jnp.where(
        core == 0, mine_ref[:, slots : slots + DS], mine_ref[:, slots + DS : slots + 2 * DS]
    )
    group = ZH * ZL * CAP
    contract = (((0,), (0,)), ((), ()))
    copies = []
    for y in range(Y):
        cols = slice(y * group, (y + 1) * group)
        mixed = lax.dot_general(
            mine_ref[:, cols], weight, contract, preferred_element_type=F32
        ) + lax.dot_general(
            theirs_ref[:, cols], theirs_ref[:, slots:], contract, preferred_element_type=F32
        )
        for zl in range(ZL):
            place = zl ^ (2 * core)
            for zh in range(ZH):
                src = (zh * ZL + zl) * CAP
                dst = pl.multiple_of(y * group + (place * ZH + zh) * CAP, 8)
                out_ref[pl.ds(dst, CAP), :] = mixed[src : src + CAP, :]
        rows = pl.ds(y * group, group)
        rounded[rows, :] = out_ref[rows, :].astype(BF16)
        copies.append(pltpu.make_async_copy(rounded.at[rows], out_hbm.at[rows], sems.at[y]))
        copies[-1].start()
    for copy in copies:
        copy.wait()


def plan(ids, logits, key_ref, probs_ref):
    raised = jnp.exp(logits)
    probs = raised / jnp.sum(raised, axis=0, keepdims=True)
    expert = lax.broadcasted_iota(jnp.int32, (EXPERTS, TOK), 0)
    hits = jnp.zeros((EXPERTS, TOK), F32)
    spread = jnp.zeros((EXPERTS, TOK), F32)
    for k in range(TOPK):
        mine = ids[k : k + 1, :] == expert
        hits = hits + mine.astype(F32)
        spread = spread + jnp.where(mine, probs[k : k + 1, :], 0.0)
    earlier = lax.broadcasted_iota(jnp.int32, (TOK, TOK), 0) < lax.broadcasted_iota(
        jnp.int32, (TOK, TOK), 1
    )
    before = jnp.dot(hits.astype(BF16), earlier.astype(BF16), preferred_element_type=F32)
    key_ref[...] = jnp.where(hits > 0, before, -1.0)
    probs_ref[...] = spread


def mix(core, mine, theirs, ids, logits):
    table = pltpu.VMEM((EXPERTS, TOK), F32)
    return pl.pallas_call(
        mix_kernel,
        out_shape=(pltpu.HBM((EXPERTS * CAP, DS), BF16), table, table),
        in_specs=[pl.BlockSpec(memory_space=pltpu.SMEM)]
        + [pl.BlockSpec(memory_space=pltpu.VMEM)] * 4,
        out_specs=(pl.BlockSpec(memory_space=pltpu.HBM),) + (pl.BlockSpec(memory_space=pltpu.VMEM),) * 2,
        scratch_shapes=[
            pltpu.VMEM((EXPERTS * CAP, DS), F32),
            pltpu.VMEM((EXPERTS * CAP, DS), BF16),
            pltpu.SemaphoreType.DMA((Y,)),
        ],
        compiler_params=pltpu.CompilerParams(vmem_limit_bytes=16 << 20),
    )(core, mine, theirs, ids, logits)


def value_kernel(core_ref, rows_hbm, mixed_hbm, out_ref, rows_ref, mixed_ref, sems):
    steps = 4
    per = NEAR // steps
    copies = []
    for i in range(steps):
        near, slots = pl.ds(i * per, per), pl.ds(i * per * ZH * CAP, per * ZH * CAP)
        copies.append(
            (
                pltpu.make_async_copy(rows_hbm.at[near], rows_ref.at[near], sems.at[0, i]),
                pltpu.make_async_copy(mixed_hbm.at[slots], mixed_ref.at[slots], sems.at[1, i]),
            )
        )
    for pair in copies:
        for copy in pair:
            copy.start()
    slot = lax.broadcasted_iota(jnp.int32, (CAP, 128), 0)
    lane = lax.broadcasted_iota(jnp.int32, (CAP, 128), 1)
    own_lane = (lane == slot, lane == slot + 64)
    for i in range(steps):
        for copy in copies[i]:
            copy.wait()
        for e in range(i * per, (i + 1) * per, 2):
            sums = []
            for odd in range(2):
                rows = rows_ref[e + odd].astype(F32) * mixed_ref[
                    (e + odd) * ZH * CAP : (e + odd + 1) * ZH * CAP, :
                ].astype(F32)
                sums.append(jnp.sum(rows[:, 0:128] + rows[:, 128:256], axis=1, keepdims=True))
            for b in range(ZH):
                slots = slice(b * CAP, (b + 1) * CAP)
                lanes = jnp.where(own_lane[0], sums[0][slots, :], 0.0) + jnp.where(
                    own_lane[1], sums[1][slots, :], 0.0
                )
                place = (e // ZL * ZH + b) * 2 + ((e % ZL // 2) ^ core_ref[0])
                out_ref[place] = jnp.sum(lanes, axis=0, keepdims=True)


def slot_sums(core, rows, mixed):
    return pl.pallas_call(
        value_kernel,
        out_shape=jax.ShapeDtypeStruct((EXPERTS // 2, 1, 128), F32),
        in_specs=[
            pl.BlockSpec(memory_space=pltpu.SMEM),
            pl.BlockSpec(memory_space=pltpu.HBM),
            pl.BlockSpec(memory_space=pltpu.HBM),
        ],
        out_specs=pl.BlockSpec(memory_space=pltpu.VMEM),
        scratch_shapes=[
            pltpu.VMEM(rows.shape, BF16),
            pltpu.VMEM(mixed.shape, BF16),
            pltpu.SemaphoreType.DMA((2, 4)),
        ],
        compiler_params=pltpu.CompilerParams(vmem_limit_bytes=16 << 20),
    )(core, in_hbm(rows), in_hbm(mixed))


def head_sum_kernel(parts_ref, out_ref):
    for y in range(Y):
        total = parts_ref[0, y]
        for i in range(1, X):
            total = total + parts_ref[i, y]
        turned = pltpu.roll(total, 64, 1)
        for z in range(0, ZH * ZL, 2):
            out_ref[z, :, y * 128 : (y + 1) * 128] = total[z // 2 : z // 2 + 1, :]
            out_ref[z + 1, :, y * 128 : (y + 1) * 128] = turned[z // 2 : z // 2 + 1, :]


def head_sums(parts):
    return pl.pallas_call(
        head_sum_kernel,
        out_shape=jax.ShapeDtypeStruct((ZH * ZL, 1, Y * 128), F32),
    )(in_vmem(parts))


def final_kernel(
    parts_ref, key_ref, probs_ref, ids_ref, router_hbm, grad_ref, weight_ref,
    router_ref, total, sem,
):
    load_router = pltpu.make_async_copy(router_hbm, router_ref, sem)
    load_router.start()
    for y in range(Y):
        total[y * ZH * ZL : (y + 1) * ZH * ZL, :] = parts_ref[:, 0, y * 128 : (y + 1) * 128]
    back = total[...]
    key = key_ref[...]
    probs = probs_ref[...]
    dense = jnp.zeros((EXPERTS, TOK), F32)
    for c in range(CAP):
        dense = jnp.where(key == float(c), back[:, c : c + 1], dense)
    mean = jnp.sum(probs * dense, axis=0, keepdims=True)
    logit = (probs * (dense - mean)).astype(BF16)
    load_router.wait()
    grad_ref[...] = lax.dot_general(
        logit, router_ref[...], (((0,), (0,)), ((), ())), preferred_element_type=F32
    ).astype(BF16)
    ids = ids_ref[...]
    expert = lax.broadcasted_iota(jnp.int32, (EXPERTS, TOK), 0)
    for k in range(TOPK):
        weight_ref[k : k + 1, :] = jnp.sum(
            jnp.where(ids[k : k + 1, :] == expert, dense, 0.0), axis=0, keepdims=True
        )


def finish(parts, key, probs, ids, router):
    far, near = pl.BlockSpec(memory_space=pltpu.HBM), pl.BlockSpec(memory_space=pltpu.VMEM)
    return pl.pallas_call(
        final_kernel,
        out_shape=(
            jax.ShapeDtypeStruct((TOK, DS), BF16),
            jax.ShapeDtypeStruct((TOPK, TOK), F32),
        ),
        in_specs=[near, near, near, near, far],
        out_specs=(near, near),
        scratch_shapes=[
            pltpu.VMEM(router.shape, BF16),
            pltpu.VMEM((EXPERTS, 128), F32),
            pltpu.SemaphoreType.DMA(()),
        ],
        compiler_params=pltpu.CompilerParams(vmem_limit_bytes=16 << 20),
    )(in_vmem(parts), in_vmem(key), in_vmem(probs), ids, in_hbm(router))


def body(out_grad, expert_ids, chosen_logits, down_weight, saved_hidden, router_weight):
    x, core = lax.axis_index("x"), lax.axis_index("core")
    head = x * CORES + core
    width = down_weight.shape[1]
    slots = EXPERTS * CAP
    ids, logits = expert_ids.T, chosen_logits.T
    along, block = exchange_blocks(
        head.reshape(1).astype(jnp.int32),
        ids,
        out_grad,
        saved_hidden[0].reshape(slots, width),
        down_weight[0],
    )
    along = lax.all_to_all(along, "x", split_axis=0, concat_axis=0, tiled=True)
    mine = along.reshape(X * width, slots + CORES * DS)
    weight_other = lax.dynamic_slice_in_dim(mine, slots + (1 - core) * DS, DS, axis=1)
    theirs = lax.ppermute(
        jnp.concatenate([mine[:, :slots], weight_other], axis=1), "core", [(0, 1), (1, 0)]
    )
    core_scalar = core.reshape(1).astype(jnp.int32)
    mixed, key, probs = mix(core_scalar, mine, theirs, ids, logits)
    blocks = lax.all_gather(block, "zh", axis=0, tiled=False)
    z = lax.axis_index("zh") * ZL + lax.axis_index("zl")
    base = ((z - 2 * core) & (ZH * ZL - ZL)) + 2 * core
    outgoing = select_rows(base.reshape(1).astype(jnp.int32), blocks)
    received = lax.all_to_all(
        outgoing,
        ("core", "y", "zh", "zl"),
        split_axis=0,
        concat_axis=0,
        tiled=True,
        axis_index_groups=NEAR_GROUPS,
    )
    part = slot_sums(core_scalar, received, mixed)
    rows = ZH * ZL // 2
    part = jnp.sum(lax.all_gather(part, "core", axis=0, tiled=False), axis=0)
    part = jnp.broadcast_to(part.reshape(1, Y, rows, 128), (X, Y, rows, 128))
    part = lax.all_to_all(
        part.reshape(X * Y, rows, 128), ("x", "y"), split_axis=0, concat_axis=0, tiled=True
    )
    part = head_sums(part.reshape(X, Y, rows, 128))
    part = lax.all_to_all(part, ("zh", "zl"), split_axis=0, concat_axis=0, tiled=True)
    grad, weight_grad = finish(part, key, probs, ids, router_weight.T)
    return grad, weight_grad.T


def solution(mesh):
    fine = Mesh(
        mesh.devices.reshape(X, CORES, Y, ZH, ZL), ("x", "core", "y", "zh", "zl")
    )
    return jax.shard_map(
        body,
        mesh=fine,
        in_specs=(
            P(EXPERT, None),
            P(EXPERT, None),
            P(EXPERT, None),
            P(EXPERT, HEAD, None),
            P(EXPERT, None, None, HEAD),
            P(HEAD, None),
        ),
        out_specs=(P(EXPERT, HEAD), P(EXPERT, None)),
        check_vma=False,
    )
```

```python
import jax
import jax.numpy as jnp
from jax import lax
from jax.experimental import pallas as pl
from jax.experimental.pallas import tpu as pltpu
from jax.sharding import Mesh, PartitionSpec as P

X, CORES, Y, ZH, ZL = 4, 2, 4, 4, 4
EXPERT = ("y", "zh", "zl")
HEAD = ("x", "core")
TOK = 256
CAP = 40
TOPK = 8
EXPERTS = 64
DS = 256
NEAR = Y * ZL
F32 = jnp.float32
NEAR_GROUPS = [
    [c * Y * ZH * ZL + y * ZH * ZL + (q * ZL + r + 2 * c) % (ZH * ZL) for y in range(Y) for r in range(ZL)]
    for c in range(CORES)
    for q in range(ZH)
]
BF16 = jnp.bfloat16


def in_vmem(array):
    return pltpu.with_memory_space_constraint(array, pltpu.VMEM)


def in_hbm(array):
    return pltpu.with_memory_space_constraint(array, pltpu.HBM)


def select_kernel(base_ref, blocks_ref, out_hbm, picked, rows_out, sems):
    base = base_ref[0]
    j = lax.broadcasted_iota(jnp.int32, (NEAR, TOK), 0)
    expert = ((j // ZL) * (ZH * ZL) + ((base + j % ZL) & (ZH * ZL - 1))).astype(F32)
    hits = []
    for b in range(ZH):
        ids = blocks_ref[b, TOK : TOK + 16, :].astype(F32)
        hit = jnp.zeros((NEAR, TOK), F32)
        for k in range(TOPK):
            hit = hit + (ids[k : k + 1, :] == expert).astype(F32)
        hits.append(hit)
    hits = jnp.concatenate(hits, axis=0)
    earlier = lax.broadcasted_iota(jnp.int32, (TOK, TOK), 0) < lax.broadcasted_iota(
        jnp.int32, (TOK, TOK), 1
    )
    before = jnp.dot(hits.astype(BF16), earlier.astype(BF16), preferred_element_type=F32)
    key = jnp.where(hits > 0, before, -1.0)
    slot = lax.broadcasted_iota(jnp.int32, (CAP, TOK), 0).astype(F32)
    copies = []
    for y in range(Y):
        for b in range(ZH):
            first = b * NEAR + y * ZL
            pick = jnp.concatenate(
                [(key[e : e + 1, :] == slot).astype(F32) for e in range(first, first + ZL)], axis=0
            )
            picked[b] = jnp.dot(
                pick.astype(BF16), blocks_ref[b, 0:TOK, :], preferred_element_type=F32
            )
        for e in range(ZL):
            rows = [picked[b, e * CAP : (e + 1) * CAP, :] for b in range(ZH)]
            rows_out[y * ZL + e] = jnp.concatenate(rows, axis=0).astype(BF16)
        near = pl.ds(y * ZL, ZL)
        copies.append(pltpu.make_async_copy(rows_out.at[near], out_hbm.at[near], sems.at[y]))
        copies[-1].start()
    for copy in copies:
        copy.wait()


def select_rows(base, blocks):
    return pl.pallas_call(
        select_kernel,
        out_shape=pltpu.HBM((NEAR, ZH * CAP, DS), BF16),
        in_specs=[
            pl.BlockSpec(memory_space=pltpu.SMEM),
            pl.BlockSpec(memory_space=pltpu.VMEM),
        ],
        out_specs=pl.BlockSpec(memory_space=pltpu.HBM),
        scratch_shapes=[
            pltpu.VMEM((ZH, ZL * CAP, DS), F32),
            pltpu.VMEM((NEAR, ZH * CAP, DS), BF16),
            pltpu.SemaphoreType.DMA((Y,)),
        ],
        compiler_params=pltpu.CompilerParams(vmem_limit_bytes=16 << 20),
    )(base, blocks)


def exchange_kernel(
    head_ref, ids_hbm, grad_hbm, hidden_hbm, weight_hbm, out_hbm, block_ref, ids_ref, hidden, weight, turned, sems
):
    slots = EXPERTS * CAP
    piece = slots // 4
    pieces = [pl.ds(i * piece, piece) for i in range(4)]
    loads = [
        pltpu.make_async_copy(hidden_hbm.at[pieces[i]], hidden.at[pieces[i]], sems.at[i])
        for i in range(4)
    ]
    columns = pl.ds(pl.multiple_of(head_ref[0] * DS, DS), DS)
    load_weight = pltpu.make_async_copy(weight_hbm, weight, sems.at[10])
    load_ids = pltpu.make_async_copy(ids_hbm, ids_ref, sems.at[9])
    load_grad = pltpu.make_async_copy(
        grad_hbm.at[:, columns], block_ref.at[pl.ds(0, TOK)], sems.at[8]
    )
    for copy in [load_weight] + loads + [load_ids, load_grad]:
        copy.start()
    others = [load_grad]
    load_ids.wait()
    ids = ids_ref[...].astype(F32)
    block_ref[TOK : TOK + 16, :] = jnp.concatenate([ids, jnp.zeros_like(ids)], axis=0).astype(BF16)
    load_weight.wait()
    for j in range(X):
        copy = pltpu.make_async_copy(
            weight.at[:, pl.ds(j * CORES * DS, CORES * DS)],
            out_hbm.at[j, :, pl.ds(slots, CORES * DS)],
            sems.at[4 + j],
        )
        copy.start()
        others.append(copy)
    for i in range(4):
        loads[i].wait()
        rows = slice(i * piece, (i + 1) * piece)
        turned[:, rows] = hidden[rows, :].astype(F32).T.astype(BF16)
        for j in range(X):
            copy = pltpu.make_async_copy(
                turned.at[:, pieces[i]], out_hbm.at[j, :, pieces[i]], sems.at[11 + i * X + j]
            )
            copy.start()
            others.append(copy)
    for copy in others:
        copy.wait()


def exchange_blocks(head, ids, grad, hidden, weight):
    width = weight.shape[0]
    far = pl.BlockSpec(memory_space=pltpu.HBM)
    return pl.pallas_call(
        exchange_kernel,
        out_shape=(
            pltpu.HBM((X, width, EXPERTS * CAP + CORES * DS), BF16),
            jax.ShapeDtypeStruct((TOK + 16, DS), BF16),
        ),
        in_specs=[
            pl.BlockSpec(memory_space=pltpu.SMEM),
            far,
            far,
            far,
            far,
        ],
        out_specs=(far, pl.BlockSpec(memory_space=pltpu.VMEM)),
        scratch_shapes=[
            pltpu.VMEM(ids.shape, jnp.int32),
            pltpu.VMEM(hidden.shape, BF16),
            pltpu.VMEM(weight.shape, BF16),
            pltpu.VMEM((width, EXPERTS * CAP), BF16),
            pltpu.SemaphoreType.DMA((11 + 4 * X,)),
        ],
        compiler_params=pltpu.CompilerParams(vmem_limit_bytes=16 << 20),
    )(head, in_hbm(ids), in_hbm(grad), in_hbm(hidden), in_hbm(weight))


def mix_kernel(
    core_ref, mine_ref, theirs_ref, ids_ref, logits_ref, out_hbm, key_ref, probs_ref, out_ref, rounded, sems
):
    plan(ids_ref[...], logits_ref[...], key_ref, probs_ref)
    slots = EXPERTS * CAP
    core = core_ref[0]
    weight = jnp.where(
        core == 0, mine_ref[:, slots : slots + DS], mine_ref[:, slots + DS : slots + 2 * DS]
    )
    group = ZH * ZL * CAP
    contract = (((0,), (0,)), ((), ()))
    copies = []
    for y in range(Y):
        cols = slice(y * group, (y + 1) * group)
        mixed = lax.dot_general(
            mine_ref[:, cols], weight, contract, preferred_element_type=F32
        ) + lax.dot_general(
            theirs_ref[:, cols], theirs_ref[:, slots:], contract, preferred_element_type=F32
        )
        for zl in range(ZL):
            place = zl ^ (2 * core)
            for zh in range(ZH):
                src = (zh * ZL + zl) * CAP
                dst = pl.multiple_of(y * group + (place * ZH + zh) * CAP, 8)
                out_ref[pl.ds(dst, CAP), :] = mixed[src : src + CAP, :]
        rows = pl.ds(y * group, group)
        rounded[rows, :] = out_ref[rows, :].astype(BF16)
        copies.append(pltpu.make_async_copy(rounded.at[rows], out_hbm.at[rows], sems.at[y]))
        copies[-1].start()
    for copy in copies:
        copy.wait()


def plan(ids, logits, key_ref, probs_ref):
    raised = jnp.exp(logits)
    probs = raised / jnp.sum(raised, axis=0, keepdims=True)
    expert = lax.broadcasted_iota(jnp.int32, (EXPERTS, TOK), 0)
    hits = jnp.zeros((EXPERTS, TOK), F32)
    spread = jnp.zeros((EXPERTS, TOK), F32)
    for k in range(TOPK):
        mine = ids[k : k + 1, :] == expert
        hits = hits + mine.astype(F32)
        spread = spread + jnp.where(mine, probs[k : k + 1, :], 0.0)
    earlier = lax.broadcasted_iota(jnp.int32, (TOK, TOK), 0) < lax.broadcasted_iota(
        jnp.int32, (TOK, TOK), 1
    )
    before = jnp.dot(hits.astype(BF16), earlier.astype(BF16), preferred_element_type=F32)
    key_ref[...] = jnp.where(hits > 0, before, -1.0)
    probs_ref[...] = spread


def mix(core, mine, theirs, ids, logits):
    table = pltpu.VMEM((EXPERTS, TOK), F32)
    return pl.pallas_call(
        mix_kernel,
        out_shape=(pltpu.HBM((EXPERTS * CAP, DS), BF16), table, table),
        in_specs=[pl.BlockSpec(memory_space=pltpu.SMEM)]
        + [pl.BlockSpec(memory_space=pltpu.VMEM)] * 4,
        out_specs=(pl.BlockSpec(memory_space=pltpu.HBM),) + (pl.BlockSpec(memory_space=pltpu.VMEM),) * 2,
        scratch_shapes=[
            pltpu.VMEM((EXPERTS * CAP, DS), F32),
            pltpu.VMEM((EXPERTS * CAP, DS), BF16),
            pltpu.SemaphoreType.DMA((Y,)),
        ],
        compiler_params=pltpu.CompilerParams(vmem_limit_bytes=16 << 20),
    )(core, mine, theirs, ids, logits)


def value_kernel(core_ref, rows_hbm, mixed_hbm, out_ref, rows_ref, mixed_ref, sems):
    steps = 4
    per = NEAR // steps
    copies = []
    for i in range(steps):
        near, slots = pl.ds(i * per, per), pl.ds(i * per * ZH * CAP, per * ZH * CAP)
        copies.append(
            (
                pltpu.make_async_copy(rows_hbm.at[near], rows_ref.at[near], sems.at[0, i]),
                pltpu.make_async_copy(mixed_hbm.at[slots], mixed_ref.at[slots], sems.at[1, i]),
            )
        )
    for pair in copies:
        for copy in pair:
            copy.start()
    slot = lax.broadcasted_iota(jnp.int32, (CAP, 128), 0)
    lane = lax.broadcasted_iota(jnp.int32, (CAP, 128), 1)
    own_lane = (lane == slot, lane == slot + 64)
    for i in range(steps):
        for copy in copies[i]:
            copy.wait()
        for e in range(i * per, (i + 1) * per, 2):
            sums = []
            for odd in range(2):
                rows = rows_ref[e + odd].astype(F32) * mixed_ref[
                    (e + odd) * ZH * CAP : (e + odd + 1) * ZH * CAP, :
                ].astype(F32)
                sums.append(jnp.sum(rows[:, 0:128] + rows[:, 128:256], axis=1, keepdims=True))
            for b in range(ZH):
                slots = slice(b * CAP, (b + 1) * CAP)
                lanes = jnp.where(own_lane[0], sums[0][slots, :], 0.0) + jnp.where(
                    own_lane[1], sums[1][slots, :], 0.0
                )
                place = (e // ZL * ZH + b) * 2 + ((e % ZL // 2) ^ core_ref[0])
                out_ref[place] = jnp.sum(lanes, axis=0, keepdims=True)


def slot_sums(core, rows, mixed):
    return pl.pallas_call(
        value_kernel,
        out_shape=jax.ShapeDtypeStruct((EXPERTS // 2, 1, 128), F32),
        in_specs=[
            pl.BlockSpec(memory_space=pltpu.SMEM),
            pl.BlockSpec(memory_space=pltpu.HBM),
            pl.BlockSpec(memory_space=pltpu.HBM),
        ],
        out_specs=pl.BlockSpec(memory_space=pltpu.VMEM),
        scratch_shapes=[
            pltpu.VMEM(rows.shape, BF16),
            pltpu.VMEM(mixed.shape, BF16),
            pltpu.SemaphoreType.DMA((2, 4)),
        ],
        compiler_params=pltpu.CompilerParams(vmem_limit_bytes=16 << 20),
    )(core, in_hbm(rows), in_hbm(mixed))


def head_sum_kernel(parts_ref, out_ref):
    total = parts_ref[0]
    for i in range(1, X * CORES):
        total = total + parts_ref[i]
    turned = pltpu.roll(total, 64, 1)
    for row in range(EXPERTS // 2):
        out_ref[2 * row] = total[row : row + 1, :]
        out_ref[2 * row + 1] = turned[row : row + 1, :]


def head_sums(parts):
    return pl.pallas_call(
        head_sum_kernel,
        out_shape=jax.ShapeDtypeStruct((EXPERTS, 1, 128), F32),
    )(in_vmem(parts))


def final_kernel(
    parts_ref, key_ref, probs_ref, ids_ref, router_hbm, grad_ref, weight_ref,
    router_ref, total, sem,
):
    load_router = pltpu.make_async_copy(router_hbm, router_ref, sem)
    load_router.start()
    total[...] = parts_ref[:, 0, :]
    back = total[...]
    key = key_ref[...]
    probs = probs_ref[...]
    dense = jnp.zeros((EXPERTS, TOK), F32)
    for c in range(CAP):
        dense = jnp.where(key == float(c), back[:, c : c + 1], dense)
    mean = jnp.sum(probs * dense, axis=0, keepdims=True)
    logit = (probs * (dense - mean)).astype(BF16)
    load_router.wait()
    grad_ref[...] = lax.dot_general(
        logit, router_ref[...], (((0,), (0,)), ((), ())), preferred_element_type=F32
    ).astype(BF16)
    ids = ids_ref[...]
    expert = lax.broadcasted_iota(jnp.int32, (EXPERTS, TOK), 0)
    for k in range(TOPK):
        weight_ref[k : k + 1, :] = jnp.sum(
            jnp.where(ids[k : k + 1, :] == expert, dense, 0.0), axis=0, keepdims=True
        )


def finish(parts, key, probs, ids, router):
    far, near = pl.BlockSpec(memory_space=pltpu.HBM), pl.BlockSpec(memory_space=pltpu.VMEM)
    return pl.pallas_call(
        final_kernel,
        out_shape=(
            jax.ShapeDtypeStruct((TOK, DS), BF16),
            jax.ShapeDtypeStruct((TOPK, TOK), F32),
        ),
        in_specs=[near, near, near, near, far],
        out_specs=(near, near),
        scratch_shapes=[
            pltpu.VMEM(router.shape, BF16),
            pltpu.VMEM((EXPERTS, 128), F32),
            pltpu.SemaphoreType.DMA(()),
        ],
        compiler_params=pltpu.CompilerParams(vmem_limit_bytes=16 << 20),
    )(in_vmem(parts), in_vmem(key), in_vmem(probs), ids, in_hbm(router))


def body(out_grad, expert_ids, chosen_logits, down_weight, saved_hidden, router_weight):
    x, core = lax.axis_index("x"), lax.axis_index("core")
    head = x * CORES + core
    width = down_weight.shape[1]
    slots = EXPERTS * CAP
    ids, logits = expert_ids.T, chosen_logits.T
    along, block = exchange_blocks(
        head.reshape(1).astype(jnp.int32),
        ids,
        out_grad,
        saved_hidden[0].reshape(slots, width),
        down_weight[0],
    )
    along = lax.all_to_all(along, "x", split_axis=0, concat_axis=0, tiled=True)
    mine = along.reshape(X * width, slots + CORES * DS)
    weight_other = lax.dynamic_slice_in_dim(mine, slots + (1 - core) * DS, DS, axis=1)
    theirs = lax.ppermute(
        jnp.concatenate([mine[:, :slots], weight_other], axis=1), "core", [(0, 1), (1, 0)]
    )
    core_scalar = core.reshape(1).astype(jnp.int32)
    mixed, key, probs = mix(core_scalar, mine, theirs, ids, logits)
    blocks = lax.all_gather(block, "zh", axis=0, tiled=False)
    z = lax.axis_index("zh") * ZL + lax.axis_index("zl")
    base = ((z - 2 * core) & (ZH * ZL - ZL)) + 2 * core
    outgoing = select_rows(base.reshape(1).astype(jnp.int32), blocks)
    received = lax.all_to_all(
        outgoing,
        ("core", "y", "zh", "zl"),
        split_axis=0,
        concat_axis=0,
        tiled=True,
        axis_index_groups=NEAR_GROUPS,
    )
    part = slot_sums(core_scalar, received, mixed)
    part = part.reshape(1, EXPERTS // 2, 128)
    part = jnp.broadcast_to(part, (X * CORES,) + part.shape[1:])
    part = lax.all_to_all(part, HEAD, split_axis=0, concat_axis=0, tiled=True)
    part = lax.all_to_all(head_sums(part), EXPERT, split_axis=0, concat_axis=0, tiled=True)
    grad, weight_grad = finish(part, key, probs, ids, router_weight.T)
    return grad, weight_grad.T


def solution(mesh):
    fine = Mesh(
        mesh.devices.reshape(X, CORES, Y, ZH, ZL), ("x", "core", "y", "zh", "zl")
    )
    return jax.shard_map(
        body,
        mesh=fine,
        in_specs=(
            P(EXPERT, None),
            P(EXPERT, None),
            P(EXPERT, None),
            P(EXPERT, HEAD, None),
            P(EXPERT, None, None, HEAD),
            P(HEAD, None),
        ),
        out_specs=(P(EXPERT, HEAD), P(EXPERT, None)),
        check_vma=False,
    )
```

```python
import jax
import jax.numpy as jnp
from jax import lax
from jax.experimental import pallas as pl
from jax.experimental.pallas import tpu as pltpu
from jax.sharding import Mesh, PartitionSpec as P

X, CORES, Y, ZH, ZL = 4, 2, 4, 4, 4
EXPERT = ("y", "zh", "zl")
HEAD = ("x", "core")
TOK = 256
CAP = 40
TOPK = 8
EXPERTS = 64
DS = 256
NEAR = Y * ZL
F32 = jnp.float32
NEAR_GROUPS = [
    [c * Y * ZH * ZL + y * ZH * ZL + (q * ZL + r + 2 * c) % (ZH * ZL) for y in range(Y) for r in range(ZL)]
    for c in range(CORES)
    for q in range(ZH)
]
BF16 = jnp.bfloat16


def in_vmem(array):
    return pltpu.with_memory_space_constraint(array, pltpu.VMEM)


def in_hbm(array):
    return pltpu.with_memory_space_constraint(array, pltpu.HBM)


def select_kernel(base_ref, blocks_ref, out_hbm, picked, rows_out, sems):
    base = base_ref[0]
    j = lax.broadcasted_iota(jnp.int32, (NEAR, TOK), 0)
    expert = ((j // ZL) * (ZH * ZL) + ((base + j % ZL) & (ZH * ZL - 1))).astype(F32)
    hits = []
    for b in range(ZH):
        ids = blocks_ref[b, TOK : TOK + 16, :].astype(F32)
        hit = jnp.zeros((NEAR, TOK), F32)
        for k in range(TOPK):
            hit = hit + (ids[k : k + 1, :] == expert).astype(F32)
        hits.append(hit)
    hits = jnp.concatenate(hits, axis=0)
    earlier = lax.broadcasted_iota(jnp.int32, (TOK, TOK), 0) < lax.broadcasted_iota(
        jnp.int32, (TOK, TOK), 1
    )
    before = jnp.dot(hits.astype(BF16), earlier.astype(BF16), preferred_element_type=F32)
    key = jnp.where(hits > 0, before, -1.0)
    slot = lax.broadcasted_iota(jnp.int32, (CAP, TOK), 0).astype(F32)
    copies = []
    for y in range(Y):
        for b in range(ZH):
            first = b * NEAR + y * ZL
            pick = jnp.concatenate(
                [(key[e : e + 1, :] == slot).astype(F32) for e in range(first, first + ZL)], axis=0
            )
            picked[b] = jnp.dot(
                pick.astype(BF16), blocks_ref[b, 0:TOK, :], preferred_element_type=F32
            )
        for e in range(ZL):
            rows = [picked[b, e * CAP : (e + 1) * CAP, :] for b in range(ZH)]
            rows_out[y * ZL + e] = jnp.concatenate(rows, axis=0).astype(BF16)
        near = pl.ds(y * ZL, ZL)
        copies.append(pltpu.make_async_copy(rows_out.at[near], out_hbm.at[near], sems.at[y]))
        copies[-1].start()
    for copy in copies:
        copy.wait()


def select_rows(base, blocks):
    return pl.pallas_call(
        select_kernel,
        out_shape=pltpu.HBM((NEAR, ZH * CAP, DS), BF16),
        in_specs=[
            pl.BlockSpec(memory_space=pltpu.SMEM),
            pl.BlockSpec(memory_space=pltpu.VMEM),
        ],
        out_specs=pl.BlockSpec(memory_space=pltpu.HBM),
        scratch_shapes=[
            pltpu.VMEM((ZH, ZL * CAP, DS), F32),
            pltpu.VMEM((NEAR, ZH * CAP, DS), BF16),
            pltpu.SemaphoreType.DMA((Y,)),
        ],
        compiler_params=pltpu.CompilerParams(vmem_limit_bytes=16 << 20),
    )(base, blocks)


def exchange_kernel(
    head_ref, ids_hbm, grad_hbm, hidden_hbm, weight_hbm, out_hbm, block_ref, ids_ref, hidden, weight, turned, sems
):
    slots = EXPERTS * CAP
    piece = slots // 4
    pieces = [pl.ds(i * piece, piece) for i in range(4)]
    loads = [
        pltpu.make_async_copy(hidden_hbm.at[pieces[i]], hidden.at[pieces[i]], sems.at[i])
        for i in range(4)
    ]
    columns = pl.ds(pl.multiple_of(head_ref[0] * DS, DS), DS)
    load_weight = pltpu.make_async_copy(weight_hbm, weight, sems.at[10])
    load_ids = pltpu.make_async_copy(ids_hbm, ids_ref, sems.at[9])
    load_grad = pltpu.make_async_copy(
        grad_hbm.at[:, columns], block_ref.at[pl.ds(0, TOK)], sems.at[8]
    )
    for copy in [load_weight] + loads + [load_ids, load_grad]:
        copy.start()
    others = [load_grad]
    load_ids.wait()
    ids = ids_ref[...].astype(F32)
    block_ref[TOK : TOK + 16, :] = jnp.concatenate([ids, jnp.zeros_like(ids)], axis=0).astype(BF16)
    load_weight.wait()
    for j in range(X):
        copy = pltpu.make_async_copy(
            weight.at[:, pl.ds(j * CORES * DS, CORES * DS)],
            out_hbm.at[j, :, pl.ds(slots, CORES * DS)],
            sems.at[4 + j],
        )
        copy.start()
        others.append(copy)
    for i in range(4):
        loads[i].wait()
        rows = slice(i * piece, (i + 1) * piece)
        turned[:, rows] = hidden[rows, :].astype(F32).T.astype(BF16)
        for j in range(X):
            copy = pltpu.make_async_copy(
                turned.at[:, pieces[i]], out_hbm.at[j, :, pieces[i]], sems.at[11 + i * X + j]
            )
            copy.start()
            others.append(copy)
    for copy in others:
        copy.wait()


def exchange_blocks(head, ids, grad, hidden, weight):
    width = weight.shape[0]
    far = pl.BlockSpec(memory_space=pltpu.HBM)
    return pl.pallas_call(
        exchange_kernel,
        out_shape=(
            pltpu.HBM((X, width, EXPERTS * CAP + CORES * DS), BF16),
            jax.ShapeDtypeStruct((TOK + 16, DS), BF16),
        ),
        in_specs=[
            pl.BlockSpec(memory_space=pltpu.SMEM),
            far,
            far,
            far,
            far,
        ],
        out_specs=(far, pl.BlockSpec(memory_space=pltpu.VMEM)),
        scratch_shapes=[
            pltpu.VMEM(ids.shape, jnp.int32),
            pltpu.VMEM(hidden.shape, BF16),
            pltpu.VMEM(weight.shape, BF16),
            pltpu.VMEM((width, EXPERTS * CAP), BF16),
            pltpu.SemaphoreType.DMA((11 + 4 * X,)),
        ],
        compiler_params=pltpu.CompilerParams(vmem_limit_bytes=16 << 20),
    )(head, in_hbm(ids), in_hbm(grad), in_hbm(hidden), in_hbm(weight))


def mix_kernel(
    core_ref, mine_ref, theirs_ref, ids_ref, logits_ref, out_hbm, key_ref, probs_ref, out_ref, rounded, sems
):
    plan(ids_ref[...], logits_ref[...], key_ref, probs_ref)
    slots = EXPERTS * CAP
    core = core_ref[0]
    weight = jnp.where(
        core == 0, mine_ref[:, slots : slots + DS], mine_ref[:, slots + DS : slots + 2 * DS]
    )
    group = ZH * ZL * CAP
    contract = (((0,), (0,)), ((), ()))
    copies = []
    for y in range(Y):
        cols = slice(y * group, (y + 1) * group)
        mixed = lax.dot_general(
            mine_ref[:, cols], weight, contract, preferred_element_type=F32
        ) + lax.dot_general(
            theirs_ref[:, cols], theirs_ref[:, slots:], contract, preferred_element_type=F32
        )
        for zl in range(ZL):
            place = zl ^ (2 * core)
            for zh in range(ZH):
                src = (zh * ZL + zl) * CAP
                dst = pl.multiple_of(y * group + (place * ZH + zh) * CAP, 8)
                out_ref[pl.ds(dst, CAP), :] = mixed[src : src + CAP, :]
        rows = pl.ds(y * group, group)
        rounded[rows, :] = out_ref[rows, :].astype(BF16)
        copies.append(pltpu.make_async_copy(rounded.at[rows], out_hbm.at[rows], sems.at[y]))
        copies[-1].start()
    for copy in copies:
        copy.wait()


def plan(ids, logits, key_ref, probs_ref):
    raised = jnp.exp(logits)
    probs = raised / jnp.sum(raised, axis=0, keepdims=True)
    expert = lax.broadcasted_iota(jnp.int32, (EXPERTS, TOK), 0)
    hits = jnp.zeros((EXPERTS, TOK), F32)
    spread = jnp.zeros((EXPERTS, TOK), F32)
    for k in range(TOPK):
        mine = ids[k : k + 1, :] == expert
        hits = hits + mine.astype(F32)
        spread = spread + jnp.where(mine, probs[k : k + 1, :], 0.0)
    earlier = lax.broadcasted_iota(jnp.int32, (TOK, TOK), 0) < lax.broadcasted_iota(
        jnp.int32, (TOK, TOK), 1
    )
    before = jnp.dot(hits.astype(BF16), earlier.astype(BF16), preferred_element_type=F32)
    key_ref[...] = jnp.where(hits > 0, before, -1.0)
    probs_ref[...] = spread


def mix(core, mine, theirs, ids, logits):
    table = pltpu.VMEM((EXPERTS, TOK), F32)
    return pl.pallas_call(
        mix_kernel,
        out_shape=(pltpu.HBM((EXPERTS * CAP, DS), BF16), table, table),
        in_specs=[pl.BlockSpec(memory_space=pltpu.SMEM)]
        + [pl.BlockSpec(memory_space=pltpu.VMEM)] * 4,
        out_specs=(pl.BlockSpec(memory_space=pltpu.HBM),) + (pl.BlockSpec(memory_space=pltpu.VMEM),) * 2,
        scratch_shapes=[
            pltpu.VMEM((EXPERTS * CAP, DS), F32),
            pltpu.VMEM((EXPERTS * CAP, DS), BF16),
            pltpu.SemaphoreType.DMA((Y,)),
        ],
        compiler_params=pltpu.CompilerParams(vmem_limit_bytes=16 << 20),
    )(core, mine, theirs, ids, logits)


def value_kernel(core_ref, rows_hbm, mixed_hbm, out_ref, rows_ref, mixed_ref, sems):
    steps = 2
    per = NEAR // steps
    copies = []
    for i in range(steps):
        near, slots = pl.ds(i * per, per), pl.ds(i * per * ZH * CAP, per * ZH * CAP)
        copies.append(
            (
                pltpu.make_async_copy(rows_hbm.at[near], rows_ref.at[near], sems.at[0, i]),
                pltpu.make_async_copy(mixed_hbm.at[slots], mixed_ref.at[slots], sems.at[1, i]),
            )
        )
    for pair in copies:
        for copy in pair:
            copy.start()
    slot = lax.broadcasted_iota(jnp.int32, (CAP, 128), 0)
    lane = lax.broadcasted_iota(jnp.int32, (CAP, 128), 1)
    own_lane = (lane == slot, lane == slot + 64)
    for i in range(steps):
        for copy in copies[i]:
            copy.wait()
        for e in range(i * per, (i + 1) * per, 2):
            sums = []
            for odd in range(2):
                rows = rows_ref[e + odd].astype(F32) * mixed_ref[
                    (e + odd) * ZH * CAP : (e + odd + 1) * ZH * CAP, :
                ].astype(F32)
                sums.append(jnp.sum(rows[:, 0:128] + rows[:, 128:256], axis=1, keepdims=True))
            for b in range(ZH):
                slots = slice(b * CAP, (b + 1) * CAP)
                lanes = jnp.where(own_lane[0], sums[0][slots, :], 0.0) + jnp.where(
                    own_lane[1], sums[1][slots, :], 0.0
                )
                place = (e // ZL * ZH + b) * 2 + ((e % ZL // 2) ^ core_ref[0])
                out_ref[place] = jnp.sum(lanes, axis=0, keepdims=True)


def slot_sums(core, rows, mixed):
    return pl.pallas_call(
        value_kernel,
        out_shape=jax.ShapeDtypeStruct((EXPERTS // 2, 1, 128), F32),
        in_specs=[
            pl.BlockSpec(memory_space=pltpu.SMEM),
            pl.BlockSpec(memory_space=pltpu.HBM),
            pl.BlockSpec(memory_space=pltpu.HBM),
        ],
        out_specs=pl.BlockSpec(memory_space=pltpu.VMEM),
        scratch_shapes=[
            pltpu.VMEM(rows.shape, BF16),
            pltpu.VMEM(mixed.shape, BF16),
            pltpu.SemaphoreType.DMA((2, 4)),
        ],
        compiler_params=pltpu.CompilerParams(vmem_limit_bytes=16 << 20),
    )(core, in_hbm(rows), in_hbm(mixed))


def head_sum_kernel(parts_ref, out_ref):
    for y in range(Y):
        total = parts_ref[0, y]
        for i in range(1, X * CORES):
            total = total + parts_ref[i, y]
        turned = pltpu.roll(total, 64, 1)
        for z in range(0, ZH * ZL, 2):
            out_ref[z, :, y * 128 : (y + 1) * 128] = total[z // 2 : z // 2 + 1, :]
            out_ref[z + 1, :, y * 128 : (y + 1) * 128] = turned[z // 2 : z // 2 + 1, :]


def head_sums(parts):
    return pl.pallas_call(
        head_sum_kernel,
        out_shape=jax.ShapeDtypeStruct((ZH * ZL, 1, Y * 128), F32),
    )(in_vmem(parts))


def final_kernel(
    parts_ref, key_ref, probs_ref, ids_ref, router_hbm, grad_ref, weight_ref,
    router_ref, total, sem,
):
    load_router = pltpu.make_async_copy(router_hbm, router_ref, sem)
    load_router.start()
    for y in range(Y):
        total[y * ZH * ZL : (y + 1) * ZH * ZL, :] = parts_ref[:, 0, y * 128 : (y + 1) * 128]
    back = total[...]
    key = key_ref[...]
    probs = probs_ref[...]
    dense = jnp.zeros((EXPERTS, TOK), F32)
    for c in range(CAP):
        dense = jnp.where(key == float(c), back[:, c : c + 1], dense)
    mean = jnp.sum(probs * dense, axis=0, keepdims=True)
    logit = (probs * (dense - mean)).astype(BF16)
    load_router.wait()
    grad_ref[...] = lax.dot_general(
        logit, router_ref[...], (((0,), (0,)), ((), ())), preferred_element_type=F32
    ).astype(BF16)
    ids = ids_ref[...]
    expert = lax.broadcasted_iota(jnp.int32, (EXPERTS, TOK), 0)
    for k in range(TOPK):
        weight_ref[k : k + 1, :] = jnp.sum(
            jnp.where(ids[k : k + 1, :] == expert, dense, 0.0), axis=0, keepdims=True
        )


def finish(parts, key, probs, ids, router):
    far, near = pl.BlockSpec(memory_space=pltpu.HBM), pl.BlockSpec(memory_space=pltpu.VMEM)
    return pl.pallas_call(
        final_kernel,
        out_shape=(
            jax.ShapeDtypeStruct((TOK, DS), BF16),
            jax.ShapeDtypeStruct((TOPK, TOK), F32),
        ),
        in_specs=[near, near, near, near, far],
        out_specs=(near, near),
        scratch_shapes=[
            pltpu.VMEM(router.shape, BF16),
            pltpu.VMEM((EXPERTS, 128), F32),
            pltpu.SemaphoreType.DMA(()),
        ],
        compiler_params=pltpu.CompilerParams(vmem_limit_bytes=16 << 20),
    )(in_vmem(parts), in_vmem(key), in_vmem(probs), ids, in_hbm(router))


def body(out_grad, expert_ids, chosen_logits, down_weight, saved_hidden, router_weight):
    x, core = lax.axis_index("x"), lax.axis_index("core")
    head = x * CORES + core
    width = down_weight.shape[1]
    slots = EXPERTS * CAP
    ids, logits = expert_ids.T, chosen_logits.T
    along, block = exchange_blocks(
        head.reshape(1).astype(jnp.int32),
        ids,
        out_grad,
        saved_hidden[0].reshape(slots, width),
        down_weight[0],
    )
    along = lax.all_to_all(along, "x", split_axis=0, concat_axis=0, tiled=True)
    mine = along.reshape(X * width, slots + CORES * DS)
    weight_other = lax.dynamic_slice_in_dim(mine, slots + (1 - core) * DS, DS, axis=1)
    theirs = lax.ppermute(
        jnp.concatenate([mine[:, :slots], weight_other], axis=1), "core", [(0, 1), (1, 0)]
    )
    core_scalar = core.reshape(1).astype(jnp.int32)
    mixed, key, probs = mix(core_scalar, mine, theirs, ids, logits)
    blocks = lax.all_gather(block, "zh", axis=0, tiled=False)
    z = lax.axis_index("zh") * ZL + lax.axis_index("zl")
    base = ((z - 2 * core) & (ZH * ZL - ZL)) + 2 * core
    outgoing = select_rows(base.reshape(1).astype(jnp.int32), blocks)
    received = lax.all_to_all(
        outgoing,
        ("core", "y", "zh", "zl"),
        split_axis=0,
        concat_axis=0,
        tiled=True,
        axis_index_groups=NEAR_GROUPS,
    )
    part = slot_sums(core_scalar, received, mixed)
    rows = ZH * ZL // 2
    part = jnp.broadcast_to(part.reshape(1, Y, rows, 128), (X * CORES, Y, rows, 128))
    part = lax.all_to_all(
        part.reshape(X * CORES * Y, rows, 128),
        ("x", "core", "y"),
        split_axis=0,
        concat_axis=0,
        tiled=True,
    )
    part = head_sums(part.reshape(X * CORES, Y, rows, 128))
    part = lax.all_to_all(part, ("zh", "zl"), split_axis=0, concat_axis=0, tiled=True)
    grad, weight_grad = finish(part, key, probs, ids, router_weight.T)
    return grad, weight_grad.T


def solution(mesh):
    fine = Mesh(
        mesh.devices.reshape(X, CORES, Y, ZH, ZL), ("x", "core", "y", "zh", "zl")
    )
    return jax.shard_map(
        body,
        mesh=fine,
        in_specs=(
            P(EXPERT, None),
            P(EXPERT, None),
            P(EXPERT, None),
            P(EXPERT, HEAD, None),
            P(EXPERT, None, None, HEAD),
            P(HEAD, None),
        ),
        out_specs=(P(EXPERT, HEAD), P(EXPERT, None)),
        check_vma=False,
    )
```
